256 devices in a mesh: ctx: 64 (over y, z, core), tp: 4 (over x).
Axes of the slice: x: 4, y: 4, z: 8, core: 2. Of those that a mesh axis runs over, the one named last changes fastest.
Arguments:
- queries: bfloat16 [512, 64, 128], P('ctx', 'tp')
- prefix_kv: bfloat16 [2, 2, 32768, 8, 128], P(None, None, 'ctx', 'tp'), may hold values from -6 to 6
- tail_kv: bfloat16 [512, 2, 256, 8, 128], P('ctx', None, None, 'tp'), may hold values from -6 to 6
- row_prompt: int32 [512], replicated, may hold values from 0 to 1
- prefix_len: int32 [512], replicated, may hold values from 1 to 32768
- tail_len: int32 [512], P('ctx'), may hold values from 1 to 256
- out_weight: bfloat16 [8192, 5120], P('tp', 'ctx'), may hold values from -0.0625 to 0.0625
- residual: bfloat16 [512, 5120], P('tp', 'ctx'), may hold values from -3 to 3
- norm_gain: bfloat16 [5120], replicated, may hold values from 0.5 to 1.5
- vocab_weight: bfloat16 [5120, 131072], P('tp', 'ctx')
- allowed: int32 [512, 1024], P('tp', 'ctx'), may hold values from 0 to 1, as said below
- next_token: int32 [512], P('tp'), may hold values from 0 to 131071, as said below
Outputs:
- attended: bfloat16 [512, 8192], P('ctx', 'tp')
- logprob: float32 [512], P('tp')
The draws below stay inside these ranges and needn't reach their ends.
Inputs may be any that keep to these rules, and one draw needn't show every extreme that they name: `allowed`: the block next_token // 128 of each row is marked 1. `next_token`: lies in a block that allowed marks 1 for its row.
All inputs are finite; a program needn't handle non-finite values.
Results may differ from the reference program's by a relative error of at most 0.014.
Values may be sent and summed in bfloat16 or wider, within the bound.
No kernel may reach another device: no remote copies, remote signals or barrier semaphores. Data moves between devices by JAX's collectives and lax.ppermute only.
A program may use at most 64 MiB of HBM per device.

```python
import math
import jax
import jax.numpy as jnp
from jax import lax

D = 5120
QH = 64
KVH = 8
HD = 128
VBLK = 128
NPROMPT = 2
PROMPT_DEV = 512
TAIL = 256
ROWS = 512
LEN = 32768
VOCAB = 131072
NBLK = 1024
N_CTX = 64


def grammar_draw(key):
    token = jax.random.randint(jax.random.fold_in(key, 71), (ROWS,), 0, VOCAB)
    bits = jax.random.randint(jax.random.fold_in(key, 72), (ROWS, NBLK), 0, 2)
    blocks = jnp.arange(NBLK, dtype=jnp.int32)
    marked = (blocks[None, :] == (token // VBLK)[:, None]).astype(jnp.int32)
    return (token, jnp.maximum(bits, marked))


def draw_allowed(key, part):
    shared = grammar_draw(key)
    return shared[1]


def draw_next_token(key, part):
    shared = grammar_draw(key)
    return shared[0]


def draw_queries(key, part):
    key = jax.random.fold_in(key, 11)
    base = jax.random.normal(jax.random.fold_in(key, 3), (ROWS, QH, HD), jnp.float32)
    return (3.0 * jnp.clip(base, -5.0, 5.0)).astype(jnp.bfloat16)


def draw_vocab_weight(key, part):
    key = jax.random.fold_in(key, 23)
    spread = 3.0 / D ** 0.5
    base = jax.random.normal(jax.random.fold_in(key, 3), (D, VOCAB), jnp.float32)
    return (spread * jnp.clip(base, -6.0, 6.0)).astype(jnp.bfloat16)


def set_ends(array, key, low, top_value):
    shape = array.shape
    index_at = [jax.random.randint(jax.random.fold_in(key, axis), (), 0, shape[axis]) for axis in range(len(shape))]
    array = array.at[tuple(index_at)].set(low)
    longest = shape.index(max(shape))
    index_at[longest] = (index_at[longest] + 1) % shape[longest]
    return array.at[tuple(index_at)].set(top_value)


def level_of(own_key, extent, cuts, least, top_value):
    def one(dim, parts):
        steps = jax.random.uniform(jax.random.fold_in(jax.random.fold_in(own_key, 6), dim), (parts,), jnp.float32, least / len(cuts), top_value / len(cuts))
        return jnp.repeat(jnp.exp(steps), extent[dim] // parts).reshape((-1,) + (1,) * (len(extent) - dim - 1))

    loudness = one(*cuts[0])
    for cut in cuts[1:]:
        loudness = loudness * one(*cut)
    return loudness


def gaussian(stream_key, dims, scale, limit, cuts=(), kind=jnp.bfloat16):
    loudness = level_of(stream_key, dims, cuts, -0.22, 0.18) if cuts else 1.0
    array = jax.random.normal(stream_key, dims, jnp.float32) * scale * loudness
    return jnp.minimum(jnp.maximum(array, -limit), limit).astype(kind)


def setup_inputs(seed: int = 0) -> dict:
    streams_of = jax.random.split(jax.random.key(seed), 13)
    queries = draw_queries(jax.random.fold_in(streams_of[12], 71), 0)
    prefix_kv = gaussian(streams_of[1], (NPROMPT, 2, LEN, KVH, HD), 1.0, 6.0, ((2, 64), (3, 4)))
    tail_kv = gaussian(streams_of[2], (ROWS, 2, TAIL, KVH, HD), 1.0, 6.0, ((0, 64), (3, 4)))
    row_prompt = set_ends(jax.random.randint(streams_of[3], (ROWS,), 0, NPROMPT), jax.random.fold_in(streams_of[3], 1), 0, NPROMPT - 1).astype(jnp.int32)
    prefix_len = set_ends(jax.random.randint(streams_of[4], (ROWS,), 1, LEN + 1), jax.random.fold_in(streams_of[4], 1), 1, LEN).astype(jnp.int32)
    tail_len = set_ends(jax.random.randint(streams_of[5], (ROWS,), 1, TAIL + 1), jax.random.fold_in(streams_of[5], 1), 1, TAIL).astype(jnp.int32)
    out_weight = gaussian(streams_of[6], (QH * HD, D), (QH * HD) ** -0.5, 0.0625, ((0, 4), (1, 64)))
    residual = gaussian(streams_of[7], (ROWS, D), 0.5, 3.0, ((0, 4), (1, 64)))
    norm_gain = jnp.clip(1.0 + 0.1 * jax.random.normal(streams_of[8], (D,), jnp.float32), 0.5, 1.5).astype(jnp.bfloat16)
    vocab_weight = draw_vocab_weight(jax.random.fold_in(streams_of[12], 71), 0)
    allowed = draw_allowed(jax.random.fold_in(streams_of[12], 71), 0)
    next_token = draw_next_token(jax.random.fold_in(streams_of[12], 71), 0)
    return {"queries": queries, "prefix_kv": prefix_kv, "tail_kv": tail_kv, "row_prompt": row_prompt, "prefix_len": prefix_len, "tail_len": tail_len, "out_weight": out_weight, "residual": residual, "norm_gain": norm_gain, "vocab_weight": vocab_weight, "allowed": allowed, "next_token": next_token}


lowest = -1e+30
epsilon = 1e-06

def partial_stats(scores, allowed_keys):
    masked = jnp.where(allowed_keys, scores, lowest)
    highest = lax.optimization_barrier(jnp.max(masked, axis=-1))
    weights = jnp.where(allowed_keys, jnp.exp(scores - highest[..., None]), 0.0).astype(jnp.bfloat16)
    totals = lax.optimization_barrier(jnp.sum(weights.astype(jnp.float32), axis=-1))
    return (highest, weights, totals)

def reference(queries, prefix_kv, tail_kv, row_prompt, prefix_len, tail_len, out_weight, residual, norm_gain, vocab_weight, allowed, next_token):
    inv_root = 1.0 / math.sqrt(HD)
    grouped = queries.reshape(ROWS, KVH, QH // KVH, HD).astype(jnp.float32)
    tail_keys = tail_kv[:, 0].astype(jnp.float32)
    tail_vals = tail_kv[:, 1].astype(jnp.float32)
    tail_scores = jnp.einsum('rhgd,rkhd->rhgk', grouped, tail_keys) * inv_root
    tail_keep = (jnp.arange(TAIL, dtype=jnp.int32)[None, :] < tail_len[:, None])[:, None, None, :]
    highest, weights, totals = partial_stats(tail_scores, tail_keep)
    weighted = jnp.einsum('rhgk,rkhd->rhgd', weights.astype(jnp.float32), tail_vals)
    key_index = jnp.arange(NPROMPT * PROMPT_DEV, dtype=jnp.int32)
    key_prompt = key_index // PROMPT_DEV
    same_prompt = row_prompt[:, None] == key_prompt[None, :]

    def add_slice(carry, owner):
        run_high, run_total, run_sum = carry
        offset = (owner * PROMPT_DEV).astype(jnp.int32)
        section = lax.dynamic_slice_in_dim(prefix_kv, offset, PROMPT_DEV, 2)
        keys_here = section[:, 0].reshape(NPROMPT * PROMPT_DEV, KVH, HD).astype(jnp.float32)
        vals_here = section[:, 1].reshape(NPROMPT * PROMPT_DEV, KVH, HD).astype(jnp.float32)
        scores = jnp.einsum('rhgd,khd->rhgk', grouped, keys_here) * inv_root
        key_pos = offset + key_index % PROMPT_DEV
        keep = (same_prompt & (key_pos[None, :] < prefix_len[:, None]))[:, None, None, :]
        part_high, part_weights, part_total = partial_stats(scores, keep)
        part_sum = jnp.einsum('rhgk,khd->rhgd', part_weights.astype(jnp.float32), vals_here)
        new_high = jnp.maximum(run_high, part_high)
        old_factor = jnp.exp(run_high - new_high)
        new_factor = jnp.exp(part_high - new_high)
        merged_total = run_total * old_factor + part_total * new_factor
        merged_sum = run_sum * old_factor[..., None] + part_sum * new_factor[..., None]
        return ((new_high, merged_total, merged_sum), None)
    (final_high, final_total, final_sum), _ = lax.scan(add_slice, (highest, totals, weighted), jnp.arange(N_CTX, dtype=jnp.int32))
    attended = (final_sum / final_total[..., None]).reshape(ROWS, QH * HD).astype(jnp.bfloat16)
    projected = jnp.dot(attended, out_weight, preferred_element_type=jnp.float32)
    stream = (projected + residual.astype(jnp.float32)).astype(jnp.bfloat16)
    widened = stream.astype(jnp.float32)
    second = lax.optimization_barrier(jnp.mean(widened * widened, axis=-1))
    normed = (widened * lax.rsqrt(second + epsilon)[:, None] * norm_gain.astype(jnp.float32)).astype(jnp.bfloat16)
    logits = jnp.dot(normed, vocab_weight, preferred_element_type=jnp.float32)
    keep_vocab = jnp.broadcast_to((allowed > 0)[:, :, None], (ROWS, NBLK, VBLK)).reshape(ROWS, VOCAB)
    peak = lax.optimization_barrier(jnp.max(jnp.where(keep_vocab, logits, lowest), axis=-1))
    total_vocab = lax.optimization_barrier(jnp.sum(jnp.where(keep_vocab, jnp.exp(logits - peak[:, None]), 0.0), axis=-1))
    chosen = jnp.take_along_axis(logits, next_token[:, None].astype(jnp.int32), axis=1)[:, 0]
    logprob = chosen - (peak + jnp.log(total_vocab))
    return (attended, logprob)
```

```python
import math

import jax
import jax.numpy as jnp
from jax import lax
from jax.experimental import pallas as pl
from jax.experimental.pallas import tpu as pltpu
from jax.sharding import PartitionSpec as P

lowest = -1e30
epsilon = 1e-06
LOG2E = 1.4426950408889634
NY, NZ, NC, NX = 4, 8, 2, 4
VMEM = pltpu.VMEM


def ctx_id(y, z, c):
    return (y % NY) * (NZ * NC) + (z % NZ) * NC + c % NC


def chips():
    return [(y, z, c) for y in range(NY) for z in range(NZ) for c in range(NC)]


core_swap = [(ctx_id(y, z, c), ctx_id(y, z, 1 - c)) for y, z, c in chips()]
z_groups = [[ctx_id(y, z, c) for z in range(NZ)] for y in range(NY) for c in range(NC)]
zc_groups = [[ctx_id(y, z, c) for z in range(NZ) for c in range(NC)] for y in range(NY)]


def y_shift(d):
    return [(ctx_id(y, z, c), ctx_id(y + d, z, c)) for y, z, c in chips()]


def x_shift(d):
    return [(t, (t + d) % NX) for t in range(NX)]


def turned(s):
    return [
        (ctx_id(y, z, c) * NX + t, ctx_id(t + s, z, c) * NX + y)
        for t in range(NX)
        for y, z, c in chips()
    ]


def split3(value):
    hi = value.astype(jnp.bfloat16).astype(jnp.float32)
    rest = value - hi
    mid = rest.astype(jnp.bfloat16).astype(jnp.float32)
    return hi, mid, rest - mid


def call(kernel, out_shape, args, flops, scratch=()):
    size = sum(math.prod(a.shape) * a.dtype.itemsize for a in args)
    return pl.pallas_call(
        kernel,
        out_shape=out_shape,
        in_specs=[pl.BlockSpec(memory_space=VMEM)] * len(args),
        out_specs=pl.BlockSpec(memory_space=VMEM),
        scratch_shapes=list(scratch),
        compiler_params=pltpu.CompilerParams(vmem_limit_bytes=40 * 1024 * 1024),
        cost_estimate=pl.CostEstimate(flops=flops, bytes_accessed=size, transcendentals=0),
    )(*args)


def attend_kernel(q_ref, own_ref, other_ref, reach_ref, out_ref, s_ref):
    rows = q_ref.shape[0]
    span = own_ref.shape[2]
    factor = LOG2E / math.sqrt(128)
    lane = lax.broadcasted_iota(jnp.int32, (rows, 128), 1)
    key = lax.broadcasted_iota(jnp.int32, (rows, span), 1)
    extra = jnp.zeros((rows, 128), jnp.float32)
    blocks = [(ref, p) for p in range(2) for ref in (own_ref, other_ref)]
    ones = jnp.ones((span, 128), jnp.bfloat16)
    for h in range(2):
        for half in range(2):
            heads = [h * 8 + half * 4 + g for g in range(4)]
            q = jnp.concatenate([q_ref[:, j * 128 : (j + 1) * 128] for j in heads], axis=0)
            high = jnp.full((4 * rows, 1), lowest, jnp.float32)
            for b, (ref, p) in enumerate(blocks):
                s = lax.dot_general(
                    q,
                    ref[p, 0, :, h * 128 : (h + 1) * 128],
                    (((1,), (1,)), ((), ())),
                    preferred_element_type=jnp.float32,
                )
                keep = key < reach_ref[:, b : b + 1]
                s = jnp.concatenate(
                    [
                        jnp.where(keep, s[g * rows : (g + 1) * rows] * factor, lowest)
                        for g in range(4)
                    ],
                    axis=0,
                )
                s_ref[:, b * span : (b + 1) * span] = s
                high = jnp.maximum(high, jnp.max(s, axis=1, keepdims=True))
            acc = jnp.zeros((4 * rows, 256), jnp.float32)
            for b, (ref, p) in enumerate(blocks):
                w = jnp.exp2(s_ref[:, b * span : (b + 1) * span] - high).astype(jnp.bfloat16)
                v = jnp.concatenate([ref[p, 1, :, h * 128 : (h + 1) * 128], ones], axis=1)
                acc += jnp.dot(w, v, preferred_element_type=jnp.float32)
            for g, j in enumerate(heads):
                part = slice(g * rows, (g + 1) * rows)
                total = acc[part, 128:]
                out_ref[:, j * 128 : (j + 1) * 128] = (acc[part, :128] / total).astype(jnp.bfloat16)
                level = high[part] + jnp.log2(total)
                for i, piece in enumerate(split3(level)):
                    extra = jnp.where(lane == j + 16 * i, piece, extra)
    out_ref[:, 2048:] = extra.astype(jnp.bfloat16)


def level_of(extra):
    extra = extra.astype(jnp.float32)
    return extra + pltpu.roll(extra, 112, 1) + pltpu.roll(extra, 96, 1)


def join(parts, levels):
    high = levels[0]
    for level in levels[1:]:
        high = jnp.maximum(high, level)
    shares = [jnp.exp2(level - high) for level in levels]
    total = shares[0]
    for share in shares[1:]:
        total = total + share
    shares = [share / total for share in shares]
    heads = []
    for j in range(16):
        value = None
        for part, share in zip(parts, shares):
            term = part(j).astype(jnp.float32) * share[:, j : j + 1]
            value = term if value is None else value + term
        heads.append(value)
    return heads, high + jnp.log2(total)


def join4_kernel(a_ref, b_ref, c_ref, d_ref, out_ref):
    refs = (a_ref, b_ref, c_ref, d_ref)
    parts = [lambda j, r=r: r[:, j * 128 : (j + 1) * 128] for r in refs]
    heads, level = join(parts, [level_of(r[:, 2048:]) for r in refs])
    lane = lax.broadcasted_iota(jnp.int32, level.shape, 1)
    for j, value in enumerate(heads):
        out_ref[:, j * 128 : (j + 1) * 128] = value.astype(jnp.bfloat16)
    hi, mid, lo = split3(level)
    extra = jnp.where(
        lane < 16,
        hi,
        jnp.where(
            lane < 32,
            pltpu.roll(mid, 16, 1),
            jnp.where(lane < 48, pltpu.roll(lo, 32, 1), 0.0),
        ),
    )
    out_ref[:, 2048:] = extra.astype(jnp.bfloat16)


def join9_kernel(got_ref, tail_ref, tail_level_ref, out_ref):
    parts = [lambda j, i=i: got_ref[i, :, j * 128 : (j + 1) * 128] for i in range(NZ)]
    levels = [level_of(got_ref[i, :, 2048:]) for i in range(NZ)]
    parts.append(lambda j: tail_ref[:, j * 128 : (j + 1) * 128])
    levels.append(tail_level_ref[...])
    heads, _ = join(parts, levels)
    for j, value in enumerate(heads):
        out_ref[:, j * 128 : (j + 1) * 128] = value.astype(jnp.bfloat16)


def stats_kernel(a_ref, b_ref, c_ref, d_ref, allowed_ref, column_ref, out_ref, l_ref):
    refs = (a_ref, b_ref, c_ref, d_ref)
    rows = a_ref.shape[0]
    width = allowed_ref.shape[1] * 128

    def summed(lo):
        part = [r[:, lo : lo + 128].astype(jnp.float32) for r in refs]
        return (part[0] + part[1]) + (part[2] + part[3])

    extra = summed(width)
    second = (extra[:, 0:1] + extra[:, 1:2] + extra[:, 2:3]) / 5120.0
    scale = lax.rsqrt(second + epsilon)
    lane = lax.broadcasted_iota(jnp.int32, (rows, 128), 1)
    column = column_ref[...]
    high = jnp.full((rows, 128), lowest, jnp.float32)
    pick = jnp.zeros((rows, 128), jnp.float32)
    for j in range(width // 128):
        logit = summed(j * 128) * scale
        pick += jnp.where(lane + j * 128 == column, logit, 0.0)
        logit = jnp.where(allowed_ref[:, j : j + 1] > 0, logit, lowest)
        l_ref[:, j * 128 : (j + 1) * 128] = logit
        high = jnp.maximum(high, logit)
    top = jnp.max(high, axis=1, keepdims=True)
    total = jnp.zeros((rows, 128), jnp.float32)
    for j in range(width // 128):
        logit = l_ref[:, j * 128 : (j + 1) * 128]
        total += jnp.where(allowed_ref[:, j : j + 1] > 0, jnp.exp(logit - top), 0.0)
    total = jnp.sum(total, axis=1, keepdims=True)
    pick = jnp.sum(pick, axis=1, keepdims=True)
    table = jnp.where(lane == 0, top, jnp.where(lane == 1, total, jnp.where(lane == 2, pick, 0.0)))
    out_ref[...] = jnp.transpose(table)[:8]


def per_device(
    queries,
    prefix_kv,
    tail_kv,
    row_prompt,
    prefix_len,
    tail_len,
    out_weight,
    residual,
    norm_gain,
    vocab_weight,
    allowed,
    next_token,
):
    rows_dev, heads, head_dim = queries.shape
    kv_heads = tail_kv.shape[3]
    tail_width = tail_kv.shape[2]
    group = heads // kv_heads
    width = heads * head_dim
    owner = lax.axis_index("ctx")
    x = lax.axis_index("tp")
    y, z, c = owner // (NZ * NC), (owner // NC) % NZ, owner % NC
    inv_root = 1.0 / math.sqrt(head_dim)
    span = prefix_kv.shape[2]

    flat_q = queries.reshape(rows_dev, width)
    q_z = lax.all_to_all(
        jnp.broadcast_to(flat_q[None], (NZ, rows_dev, width)),
        "ctx",
        split_axis=0,
        concat_axis=0,
        tiled=True,
        axis_index_groups=z_groups,
    ).reshape(NZ * rows_dev, width)
    kv_own = prefix_kv.reshape(2, 2, span, kv_heads * head_dim)
    kv_other = lax.ppermute(kv_own, "ctx", core_swap)

    weight_all = lax.all_gather(
        out_weight, "ctx", axis=1, tiled=True, axis_index_groups=zc_groups
    )
    residual_t = lax.ppermute(residual, ("ctx", "tp"), turned(0))
    residual_all = lax.all_gather(
        residual_t, "ctx", axis=1, tiled=True, axis_index_groups=zc_groups
    )
    residual_rows = lax.dynamic_slice_in_dim(
        residual_all, (z * NC + c) * rows_dev, rows_dev, 0
    ).astype(jnp.float32)

    own_queries = queries.reshape(rows_dev, kv_heads, group, head_dim)
    tail_scores = (
        jnp.einsum(
            "rhgd,rkhd->rhgk", own_queries, tail_kv[:, 0], preferred_element_type=jnp.float32
        )
        * inv_root
    )
    tail_keep = (jnp.arange(tail_width, dtype=jnp.int32)[None, :] < tail_len[:, None])[
        :, None, None, :
    ]
    tail_high = jnp.max(jnp.where(tail_keep, tail_scores, lowest), axis=-1)
    tail_weights = jnp.where(tail_keep, jnp.exp(tail_scores - tail_high[..., None]), 0.0).astype(
        jnp.bfloat16
    )
    tail_total = jnp.sum(tail_weights.astype(jnp.float32), axis=-1)
    tail_sum = jnp.einsum(
        "rhgk,rkhd->rhgd", tail_weights, tail_kv[:, 1], preferred_element_type=jnp.float32
    )
    tail_out = (tail_sum / tail_total[..., None]).reshape(rows_dev, width)
    tail_level = (tail_high * LOG2E + jnp.log2(tail_total)).reshape(rows_dev, heads)
    tail_level = jnp.pad(tail_level, ((0, 0), (0, 128 - heads)))

    base = jnp.stack([owner * span, (owner + 1 - 2 * c) * span])
    limit = jnp.clip(prefix_len[:, None] - base[None, :], 0, span)
    reach = jnp.where(
        row_prompt[:, None, None] == jnp.arange(2, dtype=jnp.int32)[None, :, None],
        limit[:, None, :],
        0,
    ).reshape(NY, NZ, NC, rows_dev, 4)
    reach = lax.dynamic_index_in_dim(reach, c, 2, keepdims=False).reshape(NY, NZ * rows_dev, 4)

    def attend(q, k):
        mine = lax.dynamic_index_in_dim(reach, (y + NY - k) % NY, 0, keepdims=False)
        return call(
            attend_kernel,
            jax.ShapeDtypeStruct((NZ * rows_dev, width + 128), jnp.bfloat16),
            (q, kv_own, kv_other, mine),
            flops=2 * 2 * 64 * 2048 * 2048,
            scratch=[VMEM((4 * NZ * rows_dev, 4 * span), jnp.float32)],
        )

    visitors = {k: lax.ppermute(q_z, "ctx", y_shift(k)) for k in (1, 3, 2)}
    partial = [attend(q_z, 0)]
    for k in (1, 3, 2):
        partial.append(lax.ppermute(attend(visitors[k], k), "ctx", y_shift(-k)))
    joined = call(
        join4_kernel,
        jax.ShapeDtypeStruct((NZ * rows_dev, width + 128), jnp.bfloat16),
        tuple(partial),
        flops=1000000,
    )
    got = lax.all_to_all(
        joined.reshape(NZ, rows_dev, width + 128),
        "ctx",
        split_axis=0,
        concat_axis=0,
        tiled=True,
        axis_index_groups=z_groups,
    )
    attended = call(
        join9_kernel,
        jax.ShapeDtypeStruct((rows_dev, width), jnp.bfloat16),
        (got, tail_out, tail_level),
        flops=1000000,
    )

    rows_y = jnp.concatenate(
        [attended] + [lax.ppermute(attended, "ctx", y_shift(k)) for k in (1, 2, 3)], axis=0
    )
    projected = jnp.dot(rows_y, weight_all, preferred_element_type=jnp.float32).astype(
        jnp.bfloat16
    )
    model_part = projected.shape[1]
    projected = projected.reshape(NY, rows_dev, model_part)
    stream = residual_rows
    for s in range(NY):
        piece = lax.dynamic_index_in_dim(projected, (y + 2 * NY - x - s) % NY, 0, keepdims=False)
        stream = stream + lax.ppermute(piece, ("ctx", "tp"), turned(s)).astype(jnp.float32)
    stream = stream.astype(jnp.bfloat16).astype(jnp.float32)
    gain = lax.dynamic_slice_in_dim(norm_gain, x * model_part, model_part, 0)
    second = jnp.sum(stream * stream, axis=-1, keepdims=True)
    hi = lax.reduce_precision(second, 8, 7)
    mid = lax.reduce_precision(second - hi, 8, 7)
    lo = second - hi - mid
    scaled = jnp.concatenate(
        [
            stream * gain.astype(jnp.float32)[None],
            hi,
            mid,
            lo,
            jnp.zeros((rows_dev, 125), jnp.float32),
        ],
        axis=1,
    ).astype(jnp.bfloat16)

    scaled_other = lax.ppermute(scaled, "ctx", core_swap)
    pair = jnp.concatenate(
        [jnp.where(c == 0, scaled, scaled_other), jnp.where(c == 0, scaled_other, scaled)], axis=0
    )
    block = lax.all_to_all(
        jnp.broadcast_to(pair[None], (NZ,) + pair.shape),
        "ctx",
        split_axis=0,
        concat_axis=0,
        tiled=True,
        axis_index_groups=z_groups,
    ).reshape(NZ * 2 * rows_dev, model_part + 128)
    blocks = jnp.stack([block] + [lax.ppermute(block, "ctx", y_shift(k)) for k in (1, 2, 3)])

    def logits_for(s):
        rows = lax.dynamic_index_in_dim(blocks, (y + 2 * NY - x - s) % NY, 0, keepdims=False)
        part = jnp.dot(rows[:, :model_part], vocab_weight, preferred_element_type=jnp.float32)
        return jnp.concatenate([part.astype(jnp.bfloat16), rows[:, model_part:]], axis=1)

    sums = [lax.ppermute(logits_for(s), "tp", x_shift(s)) for s in (2, 1, 3)]
    sums.append(logits_for(0))
    vocab_here = vocab_weight.shape[1]
    local_rows = next_token.shape[0]
    stats = call(
        stats_kernel,
        jax.ShapeDtypeStruct((8, local_rows), jnp.float32),
        tuple(sums) + (allowed, (next_token - owner * vocab_here)[:, None]),
        flops=1000000,
        scratch=[VMEM((local_rows, vocab_here), jnp.float32)],
    )
    every = lax.all_to_all(
        jnp.broadcast_to(stats[None], (NY * NZ * NC,) + stats.shape),
        "ctx",
        split_axis=0,
        concat_axis=0,
        tiled=True,
    )
    peak = jnp.max(every[:, 0], axis=0)
    total = jnp.sum(every[:, 1] * jnp.exp(every[:, 0] - peak[None]), axis=0)
    logprob = jnp.sum(every[:, 2], axis=0) - (peak + jnp.log(total))
    return (attended, logprob)


def solution(mesh):
    placed = (
        P("ctx", "tp", None),
        P(None, None, "ctx", "tp", None),
        P("ctx", None, None, "tp", None),
        P(),
        P(),
        P("ctx"),
        P("tp", "ctx"),
        P("tp", "ctx"),
        P(),
        P("tp", "ctx"),
        P("tp", "ctx"),
        P("tp"),
    )
    return jax.shard_map(
        per_device, mesh=mesh, in_specs=placed, out_specs=(P("ctx", "tp"), P("tp")), check_vma=False
    )
```

```python
import math

import jax
import jax.numpy as jnp
from jax import lax
from jax.experimental import pallas as pl
from jax.experimental.pallas import tpu as pltpu
from jax.sharding import PartitionSpec as P

lowest = -1e30
epsilon = 1e-06
LOG2E = 1.4426950408889634
NY, NZ, NC, NX = 4, 8, 2, 4
VMEM = pltpu.VMEM


def ctx_id(y, z, c):
    return (y % NY) * (NZ * NC) + (z % NZ) * NC + c % NC


def chips():
    return [(y, z, c) for y in range(NY) for z in range(NZ) for c in range(NC)]


core_swap = [(ctx_id(y, z, c), ctx_id(y, z, 1 - c)) for y, z, c in chips()]
z_groups = [[ctx_id(y, z, c) for z in range(NZ)] for y in range(NY) for c in range(NC)]


def y_shift(d):
    return [(ctx_id(y, z, c), ctx_id(y + d, z, c)) for y, z, c in chips()]


def x_shift(d):
    return [(t, (t + d) % NX) for t in range(NX)]


def turned(s):
    return [
        (ctx_id(y, z, c) * NX + t, ctx_id(t + s, z, c) * NX + y)
        for t in range(NX)
        for y, z, c in chips()
    ]


def split3(value):
    hi = value.astype(jnp.bfloat16).astype(jnp.float32)
    rest = value - hi
    mid = rest.astype(jnp.bfloat16).astype(jnp.float32)
    return hi, mid, rest - mid


def call(kernel, out_shape, args, flops, scratch=(), place=None, limit=24):
    size = sum(math.prod(a.shape) * a.dtype.itemsize for a in args)
    specs = [pl.BlockSpec(memory_space=VMEM)] * len(args)
    if place is not None:
        specs = [pl.BlockSpec(memory_space=pltpu.SMEM)] + specs
        args = (place,) + tuple(args)
    return pl.pallas_call(
        kernel,
        out_shape=out_shape,
        in_specs=specs,
        out_specs=jax.tree.map(lambda _: pl.BlockSpec(memory_space=VMEM), out_shape),
        scratch_shapes=list(scratch),
        compiler_params=pltpu.CompilerParams(vmem_limit_bytes=limit * 1024 * 1024),
        cost_estimate=pl.CostEstimate(flops=flops, bytes_accessed=size, transcendentals=0),
    )(*args)


def attend_kernel(q_ref, own_ref, other_ref, reach_ref, out_ref, s_ref):
    rows = q_ref.shape[0]
    span = own_ref.shape[2]
    factor = LOG2E / math.sqrt(128)
    lane = lax.broadcasted_iota(jnp.int32, (rows, 128), 1)
    key = lax.broadcasted_iota(jnp.int32, (rows, span), 1)
    extra = jnp.zeros((rows, 128), jnp.float32)
    blocks = [(ref, p) for p in range(2) for ref in (own_ref, other_ref)]
    ones = jnp.ones((span, 128), jnp.bfloat16)
    for h in range(2):
        for half in range(2):
            heads = [h * 8 + half * 4 + g for g in range(4)]
            q = jnp.concatenate([q_ref[:, j * 128 : (j + 1) * 128] for j in heads], axis=0)
            high = jnp.full((4 * rows, 1), lowest, jnp.float32)
            for b, (ref, p) in enumerate(blocks):
                s = lax.dot_general(
                    q,
                    ref[p, 0, :, h * 128 : (h + 1) * 128],
                    (((1,), (1,)), ((), ())),
                    preferred_element_type=jnp.float32,
                )
                keep = key < reach_ref[:, b : b + 1]
                s = jnp.concatenate(
                    [
                        jnp.where(keep, s[g * rows : (g + 1) * rows] * factor, lowest)
                        for g in range(4)
                    ],
                    axis=0,
                )
                s_ref[:, b * span : (b + 1) * span] = s
                high = jnp.maximum(high, jnp.max(s, axis=1, keepdims=True))
            acc = jnp.zeros((4 * rows, 256), jnp.float32)
            for b, (ref, p) in enumerate(blocks):
                w = jnp.exp2(s_ref[:, b * span : (b + 1) * span] - high).astype(jnp.bfloat16)
                v = jnp.concatenate([ref[p, 1, :, h * 128 : (h + 1) * 128], ones], axis=1)
                acc += jnp.dot(w, v, preferred_element_type=jnp.float32)
            for g, j in enumerate(heads):
                part = slice(g * rows, (g + 1) * rows)
                total = acc[part, 128:]
                out_ref[:, j * 128 : (j + 1) * 128] = (acc[part, :128] / total).astype(jnp.bfloat16)
                level = high[part] + jnp.log2(total)
                for i, piece in enumerate(split3(level)):
                    extra = jnp.where(lane == j + 16 * i, piece, extra)
    out_ref[:, 2048:] = extra.astype(jnp.bfloat16)


def level_of(extra):
    extra = extra.astype(jnp.float32)
    return extra + pltpu.roll(extra, 112, 1) + pltpu.roll(extra, 96, 1)


def join(parts, levels):
    high = levels[0]
    for level in levels[1:]:
        high = jnp.maximum(high, level)
    shares = [jnp.exp2(level - high) for level in levels]
    total = shares[0]
    for share in shares[1:]:
        total = total + share
    shares = [share / total for share in shares]
    heads = []
    for j in range(16):
        value = None
        for part, share in zip(parts, shares):
            term = part(j).astype(jnp.float32) * share[:, j : j + 1]
            value = term if value is None else value + term
        heads.append(value)
    return heads, high + jnp.log2(total)


def join4_kernel(a_ref, b_ref, c_ref, d_ref, out_ref):
    refs = (a_ref, b_ref, c_ref, d_ref)
    parts = [lambda j, r=r: r[:, j * 128 : (j + 1) * 128] for r in refs]
    heads, level = join(parts, [level_of(r[:, 2048:]) for r in refs])
    lane = lax.broadcasted_iota(jnp.int32, level.shape, 1)
    for j, value in enumerate(heads):
        out_ref[:, j * 128 : (j + 1) * 128] = value.astype(jnp.bfloat16)
    hi, mid, lo = split3(level)
    extra = jnp.where(
        lane < 16,
        hi,
        jnp.where(
            lane < 32,
            pltpu.roll(mid, 16, 1),
            jnp.where(lane < 48, pltpu.roll(lo, 32, 1), 0.0),
        ),
    )
    out_ref[:, 2048:] = extra.astype(jnp.bfloat16)


def join9_kernel(got_ref, tail_ref, tail_level_ref, out_ref, copies_ref):
    parts = [lambda j, i=i: got_ref[i, :, j * 128 : (j + 1) * 128] for i in range(NZ)]
    levels = [level_of(got_ref[i, :, 2048:]) for i in range(NZ)]
    parts.append(lambda j: tail_ref[:, j * 128 : (j + 1) * 128])
    levels.append(tail_level_ref[...])
    heads, _ = join(parts, levels)
    for j, value in enumerate(heads):
        value = value.astype(jnp.bfloat16)
        out_ref[:, j * 128 : (j + 1) * 128] = value
        for i in range(NZ):
            copies_ref[i, :, j * 128 : (j + 1) * 128] = value


def project_kernel(place_ref, own_ref, other_ref, w0_ref, w1_ref, w2_ref, w3_ref, out_ref, rows_ref):
    c, y = place_ref[0], place_ref[1]
    rows_ref[c] = own_ref[...]
    rows_ref[1 - c] = other_ref[...]
    rows = jnp.concatenate([rows_ref[0], rows_ref[1]], axis=0)
    for j, w_ref in enumerate((w0_ref, w1_ref, w2_ref, w3_ref)):
        part = lax.dot_general(
            w_ref[...], rows, (((1,), (1,)), ((), ())), preferred_element_type=jnp.float32
        )
        out_ref[lax.rem(y + j, NY)] = part.astype(jnp.bfloat16)


def stream_kernel(got_ref, residual_ref, gain_ref, out_ref):
    total = residual_ref[...].astype(jnp.float32)
    for t in range(NX):
        total = total + got_ref[t].astype(jnp.float32)
    stream = total.astype(jnp.bfloat16).astype(jnp.float32)
    second = jnp.sum(stream * stream, axis=0, keepdims=True)
    hi, mid, lo = split3(second)
    row = lax.broadcasted_iota(jnp.int32, (16, stream.shape[1]), 0)
    extra = jnp.where(row == 0, hi, jnp.where(row == 1, mid, jnp.where(row == 2, lo, 0.0)))
    scaled = (stream * gain_ref[...]).astype(jnp.bfloat16)
    extra = extra.astype(jnp.bfloat16)
    count = stream.shape[0]
    for i in range(NZ):
        out_ref[i, :count] = scaled
        out_ref[i, count:] = extra


def logits_kernel(place_ref, *refs):
    mine, theirs, w_ref = refs[:4], refs[4:8], refs[8]
    outs, a_ref = refs[9:13], refs[13]
    c, turn = place_ref[0], place_ref[2]
    for k in range(NY):
        a_ref[c, k] = mine[k][...]
        a_ref[1 - c, k] = theirs[k][...]
    chunk = mine[0].shape[0] // NZ
    count = chunk - 16
    lefts = []
    for s, out_ref in enumerate(outs):
        k = lax.rem(turn + NY - s, NY)
        left = jnp.concatenate(
            [
                a_ref[d, k, z * chunk : z * chunk + count]
                for z in range(NZ)
                for d in range(NC)
            ],
            axis=0,
        )
        extra = jnp.zeros((16, 128), jnp.float32)
        for z in range(NZ):
            for d in range(NC):
                extra += a_ref[d, k, z * chunk + count : (z + 1) * chunk].astype(jnp.float32)
        second = extra[0:1] + extra[1:2] + extra[2:3]
        hi, mid, lo = split3(second)
        row = lax.broadcasted_iota(jnp.int32, (128, 128), 0)
        table = jnp.where(row == 0, hi, jnp.where(row == 1, mid, jnp.where(row == 2, lo, 0.0)))
        out_ref[:, w_ref.shape[1] :] = jnp.transpose(table).astype(jnp.bfloat16)
        lefts.append(jnp.transpose(left))
    lefts = jnp.concatenate(lefts, axis=0)
    for n in range(w_ref.shape[1] // 512):
        part = jnp.dot(
            lefts, w_ref[:, n * 512 : (n + 1) * 512], preferred_element_type=jnp.float32
        ).astype(jnp.bfloat16)
        for s, out_ref in enumerate(outs):
            out_ref[:, n * 512 : (n + 1) * 512] = part[s * 128 : (s + 1) * 128]


def stats_kernel(a_ref, b_ref, c_ref, d_ref, allowed_ref, column_ref, out_ref, l_ref):
    refs = (a_ref, b_ref, c_ref, d_ref)
    rows = a_ref.shape[0]
    width = allowed_ref.shape[1] * 128

    def summed(lo):
        part = [r[:, lo : lo + 128].astype(jnp.float32) for r in refs]
        return (part[0] + part[1]) + (part[2] + part[3])

    extra = summed(width)
    second = (extra[:, 0:1] + extra[:, 1:2] + extra[:, 2:3]) / 5120.0
    scale = lax.rsqrt(second + epsilon)
    lane = lax.broadcasted_iota(jnp.int32, (rows, 128), 1)
    column = column_ref[...]
    high = jnp.full((rows, 128), lowest, jnp.float32)
    pick = jnp.zeros((rows, 128), jnp.float32)
    for j in range(width // 128):
        logit = summed(j * 128) * scale
        pick += jnp.where(lane + j * 128 == column, logit, 0.0)
        logit = jnp.where(allowed_ref[:, j : j + 1] > 0, logit, lowest)
        l_ref[:, j * 128 : (j + 1) * 128] = logit
        high = jnp.maximum(high, logit)
    top = jnp.max(high, axis=1, keepdims=True)
    total = jnp.zeros((rows, 128), jnp.float32)
    for j in range(width // 128):
        logit = l_ref[:, j * 128 : (j + 1) * 128]
        total += jnp.where(allowed_ref[:, j : j + 1] > 0, jnp.exp(logit - top), 0.0)
    total = jnp.sum(total, axis=1, keepdims=True)
    pick = jnp.sum(pick, axis=1, keepdims=True)
    table = jnp.where(lane == 0, top, jnp.where(lane == 1, total, jnp.where(lane == 2, pick, 0.0)))
    out_ref[...] = jnp.transpose(table)[:8]


def per_device(
    queries,
    prefix_kv,
    tail_kv,
    row_prompt,
    prefix_len,
    tail_len,
    out_weight,
    residual,
    norm_gain,
    vocab_weight,
    allowed,
    next_token,
):
    rows_dev, heads, head_dim = queries.shape
    kv_heads = tail_kv.shape[3]
    tail_width = tail_kv.shape[2]
    group = heads // kv_heads
    width = heads * head_dim
    owner = lax.axis_index("ctx")
    x = lax.axis_index("tp")
    y, z, c = owner // (NZ * NC), (owner // NC) % NZ, owner % NC
    inv_root = 1.0 / math.sqrt(head_dim)
    span = prefix_kv.shape[2]

    flat_q = queries.reshape(rows_dev, width)
    q_z = lax.all_to_all(
        jnp.broadcast_to(flat_q[None], (NZ, rows_dev, width)),
        "ctx",
        split_axis=0,
        concat_axis=0,
        tiled=True,
        axis_index_groups=z_groups,
    ).reshape(NZ * rows_dev, width)
    kv_own = prefix_kv.reshape(2, 2, span, kv_heads * head_dim)
    kv_other = lax.ppermute(kv_own, "ctx", core_swap)

    weight_own = out_weight.T
    weights = [weight_own] + [lax.ppermute(weight_own, "ctx", y_shift(-k)) for k in (1, 2, 3)]
    local_rows = residual.shape[0]

    def core_major(array):
        rest = array.shape[1:]
        array = array.reshape((NZ, NC, rows_dev) + rest)
        return jnp.swapaxes(array, 0, 1).reshape((local_rows,) + rest)

    residual_t = lax.ppermute(core_major(residual).T, ("ctx", "tp"), turned(0))
    columns_dev = residual.shape[1]
    gain = lax.dynamic_slice_in_dim(
        norm_gain, (x * NZ * NC + z * NC + c) * columns_dev, columns_dev, 0
    ).astype(jnp.float32)
    gain = jnp.broadcast_to(gain[:, None], (columns_dev, local_rows))
    place = jnp.stack([c, y, (y + NY - x) % NY, x]).astype(jnp.int32)

    own_queries = queries.reshape(rows_dev, kv_heads, group, head_dim)
    tail_scores = (
        jnp.einsum(
            "rhgd,rkhd->rhgk", own_queries, tail_kv[:, 0], preferred_element_type=jnp.float32
        )
        * inv_root
    )
    tail_keep = (jnp.arange(tail_width, dtype=jnp.int32)[None, :] < tail_len[:, None])[
        :, None, None, :
    ]
    tail_high = jnp.max(jnp.where(tail_keep, tail_scores, lowest), axis=-1)
    tail_weights = jnp.where(tail_keep, jnp.exp(tail_scores - tail_high[..., None]), 0.0).astype(
        jnp.bfloat16
    )
    tail_total = jnp.sum(tail_weights.astype(jnp.float32), axis=-1)
    tail_sum = jnp.einsum(
        "rhgk,rkhd->rhgd", tail_weights, tail_kv[:, 1], preferred_element_type=jnp.float32
    )
    tail_out = (tail_sum / tail_total[..., None]).reshape(rows_dev, width)
    tail_level = (tail_high * LOG2E + jnp.log2(tail_total)).reshape(rows_dev, heads)
    tail_level = jnp.pad(tail_level, ((0, 0), (0, 128 - heads)))

    base = jnp.stack([owner * span, (owner + 1 - 2 * c) * span])
    limit = jnp.clip(prefix_len[:, None] - base[None, :], 0, span)
    reach = jnp.where(
        row_prompt[:, None, None] == jnp.arange(2, dtype=jnp.int32)[None, :, None],
        limit[:, None, :],
        0,
    ).reshape(NY, NZ, NC, rows_dev, 4)
    reach = lax.dynamic_index_in_dim(reach, c, 2, keepdims=False).reshape(NY, NZ * rows_dev, 4)

    def attend(q, k):
        mine = lax.dynamic_index_in_dim(reach, (y + NY - k) % NY, 0, keepdims=False)
        return call(
            attend_kernel,
            jax.ShapeDtypeStruct((NZ * rows_dev, width + 128), jnp.bfloat16),
            (q, kv_own, kv_other, mine),
            flops=2 * 2 * 64 * 2048 * 2048,
            scratch=[VMEM((4 * NZ * rows_dev, 4 * span), jnp.float32)],
        )

    visitors = {k: lax.ppermute(q_z, "ctx", y_shift(k)) for k in (1, 3, 2)}
    partial = [attend(q_z, 0)]
    for k in (1, 3, 2):
        partial.append(lax.ppermute(attend(visitors[k], k), "ctx", y_shift(-k)))
    joined = call(
        join4_kernel,
        jax.ShapeDtypeStruct((NZ * rows_dev, width + 128), jnp.bfloat16),
        tuple(partial),
        flops=1000000,
    )
    got = lax.all_to_all(
        joined.reshape(NZ, rows_dev, width + 128),
        "ctx",
        split_axis=0,
        concat_axis=0,
        tiled=True,
        axis_index_groups=z_groups,
    )
    attended, copies = call(
        join9_kernel,
        (
            jax.ShapeDtypeStruct((rows_dev, width), jnp.bfloat16),
            jax.ShapeDtypeStruct((NZ, rows_dev, width), jnp.bfloat16),
        ),
        (got, tail_out, tail_level),
        flops=1000000,
    )

    rows_own = lax.all_to_all(
        copies, "ctx", split_axis=0, concat_axis=0, tiled=True, axis_index_groups=z_groups
    ).reshape(NZ * rows_dev, width)
    rows_other = lax.ppermute(rows_own, "ctx", core_swap)
    projected = call(
        project_kernel,
        jax.ShapeDtypeStruct((NY, columns_dev, local_rows), jnp.bfloat16),
        (rows_own, rows_other) + tuple(weights),
        flops=2 * 128 * 320 * 2048,
        scratch=[VMEM((NC, NZ * rows_dev, width), jnp.bfloat16)],
        place=place,
    )
    pieces = lax.all_to_all(projected, "tp", split_axis=0, concat_axis=0, tiled=True)
    streams = call(
        stream_kernel,
        jax.ShapeDtypeStruct((NZ, columns_dev + 16, local_rows), jnp.bfloat16),
        (pieces, residual_t, gain),
        flops=1000000,
    )

    block = lax.all_to_all(
        streams, "ctx", split_axis=0, concat_axis=0, tiled=True, axis_index_groups=z_groups
    ).reshape(NZ * (columns_dev + 16), local_rows)
    mine = [block] + [lax.ppermute(block, "ctx", y_shift(k)) for k in (1, 2, 3)]
    theirs = [lax.ppermute(one, "ctx", core_swap) for one in mine]
    vocab_here = vocab_weight.shape[1]
    message = jax.ShapeDtypeStruct((local_rows, vocab_here + 128), jnp.bfloat16)
    parts = call(
        logits_kernel,
        (message,) * NX,
        tuple(mine) + tuple(theirs) + (vocab_weight,),
        flops=2 * 512 * 1280 * 2048,
        scratch=[VMEM((NC, NY) + block.shape, jnp.bfloat16)],
        place=place,
        limit=32,
    )
    sums = [parts[0]] + [lax.ppermute(parts[s], "tp", x_shift(s)) for s in (2, 1, 3)]
    stats = call(
        stats_kernel,
        jax.ShapeDtypeStruct((8, local_rows), jnp.float32),
        tuple(sums)
        + (core_major(allowed), core_major((next_token - owner * vocab_here)[:, None])),
        flops=1000000,
        scratch=[VMEM((local_rows, vocab_here), jnp.float32)],
    )[:3]
    every = lax.all_to_all(
        jnp.broadcast_to(stats[None], (NY * NZ * NC,) + stats.shape),
        "ctx",
        split_axis=0,
        concat_axis=0,
        tiled=True,
    )
    peak = jnp.max(every[:, 0], axis=0)
    total = jnp.sum(every[:, 1] * jnp.exp(every[:, 0] - peak[None]), axis=0)
    logprob = jnp.sum(every[:, 2], axis=0) - (peak + jnp.log(total))
    logprob = jnp.swapaxes(logprob.reshape(NC, NZ, rows_dev), 0, 1).reshape(local_rows)
    return (attended, logprob)


def solution(mesh):
    placed = (
        P("ctx", "tp", None),
        P(None, None, "ctx", "tp", None),
        P("ctx", None, None, "tp", None),
        P(),
        P(),
        P("ctx"),
        P("tp", "ctx"),
        P("tp", "ctx"),
        P(),
        P("tp", "ctx"),
        P("tp", "ctx"),
        P("tp"),
    )
    return jax.shard_map(
        per_device, mesh=mesh, in_specs=placed, out_specs=(P("ctx", "tp"), P("tp")), check_vma=False
    )
```

```python
import functools
import math

import jax
import jax.numpy as jnp
from jax import lax
from jax.experimental import pallas as pl
from jax.experimental.pallas import tpu as pltpu
from jax.sharding import PartitionSpec as P

lowest = -1e30
epsilon = 1e-06
LOG2E = 1.4426950408889634
NY, NZ, NC, NX = 4, 8, 2, 4
VMEM = pltpu.VMEM


def ctx_id(y, z, c):
    return (y % NY) * (NZ * NC) + (z % NZ) * NC + c % NC


def chips():
    return [(y, z, c) for y in range(NY) for z in range(NZ) for c in range(NC)]


core_swap = [(ctx_id(y, z, c), ctx_id(y, z, 1 - c)) for y, z, c in chips()]
z_groups = [[ctx_id(y, z, c) for z in range(NZ)] for y in range(NY) for c in range(NC)]


def y_shift(d):
    return [(ctx_id(y, z, c), ctx_id(y + d, z, c)) for y, z, c in chips()]


def x_shift(d):
    return [(t, (t + d) % NX) for t in range(NX)]


def turned(s):
    return [
        (ctx_id(y, z, c) * NX + t, ctx_id(t + s, z, c) * NX + y)
        for t in range(NX)
        for y, z, c in chips()
    ]


def split3(value):
    hi = value.astype(jnp.bfloat16).astype(jnp.float32)
    rest = value - hi
    mid = rest.astype(jnp.bfloat16).astype(jnp.float32)
    return hi, mid, rest - mid


def call(kernel, out_shape, args, flops, scratch=(), place=None, limit=24, far=()):
    size = sum(math.prod(a.shape) * a.dtype.itemsize for a in args)
    specs = [
        pl.BlockSpec(memory_space=pl.ANY if i in far else VMEM) for i in range(len(args))
    ]
    if place is not None:
        specs = [pl.BlockSpec(memory_space=pltpu.SMEM)] + specs
        args = (place,) + tuple(args)
    return pl.pallas_call(
        kernel,
        out_shape=out_shape,
        in_specs=specs,
        out_specs=jax.tree.map(lambda _: pl.BlockSpec(memory_space=VMEM), out_shape),
        scratch_shapes=list(scratch),
        compiler_params=pltpu.CompilerParams(vmem_limit_bytes=limit * 1024 * 1024),
        cost_estimate=pl.CostEstimate(flops=flops, bytes_accessed=size, transcendentals=0),
    )(*args)


def copies_kernel(q_ref, out_ref):
    for j in range(q_ref.shape[1]):
        part = q_ref[:, j, :]
        for i in range(out_ref.shape[0]):
            out_ref[i, :, j * 128 : (j + 1) * 128] = part


def attend_kernel(first, rows, q_ref, own_ref, other_ref, reach_ref, out_ref, s_ref):
    span = own_ref.shape[2]
    factor = LOG2E / math.sqrt(128)
    each = 256 // rows
    here = slice(first, first + rows)
    lane = lax.broadcasted_iota(jnp.int32, (rows, 128), 1)
    key = lax.broadcasted_iota(jnp.int32, (rows, span), 1)
    extra = jnp.zeros((rows, 128), jnp.float32)
    blocks = [(ref, p) for p in range(2) for ref in (own_ref, other_ref)]
    ones = jnp.ones((span, 128), jnp.bfloat16)

    def score(step):
        h = step * each // 8
        q = jnp.concatenate(
            [q_ref[here, j * 128 : (j + 1) * 128] for j in range(step * each, (step + 1) * each)],
            axis=0,
        )
        high = jnp.full((each * rows, 1), lowest, jnp.float32)
        for b, (ref, p) in enumerate(blocks):
            s = lax.dot_general(
                q,
                ref[p, 0, :, h * 128 : (h + 1) * 128],
                (((1,), (1,)), ((), ())),
                preferred_element_type=jnp.float32,
            )
            keep = key < reach_ref[here, b : b + 1]
            s = jnp.concatenate(
                [
                    jnp.where(keep, s[g * rows : (g + 1) * rows] * factor, lowest)
                    for g in range(each)
                ],
                axis=0,
            )
            s_ref[step % 2, :, b * span : (b + 1) * span] = s
            high = jnp.maximum(high, jnp.max(s, axis=1, keepdims=True))
        return high

    steps = 16 // each
    later = score(0)
    for step in range(steps):
        high = later
        if step + 1 < steps:
            later = score(step + 1)
        h = step * each // 8
        acc = jnp.zeros((each * rows, 256), jnp.float32)
        for b, (ref, p) in enumerate(blocks):
            w = jnp.exp2(s_ref[step % 2, :, b * span : (b + 1) * span] - high).astype(jnp.bfloat16)
            v = jnp.concatenate([ref[p, 1, :, h * 128 : (h + 1) * 128], ones], axis=1)
            acc += jnp.dot(w, v, preferred_element_type=jnp.float32)
        for g in range(each):
            j = step * each + g
            part = slice(g * rows, (g + 1) * rows)
            total = acc[part, 128:]
            out_ref[:, j * 128 : (j + 1) * 128] = (acc[part, :128] / total).astype(jnp.bfloat16)
            level = high[part] + jnp.log2(total)
            for i, piece in enumerate(split3(level)):
                extra = jnp.where(lane == j + 16 * i, piece, extra)
    out_ref[:, 2048:] = extra.astype(jnp.bfloat16)


def level_of(extra):
    extra = extra.astype(jnp.float32)
    return extra + pltpu.roll(extra, 112, 1) + pltpu.roll(extra, 96, 1)


def join(parts, levels):
    high = levels[0]
    for level in levels[1:]:
        high = jnp.maximum(high, level)
    shares = [jnp.exp2(level - high) for level in levels]
    total = shares[0]
    for share in shares[1:]:
        total = total + share
    shares = [share / total for share in shares]
    heads = []
    for j in range(16):
        value = None
        for part, share in zip(parts, shares):
            term = part(j).astype(jnp.float32) * share[:, j : j + 1]
            value = term if value is None else value + term
        heads.append(value)
    return heads, high + jnp.log2(total)


def join4_kernel(low_ref, high_ref, b_ref, c_ref, d_ref, out_ref):
    refs = (b_ref, c_ref, d_ref)

    def own(columns):
        return jnp.concatenate([low_ref[:, columns], high_ref[:, columns]], axis=0)

    parts = [lambda j: own(slice(j * 128, (j + 1) * 128))]
    parts += [lambda j, r=r: r[:, j * 128 : (j + 1) * 128] for r in refs]
    levels = [level_of(own(slice(2048, 2176)))] + [level_of(r[:, 2048:]) for r in refs]
    heads, level = join(parts, levels)
    lane = lax.broadcasted_iota(jnp.int32, level.shape, 1)
    for j, value in enumerate(heads):
        out_ref[:, j * 128 : (j + 1) * 128] = value.astype(jnp.bfloat16)
    hi, mid, lo = split3(level)
    extra = jnp.where(
        lane < 16,
        hi,
        jnp.where(
            lane < 32,
            pltpu.roll(mid, 16, 1),
            jnp.where(lane < 48, pltpu.roll(lo, 32, 1), 0.0),
        ),
    )
    out_ref[:, 2048:] = extra.astype(jnp.bfloat16)


def join9_kernel(got_ref, tail_ref, tail_level_ref, out_ref, copies_ref):
    parts = [lambda j, i=i: got_ref[i, :, j * 128 : (j + 1) * 128] for i in range(NZ)]
    levels = [level_of(got_ref[i, :, 2048:]) for i in range(NZ)]
    parts.append(lambda j: tail_ref[:, j * 128 : (j + 1) * 128])
    levels.append(tail_level_ref[...])
    heads, _ = join(parts, levels)
    for j, value in enumerate(heads):
        value = value.astype(jnp.bfloat16)
        out_ref[:, j * 128 : (j + 1) * 128] = value
        for i in range(NZ):
            copies_ref[i, :, j * 128 : (j + 1) * 128] = value


def project_kernel(place_ref, own_ref, other_ref, w0_ref, w1_ref, w2_ref, w3_ref, out_ref, rows_ref):
    c, y = place_ref[0], place_ref[1]
    rows_ref[c] = own_ref[...]
    rows_ref[1 - c] = other_ref[...]
    rows = jnp.concatenate([rows_ref[0], rows_ref[1]], axis=0)
    for j, w_ref in enumerate((w0_ref, w1_ref, w2_ref, w3_ref)):
        part = lax.dot_general(
            w_ref[...], rows, (((1,), (1,)), ((), ())), preferred_element_type=jnp.float32
        )
        out_ref[lax.rem(y + j, NY)] = part.astype(jnp.bfloat16)


def stream_kernel(got_ref, residual_ref, gain_ref, out_ref):
    total = residual_ref[...].astype(jnp.float32)
    for t in range(NX):
        total = total + got_ref[t].astype(jnp.float32)
    stream = total.astype(jnp.bfloat16).astype(jnp.float32)
    second = jnp.sum(stream * stream, axis=0, keepdims=True)
    hi, mid, lo = split3(second)
    row = lax.broadcasted_iota(jnp.int32, (16, stream.shape[1]), 0)
    extra = jnp.where(row == 0, hi, jnp.where(row == 1, mid, jnp.where(row == 2, lo, 0.0)))
    scaled = (stream * gain_ref[...]).astype(jnp.bfloat16)
    extra = extra.astype(jnp.bfloat16)
    count = stream.shape[0]
    for i in range(NZ):
        out_ref[i, :count] = scaled
        out_ref[i, count:] = extra


def logits_kernel(place_ref, *refs):
    mine, theirs, w_hbm = refs[:4], refs[4:8], refs[8]
    own_ref, halves, a_ref, w_ref, sems = refs[9], refs[10:16], refs[16], refs[17], refs[18]
    blocks, _, span = w_ref.shape
    copies = [
        pltpu.make_async_copy(w_hbm.at[:, pl.ds(n * span, span)], w_ref.at[n], sems.at[n])
        for n in range(blocks)
    ]
    for copy in copies:
        copy.start()
    c, turn = place_ref[0], place_ref[2]
    for k in range(NY):
        a_ref[c, k] = mine[k][...]
        a_ref[1 - c, k] = theirs[k][...]
    chunk = mine[0].shape[0] // NZ
    count = chunk - 16

    def put(s, columns, value):
        if s == 0:
            own_ref[:, columns] = value
        else:
            halves[2 * s - 2][:, columns] = value[:64]
            halves[2 * s - 1][:, columns] = value[64:]

    lefts = []
    for s in range(NX):
        k = lax.rem(turn + NY - s, NY)
        left = jnp.concatenate(
            [
                a_ref[d, k, z * chunk : z * chunk + count]
                for z in range(NZ)
                for d in range(NC)
            ],
            axis=0,
        )
        extra = jnp.zeros((16, 128), jnp.float32)
        for z in range(NZ):
            for d in range(NC):
                extra += a_ref[d, k, z * chunk + count : (z + 1) * chunk].astype(jnp.float32)
        second = extra[0:1] + extra[1:2] + extra[2:3]
        hi, mid, lo = split3(second)
        row = lax.broadcasted_iota(jnp.int32, (128, 128), 0)
        table = jnp.where(row == 0, hi, jnp.where(row == 1, mid, jnp.where(row == 2, lo, 0.0)))
        put(s, slice(blocks * span, blocks * span + 128), jnp.transpose(table).astype(jnp.bfloat16))
        lefts.append(jnp.transpose(left))
    lefts = jnp.concatenate(lefts, axis=0)
    for n in range(blocks):
        copies[n].wait()
        part = jnp.dot(lefts, w_ref[n], preferred_element_type=jnp.float32).astype(jnp.bfloat16)
        for s in range(NX):
            put(s, slice(n * span, (n + 1) * span), part[s * 128 : (s + 1) * 128])


def add_kernel(a_ref, b_ref, c_ref, d_ref, ab_ref, cd_ref):
    for one, two, out_ref in ((a_ref, b_ref, ab_ref), (c_ref, d_ref, cd_ref)):
        width = one.shape[1] - 128
        value = one[:, :width].astype(jnp.float32) + two[:, :width].astype(jnp.float32)
        out_ref[:, :width] = value.astype(jnp.bfloat16)
        extra = one[:, width:].astype(jnp.float32) + two[:, width:].astype(jnp.float32)
        second = extra[:, 0:1] + extra[:, 1:2] + extra[:, 2:3]
        hi, mid, lo = split3(second)
        lane = lax.broadcasted_iota(jnp.int32, extra.shape, 1)
        extra = jnp.where(lane == 0, hi, jnp.where(lane == 1, mid, jnp.where(lane == 2, lo, 0.0)))
        out_ref[:, width:] = extra.astype(jnp.bfloat16)


def stats_kernel(own_ref, a_ref, b_ref, c_ref, d_ref, allowed_ref, column_ref, out_ref, l_ref):
    rows = own_ref.shape[0]
    width = allowed_ref.shape[1] * 128

    def summed(lo):
        part = [r[:, lo : lo + 128].astype(jnp.float32) for r in (a_ref, b_ref, c_ref, d_ref)]
        others = jnp.concatenate([part[0] + part[1], part[2] + part[3]], axis=0)
        return own_ref[:, lo : lo + 128].astype(jnp.float32) + others

    extra = summed(width)
    second = (extra[:, 0:1] + extra[:, 1:2] + extra[:, 2:3]) / 5120.0
    scale = lax.rsqrt(second + epsilon)
    lane = lax.broadcasted_iota(jnp.int32, (rows, 128), 1)
    column = column_ref[...]
    high = jnp.full((rows, 128), lowest, jnp.float32)
    pick = jnp.zeros((rows, 128), jnp.float32)
    for j in range(width // 128):
        logit = summed(j * 128) * scale
        pick += jnp.where(lane + j * 128 == column, logit, 0.0)
        logit = jnp.where(allowed_ref[:, j : j + 1] > 0, logit, lowest)
        l_ref[:, j * 128 : (j + 1) * 128] = logit
        high = jnp.maximum(high, logit)
    top = jnp.max(high, axis=1, keepdims=True)
    total = jnp.zeros((rows, 128), jnp.float32)
    for j in range(width // 128):
        logit = l_ref[:, j * 128 : (j + 1) * 128]
        total += jnp.where(allowed_ref[:, j : j + 1] > 0, jnp.exp(logit - top), 0.0)
    total = jnp.sum(total, axis=1, keepdims=True)
    pick = jnp.sum(pick, axis=1, keepdims=True)
    table = jnp.where(lane == 0, top, jnp.where(lane == 1, total, jnp.where(lane == 2, pick, 0.0)))
    out_ref[...] = jnp.transpose(table)[:8]


def per_device(
    queries,
    prefix_kv,
    tail_kv,
    row_prompt,
    prefix_len,
    tail_len,
    out_weight,
    residual,
    norm_gain,
    vocab_weight,
    allowed,
    next_token,
):
    rows_dev, heads, head_dim = queries.shape
    kv_heads = tail_kv.shape[3]
    tail_width = tail_kv.shape[2]
    group = heads // kv_heads
    width = heads * head_dim
    owner = lax.axis_index("ctx")
    x = lax.axis_index("tp")
    y, z, c = owner // (NZ * NC), (owner // NC) % NZ, owner % NC
    inv_root = 1.0 / math.sqrt(head_dim)
    span = prefix_kv.shape[2]

    q_z = lax.all_to_all(
        call(
            copies_kernel,
            jax.ShapeDtypeStruct((NZ, rows_dev, width), jnp.bfloat16),
            (queries,),
            flops=1000,
        ),
        "ctx",
        split_axis=0,
        concat_axis=0,
        tiled=True,
        axis_index_groups=z_groups,
    ).reshape(NZ * rows_dev, width)
    kv_own = prefix_kv.reshape(2, 2, span, kv_heads * head_dim)
    kv_other = lax.ppermute(kv_own, "ctx", core_swap)

    weight_own = out_weight.T
    weights = [weight_own] + [lax.ppermute(weight_own, "ctx", y_shift(-k)) for k in (1, 2, 3)]
    local_rows = residual.shape[0]

    def core_major(array):
        rest = array.shape[1:]
        array = array.reshape((NZ, NC, rows_dev) + rest)
        return jnp.swapaxes(array, 0, 1).reshape((local_rows,) + rest)

    residual_t = lax.ppermute(core_major(residual).T, ("ctx", "tp"), turned(0))
    columns_dev = residual.shape[1]
    gain = lax.dynamic_slice_in_dim(
        norm_gain, (x * NZ * NC + z * NC + c) * columns_dev, columns_dev, 0
    ).astype(jnp.float32)
    gain = jnp.broadcast_to(gain[:, None], (columns_dev, local_rows))
    place = jnp.stack([c, y, (y + NY - x) % NY, x]).astype(jnp.int32)

    own_queries = queries.reshape(rows_dev, kv_heads, group, head_dim)
    tail_scores = (
        jnp.einsum(
            "rhgd,rkhd->rhgk", own_queries, tail_kv[:, 0], preferred_element_type=jnp.float32
        )
        * inv_root
    )
    tail_keep = (jnp.arange(tail_width, dtype=jnp.int32)[None, :] < tail_len[:, None])[
        :, None, None, :
    ]
    tail_high = jnp.max(jnp.where(tail_keep, tail_scores, lowest), axis=-1)
    tail_weights = jnp.where(tail_keep, jnp.exp(tail_scores - tail_high[..., None]), 0.0).astype(
        jnp.bfloat16
    )
    tail_total = jnp.sum(tail_weights.astype(jnp.float32), axis=-1)
    tail_sum = jnp.einsum(
        "rhgk,rkhd->rhgd", tail_weights, tail_kv[:, 1], preferred_element_type=jnp.float32
    )
    tail_out = (tail_sum / tail_total[..., None]).reshape(rows_dev, width)
    tail_level = (tail_high * LOG2E + jnp.log2(tail_total)).reshape(rows_dev, heads)
    tail_level = jnp.pad(tail_level, ((0, 0), (0, 128 - heads)))

    base = jnp.stack([owner * span, (owner + 1 - 2 * c) * span])
    limit = jnp.clip(prefix_len[:, None] - base[None, :], 0, span)
    reach = jnp.where(
        row_prompt[:, None, None] == jnp.arange(2, dtype=jnp.int32)[None, :, None],
        limit[:, None, :],
        0,
    ).reshape(NY, NZ, NC, rows_dev, 4)
    reach = lax.dynamic_index_in_dim(reach, c, 2, keepdims=False).reshape(NY, NZ * rows_dev, 4)

    def attend(q, k, first=0, rows=NZ * rows_dev):
        mine = lax.dynamic_index_in_dim(reach, (y + NY - k) % NY, 0, keepdims=False)
        return call(
            functools.partial(attend_kernel, first, rows),
            jax.ShapeDtypeStruct((rows, width + 128), jnp.bfloat16),
            (q, kv_own, kv_other, mine),
            flops=2 * 2 * rows * 2048 * 2048,
            scratch=[VMEM((2, 256, 4 * span), jnp.float32)],
        )

    tied = lax.optimization_barrier((q_z, kv_other) + tuple(weights))
    q_z, kv_other, weights = tied[0], tied[1], list(tied[2:])
    half = NZ * rows_dev // 2
    visitors = {k: lax.ppermute(q_z, "ctx", y_shift(k)) for k in (2, 1, 3)}
    own_low = attend(q_z, 0, 0, half)
    back = {}
    last = own_low
    for k in (2, 1, 3):
        visitor, last = lax.optimization_barrier((visitors[k], last))
        last = attend(visitor, k)
        back[k] = lax.ppermute(last, "ctx", y_shift(-k))
    q_last, last = lax.optimization_barrier((q_z, last))
    own_high = attend(q_last, 0, half, half)
    joined = call(
        join4_kernel,
        jax.ShapeDtypeStruct((NZ * rows_dev, width + 128), jnp.bfloat16),
        (own_low, own_high, back[2], back[1], back[3]),
        flops=1000000,
    )
    got = lax.all_to_all(
        joined.reshape(NZ, rows_dev, width + 128),
        "ctx",
        split_axis=0,
        concat_axis=0,
        tiled=True,
        axis_index_groups=z_groups,
    )
    attended, copies = call(
        join9_kernel,
        (
            jax.ShapeDtypeStruct((rows_dev, width), jnp.bfloat16),
            jax.ShapeDtypeStruct((NZ, rows_dev, width), jnp.bfloat16),
        ),
        (got, tail_out, tail_level),
        flops=1000000,
    )

    rows_own = lax.all_to_all(
        copies, "ctx", split_axis=0, concat_axis=0, tiled=True, axis_index_groups=z_groups
    ).reshape(NZ * rows_dev, width)
    rows_other = lax.ppermute(rows_own, "ctx", core_swap)
    projected = call(
        project_kernel,
        jax.ShapeDtypeStruct((NY, columns_dev, local_rows), jnp.bfloat16),
        (rows_own, rows_other) + tuple(weights),
        flops=2 * 128 * 320 * 2048,
        scratch=[VMEM((NC, NZ * rows_dev, width), jnp.bfloat16)],
        place=place,
    )
    pieces = lax.all_to_all(projected, "tp", split_axis=0, concat_axis=0, tiled=True)
    streams = call(
        stream_kernel,
        jax.ShapeDtypeStruct((NZ, columns_dev + 16, local_rows), jnp.bfloat16),
        (pieces, residual_t, gain),
        flops=1000000,
    )

    block = lax.all_to_all(
        streams, "ctx", split_axis=0, concat_axis=0, tiled=True, axis_index_groups=z_groups
    ).reshape(NZ * (columns_dev + 16), local_rows)
    mine = [block] + [lax.ppermute(block, "ctx", y_shift(k)) for k in (1, 2, 3)]
    theirs = [lax.ppermute(one, "ctx", core_swap) for one in mine]
    vocab_here = vocab_weight.shape[1]
    whole = jax.ShapeDtypeStruct((local_rows, vocab_here + 128), jnp.bfloat16)
    part = jax.ShapeDtypeStruct((local_rows // 2, vocab_here + 128), jnp.bfloat16)
    own, low1, high1, low2, high2, low3, high3 = call(
        logits_kernel,
        (whole,) + (part,) * 6,
        tuple(mine) + tuple(theirs) + (vocab_weight,),
        flops=2 * 512 * 1280 * 2048,
        scratch=[
            VMEM((NC, NY) + block.shape, jnp.bfloat16),
            VMEM((4, vocab_weight.shape[0], vocab_here // 4), jnp.bfloat16),
            pltpu.SemaphoreType.DMA((4,)),
        ],
        place=place,
        limit=32,
        far=(8,),
    )
    up, down = x_shift(1), x_shift(3)
    via_up = lax.ppermute(low2, "tp", up)
    via_down = lax.ppermute(high2, "tp", down)
    high_up = lax.ppermute(high1, "tp", up)
    low_down = lax.ppermute(low3, "tp", down)
    low_sum, high_sum = call(
        add_kernel, (part, part), (via_up, low1, via_down, high3), flops=1000000
    )
    low_up = lax.ppermute(low_sum, "tp", up)
    high_down = lax.ppermute(high_sum, "tp", down)
    sums = (own, low_up, low_down, high_up, high_down)
    stats = call(
        stats_kernel,
        jax.ShapeDtypeStruct((8, local_rows), jnp.float32),
        tuple(sums)
        + (core_major(allowed), core_major((next_token - owner * vocab_here)[:, None])),
        flops=1000000,
        scratch=[VMEM((local_rows, vocab_here), jnp.float32)],
    )[:3]
    every = lax.all_to_all(
        jnp.broadcast_to(stats[None], (NY * NZ * NC,) + stats.shape),
        "ctx",
        split_axis=0,
        concat_axis=0,
        tiled=True,
    )
    peak = jnp.max(every[:, 0], axis=0)
    total = jnp.sum(every[:, 1] * jnp.exp(every[:, 0] - peak[None]), axis=0)
    logprob = jnp.sum(every[:, 2], axis=0) - (peak + jnp.log(total))
    logprob = jnp.swapaxes(logprob.reshape(NC, NZ, rows_dev), 0, 1).reshape(local_rows)
    return (attended, logprob)


def solution(mesh):
    placed = (
        P("ctx", "tp", None),
        P(None, None, "ctx", "tp", None),
        P("ctx", None, None, "tp", None),
        P(),
        P(),
        P("ctx"),
        P("tp", "ctx"),
        P("tp", "ctx"),
        P(),
        P("tp", "ctx"),
        P("tp", "ctx"),
        P("tp"),
    )
    return jax.shard_map(
        per_device, mesh=mesh, in_specs=placed, out_specs=(P("ctx", "tp"), P("tp")), check_vma=False
    )
```

```python
import functools
import math

import jax
import jax.numpy as jnp
from jax import lax
from jax.experimental import pallas as pl
from jax.experimental.pallas import tpu as pltpu
from jax.sharding import PartitionSpec as P

lowest = -1e30
epsilon = 1e-06
LOG2E = 1.4426950408889634
NY, NZ, NC, NX = 4, 8, 2, 4
VMEM = pltpu.VMEM


def ctx_id(y, z, c):
    return (y % NY) * (NZ * NC) + (z % NZ) * NC + c % NC


def chips():
    return [(y, z, c) for y in range(NY) for z in range(NZ) for c in range(NC)]


core_swap = [(ctx_id(y, z, c), ctx_id(y, z, 1 - c)) for y, z, c in chips()]
z_groups = [[ctx_id(y, z, c) for z in range(NZ)] for y in range(NY) for c in range(NC)]


def y_shift(d):
    return [(ctx_id(y, z, c), ctx_id(y + d, z, c)) for y, z, c in chips()]


def x_shift(d):
    return [(t, (t + d) % NX) for t in range(NX)]


def turned(s):
    return [
        (ctx_id(y, z, c) * NX + t, ctx_id(t + s, z, c) * NX + y)
        for t in range(NX)
        for y, z, c in chips()
    ]


def split3(value):
    hi = value.astype(jnp.bfloat16).astype(jnp.float32)
    rest = value - hi
    mid = rest.astype(jnp.bfloat16).astype(jnp.float32)
    return hi, mid, rest - mid


def call(kernel, out_shape, args, flops, scratch=(), place=None, limit=24, far=()):
    size = sum(math.prod(a.shape) * a.dtype.itemsize for a in args)
    specs = [
        pl.BlockSpec(memory_space=pltpu.HBM if i in far else VMEM) for i in range(len(args))
    ]
    if place is not None:
        specs = [pl.BlockSpec(memory_space=pltpu.SMEM)] + specs
        args = (place,) + tuple(args)
    return pl.pallas_call(
        kernel,
        out_shape=out_shape,
        in_specs=specs,
        out_specs=jax.tree.map(lambda _: pl.BlockSpec(memory_space=VMEM), out_shape),
        scratch_shapes=list(scratch),
        compiler_params=pltpu.CompilerParams(vmem_limit_bytes=limit * 1024 * 1024),
        cost_estimate=pl.CostEstimate(flops=flops, bytes_accessed=size, transcendentals=0),
    )(*args)


def copies_kernel(q_ref, out_ref):
    for j in range(q_ref.shape[1]):
        part = q_ref[:, j, :]
        for i in range(out_ref.shape[0]):
            out_ref[i, :, j * 128 : (j + 1) * 128] = part


def sort_kernel(q_ref, order_ref, out_ref):
    out_ref[...] = jnp.dot(
        order_ref[...], q_ref[...], preferred_element_type=jnp.float32
    ).astype(jnp.bfloat16)


def attend_kernel(first_ref, q_ref, own_ref, other_ref, reach_ref, out_ref, s_ref):
    count = first_ref[0]
    span = own_ref.shape[2]
    rows = 16
    factor = LOG2E / math.sqrt(128)
    lane = lax.broadcasted_iota(jnp.int32, (rows, 128), 1)
    key = lax.broadcasted_iota(jnp.int32, (rows, span), 1)
    ones = jnp.ones((span, 128), jnp.bfloat16)

    def tile(start, p):
        here = slice(start, start + rows)
        fresh = lax.broadcasted_iota(jnp.int32, (rows, 128), 0) + start >= count
        keeps = [
            key < reach_ref[here, 2 * p + b : 2 * p + b + 1] for b in range(2)
        ]

        def score(h):
            q = jnp.concatenate(
                [q_ref[here, j * 128 : (j + 1) * 128] for j in range(h * 8, h * 8 + 8)], axis=0
            )
            high = jnp.full((8 * rows, 1), lowest, jnp.float32)
            for b, ref in enumerate((own_ref, other_ref)):
                s = lax.dot_general(
                    q,
                    ref[p, 0, :, h * 128 : (h + 1) * 128],
                    (((1,), (1,)), ((), ())),
                    preferred_element_type=jnp.float32,
                )
                s = jnp.concatenate(
                    [
                        jnp.where(keeps[b], s[g * rows : (g + 1) * rows] * factor, lowest)
                        for g in range(8)
                    ],
                    axis=0,
                )
                s_ref[h, :, b * span : (b + 1) * span] = s
                high = jnp.maximum(high, jnp.max(s, axis=1, keepdims=True))
            return high

        extra = jnp.zeros((rows, 128), jnp.float32)
        highs = [score(h) for h in range(2)]
        for h, high in enumerate(highs):
            acc = jnp.zeros((8 * rows, 256), jnp.float32)
            for b, ref in enumerate((own_ref, other_ref)):
                w = jnp.exp2(s_ref[h, :, b * span : (b + 1) * span] - high).astype(jnp.bfloat16)
                v = jnp.concatenate([ref[p, 1, :, h * 128 : (h + 1) * 128], ones], axis=1)
                acc += jnp.dot(w, v, preferred_element_type=jnp.float32)
            for g in range(8):
                j = h * 8 + g
                part = slice(g * rows, (g + 1) * rows)
                columns = slice(j * 128, (j + 1) * 128)
                total = acc[part, 128:]
                value = acc[part, :128] / total
                if p == 1:
                    value = jnp.where(fresh, value, out_ref[here, columns].astype(jnp.float32))
                out_ref[here, columns] = value.astype(jnp.bfloat16)
                level = high[part] + jnp.log2(total)
                for i, piece in enumerate(split3(level)):
                    extra = jnp.where(lane == j + 16 * i, piece, extra)
        if p == 1:
            extra = jnp.where(fresh, extra, out_ref[here, 2048:].astype(jnp.float32))
        out_ref[here, 2048:] = extra.astype(jnp.bfloat16)

    for start in range(0, q_ref.shape[0], rows):

        @pl.when(count > start)
        def _():
            tile(start, 0)

        @pl.when(count < start + rows)
        def _():
            tile(start, 1)


def level_of(extra):
    extra = extra.astype(jnp.float32)
    return extra + pltpu.roll(extra, 112, 1) + pltpu.roll(extra, 96, 1)


def join(parts, levels):
    high = levels[0]
    for level in levels[1:]:
        high = jnp.maximum(high, level)
    shares = [jnp.exp2(level - high) for level in levels]
    total = shares[0]
    for share in shares[1:]:
        total = total + share
    shares = [share / total for share in shares]
    heads = []
    for j in range(16):
        value = None
        for part, share in zip(parts, shares):
            term = part(j).astype(jnp.float32) * share[:, j : j + 1]
            value = term if value is None else value + term
        heads.append(value)
    return heads, high + jnp.log2(total)


def join4_kernel(a_ref, b_ref, c_ref, d_ref, order_ref, out_ref, sorted_ref):
    refs = (a_ref, b_ref, c_ref, d_ref)
    parts = [lambda j, r=r: r[:, j * 128 : (j + 1) * 128] for r in refs]
    heads, level = join(parts, [level_of(r[:, 2048:]) for r in refs])
    lane = lax.broadcasted_iota(jnp.int32, level.shape, 1)
    for j, value in enumerate(heads):
        sorted_ref[:, j * 128 : (j + 1) * 128] = value.astype(jnp.bfloat16)
    hi, mid, lo = split3(level)
    extra = jnp.where(
        lane < 16,
        hi,
        jnp.where(
            lane < 32,
            pltpu.roll(mid, 16, 1),
            jnp.where(lane < 48, pltpu.roll(lo, 32, 1), 0.0),
        ),
    )
    sorted_ref[:, 2048:] = extra.astype(jnp.bfloat16)
    out_ref[...] = jnp.dot(
        order_ref[...], sorted_ref[...], preferred_element_type=jnp.float32
    ).astype(jnp.bfloat16)


def join9_kernel(got_ref, tail_ref, tail_level_ref, out_ref, copies_ref):
    parts = [lambda j, i=i: got_ref[i, :, j * 128 : (j + 1) * 128] for i in range(NZ)]
    levels = [level_of(got_ref[i, :, 2048:]) for i in range(NZ)]
    parts.append(lambda j: tail_ref[:, j * 128 : (j + 1) * 128])
    levels.append(tail_level_ref[...])
    heads, _ = join(parts, levels)
    for j, value in enumerate(heads):
        value = value.astype(jnp.bfloat16)
        out_ref[:, j * 128 : (j + 1) * 128] = value
        for i in range(NZ):
            copies_ref[i, :, j * 128 : (j + 1) * 128] = value


def project_kernel(place_ref, own_ref, other_ref, w0_ref, w1_ref, w2_ref, w3_ref, out_ref, rows_ref):
    c, y = place_ref[0], place_ref[1]
    rows_ref[c] = own_ref[...]
    rows_ref[1 - c] = other_ref[...]
    rows = jnp.concatenate([rows_ref[0], rows_ref[1]], axis=0)
    for j, w_ref in enumerate((w0_ref, w1_ref, w2_ref, w3_ref)):
        part = lax.dot_general(
            w_ref[...], rows, (((1,), (1,)), ((), ())), preferred_element_type=jnp.float32
        )
        out_ref[lax.rem(y + j, NY)] = part.astype(jnp.bfloat16)


def stream_kernel(got_ref, residual_ref, gain_ref, out_ref):
    total = residual_ref[...].astype(jnp.float32)
    for t in range(NX):
        total = total + got_ref[t].astype(jnp.float32)
    stream = total.astype(jnp.bfloat16).astype(jnp.float32)
    second = jnp.sum(stream * stream, axis=0, keepdims=True)
    hi, mid, lo = split3(second)
    row = lax.broadcasted_iota(jnp.int32, (16, stream.shape[1]), 0)
    extra = jnp.where(row == 0, hi, jnp.where(row == 1, mid, jnp.where(row == 2, lo, 0.0)))
    scaled = (stream * gain_ref[...]).astype(jnp.bfloat16)
    extra = extra.astype(jnp.bfloat16)
    count = stream.shape[0]
    for i in range(NZ):
        out_ref[i, :count] = scaled
        out_ref[i, count:] = extra


def fetch_kernel(w_hbm, out_ref, sem):
    copy = pltpu.make_async_copy(w_hbm, out_ref, sem)
    copy.start()
    copy.wait()


def logits_kernel(place_ref, *refs):
    mine, theirs, w_ref = refs[:4], refs[4:8], refs[8]
    own_ref, halves, a_ref = refs[9], refs[10:16], refs[16]
    span = 512
    blocks = w_ref.shape[1] // span
    c, turn = place_ref[0], place_ref[2]
    for k in range(NY):
        a_ref[c, k] = mine[k][...]
        a_ref[1 - c, k] = theirs[k][...]
    chunk = mine[0].shape[0] // NZ
    count = chunk - 16

    def put(s, columns, value):
        if s == 0:
            own_ref[:, columns] = value
        else:
            halves[2 * s - 2][:, columns] = value[:64]
            halves[2 * s - 1][:, columns] = value[64:]

    lefts = []
    for s in range(NX):
        k = lax.rem(turn + NY - s, NY)
        left = jnp.concatenate(
            [
                a_ref[d, k, z * chunk : z * chunk + count]
                for z in range(NZ)
                for d in range(NC)
            ],
            axis=0,
        )
        extra = jnp.zeros((16, 128), jnp.float32)
        for z in range(NZ):
            for d in range(NC):
                extra += a_ref[d, k, z * chunk + count : (z + 1) * chunk].astype(jnp.float32)
        second = extra[0:1] + extra[1:2] + extra[2:3]
        hi, mid, lo = split3(second)
        row = lax.broadcasted_iota(jnp.int32, (128, 128), 0)
        table = jnp.where(row == 0, hi, jnp.where(row == 1, mid, jnp.where(row == 2, lo, 0.0)))
        put(s, slice(blocks * span, blocks * span + 128), jnp.transpose(table).astype(jnp.bfloat16))
        lefts.append(jnp.transpose(left))
    lefts = jnp.concatenate(lefts, axis=0)
    for n in range(blocks):
        part = jnp.dot(
            lefts, w_ref[:, n * span : (n + 1) * span], preferred_element_type=jnp.float32
        ).astype(jnp.bfloat16)
        for s in range(NX):
            put(s, slice(n * span, (n + 1) * span), part[s * 128 : (s + 1) * 128])


def add_kernel(a_ref, b_ref, c_ref, d_ref, ab_ref, cd_ref):
    for one, two, out_ref in ((a_ref, b_ref, ab_ref), (c_ref, d_ref, cd_ref)):
        width = one.shape[1] - 128
        value = one[:, :width].astype(jnp.float32) + two[:, :width].astype(jnp.float32)
        out_ref[:, :width] = value.astype(jnp.bfloat16)
        extra = one[:, width:].astype(jnp.float32) + two[:, width:].astype(jnp.float32)
        second = extra[:, 0:1] + extra[:, 1:2] + extra[:, 2:3]
        hi, mid, lo = split3(second)
        lane = lax.broadcasted_iota(jnp.int32, extra.shape, 1)
        extra = jnp.where(lane == 0, hi, jnp.where(lane == 1, mid, jnp.where(lane == 2, lo, 0.0)))
        out_ref[:, width:] = extra.astype(jnp.bfloat16)


def stats_kernel(own_ref, a_ref, b_ref, c_ref, d_ref, allowed_ref, column_ref, out_ref, l_ref):
    rows = own_ref.shape[0]
    width = allowed_ref.shape[1] * 128

    def summed(lo):
        part = [r[:, lo : lo + 128].astype(jnp.float32) for r in (a_ref, b_ref, c_ref, d_ref)]
        others = jnp.concatenate([part[0] + part[1], part[2] + part[3]], axis=0)
        return own_ref[:, lo : lo + 128].astype(jnp.float32) + others

    extra = summed(width)
    second = (extra[:, 0:1] + extra[:, 1:2] + extra[:, 2:3]) / 5120.0
    scale = lax.rsqrt(second + epsilon)
    lane = lax.broadcasted_iota(jnp.int32, (rows, 128), 1)
    column = column_ref[...]
    high = jnp.full((rows, 128), lowest, jnp.float32)
    pick = jnp.zeros((rows, 128), jnp.float32)
    for j in range(width // 128):
        logit = summed(j * 128) * scale
        pick += jnp.where(lane + j * 128 == column, logit, 0.0)
        logit = jnp.where(allowed_ref[:, j : j + 1] > 0, logit, lowest)
        l_ref[:, j * 128 : (j + 1) * 128] = logit
        high = jnp.maximum(high, logit)
    top = jnp.max(high, axis=1, keepdims=True)
    total = jnp.zeros((rows, 128), jnp.float32)
    for j in range(width // 128):
        logit = l_ref[:, j * 128 : (j + 1) * 128]
        total += jnp.where(allowed_ref[:, j : j + 1] > 0, jnp.exp(logit - top), 0.0)
    total = jnp.sum(total, axis=1, keepdims=True)
    pick = jnp.sum(pick, axis=1, keepdims=True)
    table = jnp.where(lane == 0, top, jnp.where(lane == 1, total, jnp.where(lane == 2, pick, 0.0)))
    out_ref[...] = jnp.transpose(table)[:8]


def per_device(
    queries,
    prefix_kv,
    tail_kv,
    row_prompt,
    prefix_len,
    tail_len,
    out_weight,
    residual,
    norm_gain,
    vocab_weight,
    allowed,
    next_token,
):
    rows_dev, heads, head_dim = queries.shape
    kv_heads = tail_kv.shape[3]
    tail_width = tail_kv.shape[2]
    group = heads // kv_heads
    width = heads * head_dim
    owner = lax.axis_index("ctx")
    x = lax.axis_index("tp")
    y, z, c = owner // (NZ * NC), (owner // NC) % NZ, owner % NC
    inv_root = 1.0 / math.sqrt(head_dim)
    span = prefix_kv.shape[2]

    q_z = lax.all_to_all(
        call(
            copies_kernel,
            jax.ShapeDtypeStruct((NZ, rows_dev, width), jnp.bfloat16),
            (queries,),
            flops=1000,
        ),
        "ctx",
        split_axis=0,
        concat_axis=0,
        tiled=True,
        axis_index_groups=z_groups,
    ).reshape(NZ * rows_dev, width)
    kv_own = prefix_kv.reshape(2, 2, span, kv_heads * head_dim)
    kv_other = lax.ppermute(kv_own, "ctx", core_swap)

    weight_own = out_weight.T
    weights = [weight_own] + [lax.ppermute(weight_own, "ctx", y_shift(-k)) for k in (1, 2, 3)]
    local_rows = residual.shape[0]

    def core_major(array):
        rest = array.shape[1:]
        array = array.reshape((NZ, NC, rows_dev) + rest)
        return jnp.swapaxes(array, 0, 1).reshape((local_rows,) + rest)

    residual_t = lax.ppermute(core_major(residual).T, ("ctx", "tp"), turned(0))
    columns_dev = residual.shape[1]
    gain = lax.dynamic_slice_in_dim(
        norm_gain, (x * NZ * NC + z * NC + c) * columns_dev, columns_dev, 0
    ).astype(jnp.float32)
    gain = jnp.broadcast_to(gain[:, None], (columns_dev, local_rows))
    place = jnp.stack([c, y, (y + NY - x) % NY, x]).astype(jnp.int32)

    own_queries = queries.reshape(rows_dev, kv_heads, group, head_dim)
    tail_scores = (
        jnp.einsum(
            "rhgd,rkhd->rhgk", own_queries, tail_kv[:, 0], preferred_element_type=jnp.float32
        )
        * inv_root
    )
    tail_keep = (jnp.arange(tail_width, dtype=jnp.int32)[None, :] < tail_len[:, None])[
        :, None, None, :
    ]
    tail_high = jnp.max(jnp.where(tail_keep, tail_scores, lowest), axis=-1)
    tail_weights = jnp.where(tail_keep, jnp.exp(tail_scores - tail_high[..., None]), 0.0).astype(
        jnp.bfloat16
    )
    tail_total = jnp.sum(tail_weights.astype(jnp.float32), axis=-1)
    tail_sum = jnp.einsum(
        "rhgk,rkhd->rhgd", tail_weights, tail_kv[:, 1], preferred_element_type=jnp.float32
    )
    tail_out = (tail_sum / tail_total[..., None]).reshape(rows_dev, width)
    tail_level = (tail_high * LOG2E + jnp.log2(tail_total)).reshape(rows_dev, heads)
    tail_level = jnp.pad(tail_level, ((0, 0), (0, 128 - heads)))

    base = jnp.stack([owner * span, (owner + 1 - 2 * c) * span])
    limit = jnp.clip(prefix_len[:, None] - base[None, :], 0, span)
    reach = jnp.where(
        row_prompt[:, None, None] == jnp.arange(2, dtype=jnp.int32)[None, :, None],
        limit[:, None, :],
        0,
    ).reshape(NY, NZ, NC, rows_dev, 4)
    reach = lax.dynamic_index_in_dim(reach, c, 2, keepdims=False).reshape(NY, NZ * rows_dev, 4)

    group_rows = NZ * rows_dev
    prompt = lax.dynamic_index_in_dim(
        row_prompt.reshape(NY, NZ, NC, rows_dev), c, 2, keepdims=False
    ).reshape(NY, group_rows)
    index = jnp.arange(group_rows, dtype=jnp.int32)
    sort_key = prompt * group_rows + index[None]
    rank = jnp.sum((sort_key[:, None, :] < sort_key[:, :, None]).astype(jnp.int32), axis=-1)
    order = rank[:, None, :] == index[None, :, None]
    reach = jnp.sum(jnp.where(order[..., None], reach[:, None], 0), axis=2)
    firsts = jnp.sum((prompt == 0).astype(jnp.int32), axis=-1)
    order = lax.dynamic_index_in_dim(order, y, 0, keepdims=False).astype(jnp.bfloat16)
    back_order = order.T
    by_shift = [(y + NY - k) % NY for k in range(NY)]
    reaches = [lax.dynamic_index_in_dim(reach, i, 0, keepdims=False) for i in by_shift]
    firsts = [lax.dynamic_slice_in_dim(firsts, i, 1, 0) for i in by_shift]
    vocab_local = call(
        fetch_kernel,
        jax.ShapeDtypeStruct(vocab_weight.shape, jnp.bfloat16),
        (vocab_weight,),
        flops=1000,
        scratch=[pltpu.SemaphoreType.DMA],
        far=(0,),
    )
    q_z, kv_other, order, back_order, reaches, firsts, vocab_local = lax.optimization_barrier(
        (q_z, kv_other, order, back_order, reaches, firsts, vocab_local)
    )

    def attend(q, k):
        return call(
            attend_kernel,
            jax.ShapeDtypeStruct((group_rows, width + 128), jnp.bfloat16),
            (q, kv_own, kv_other, reaches[k]),
            flops=2 * 2 * group_rows * 2048 * 2048,
            scratch=[VMEM((2, 128, 2 * span), jnp.float32)],
            place=firsts[k],
        )

    q_sorted = call(
        sort_kernel,
        jax.ShapeDtypeStruct((group_rows, width), jnp.bfloat16),
        (q_z, order),
        flops=2 * group_rows * group_rows * width,
    )
    visitors = {k: lax.ppermute(q_sorted, "ctx", y_shift(k)) for k in (2, 1, 3)}
    own_part = attend(q_sorted, 0)
    back = {}
    last = own_part
    for k in (2, 1, 3):
        visitor, last = lax.optimization_barrier((visitors[k], last))
        last = attend(visitor, k)
        back[k] = lax.ppermute(last, "ctx", y_shift(-k))
    joined = call(
        join4_kernel,
        jax.ShapeDtypeStruct((group_rows, width + 128), jnp.bfloat16),
        (own_part, back[2], back[1], back[3], back_order),
        flops=1000000,
        scratch=[VMEM((group_rows, width + 128), jnp.bfloat16)],
    )
    got = lax.all_to_all(
        joined.reshape(NZ, rows_dev, width + 128),
        "ctx",
        split_axis=0,
        concat_axis=0,
        tiled=True,
        axis_index_groups=z_groups,
    )
    attended, copies = call(
        join9_kernel,
        (
            jax.ShapeDtypeStruct((rows_dev, width), jnp.bfloat16),
            jax.ShapeDtypeStruct((NZ, rows_dev, width), jnp.bfloat16),
        ),
        (got, tail_out, tail_level),
        flops=1000000,
    )

    copies, weights = lax.optimization_barrier((copies, weights))
    rows_own = lax.all_to_all(
        copies, "ctx", split_axis=0, concat_axis=0, tiled=True, axis_index_groups=z_groups
    ).reshape(NZ * rows_dev, width)
    rows_other = lax.ppermute(rows_own, "ctx", core_swap)
    projected = call(
        project_kernel,
        jax.ShapeDtypeStruct((NY, columns_dev, local_rows), jnp.bfloat16),
        (rows_own, rows_other) + tuple(weights),
        flops=2 * 128 * 320 * 2048,
        scratch=[VMEM((NC, NZ * rows_dev, width), jnp.bfloat16)],
        place=place,
    )
    pieces = lax.all_to_all(projected, "tp", split_axis=0, concat_axis=0, tiled=True)
    streams = call(
        stream_kernel,
        jax.ShapeDtypeStruct((NZ, columns_dev + 16, local_rows), jnp.bfloat16),
        (pieces, residual_t, gain),
        flops=1000000,
    )

    block = lax.all_to_all(
        streams, "ctx", split_axis=0, concat_axis=0, tiled=True, axis_index_groups=z_groups
    ).reshape(NZ * (columns_dev + 16), local_rows)
    mine = [block] + [lax.ppermute(block, "ctx", y_shift(k)) for k in (1, 2, 3)]
    theirs = [lax.ppermute(one, "ctx", core_swap) for one in mine]
    vocab_here = vocab_weight.shape[1]
    whole = jax.ShapeDtypeStruct((local_rows, vocab_here + 128), jnp.bfloat16)
    part = jax.ShapeDtypeStruct((local_rows // 2, vocab_here + 128), jnp.bfloat16)
    own, low1, high1, low2, high2, low3, high3 = call(
        logits_kernel,
        (whole,) + (part,) * 6,
        tuple(mine) + tuple(theirs) + (vocab_local,),
        flops=2 * 512 * 1280 * 2048,
        scratch=[
            VMEM((NC, NY) + block.shape, jnp.bfloat16),
        ],
        place=place,
        limit=24,
    )
    up, down = x_shift(1), x_shift(3)
    via_up = lax.ppermute(low2, "tp", up)
    via_down = lax.ppermute(high2, "tp", down)
    high_up = lax.ppermute(high1, "tp", up)
    low_down = lax.ppermute(low3, "tp", down)
    low_sum, high_sum = call(
        add_kernel, (part, part), (via_up, low1, via_down, high3), flops=1000000
    )
    low_up = lax.ppermute(low_sum, "tp", up)
    high_down = lax.ppermute(high_sum, "tp", down)
    sums = (own, low_up, low_down, high_up, high_down)
    stats = call(
        stats_kernel,
        jax.ShapeDtypeStruct((8, local_rows), jnp.float32),
        tuple(sums)
        + (core_major(allowed), core_major((next_token - owner * vocab_here)[:, None])),
        flops=1000000,
        scratch=[VMEM((local_rows, vocab_here), jnp.float32)],
    )[:3]
    every = lax.all_to_all(
        jnp.broadcast_to(stats[None], (NY * NZ * NC,) + stats.shape),
        "ctx",
        split_axis=0,
        concat_axis=0,
        tiled=True,
    )
    peak = jnp.max(every[:, 0], axis=0)
    total = jnp.sum(every[:, 1] * jnp.exp(every[:, 0] - peak[None]), axis=0)
    logprob = jnp.sum(every[:, 2], axis=0) - (peak + jnp.log(total))
    logprob = jnp.swapaxes(logprob.reshape(NC, NZ, rows_dev), 0, 1).reshape(local_rows)
    return (attended, logprob)


def solution(mesh):
    placed = (
        P("ctx", "tp", None),
        P(None, None, "ctx", "tp", None),
        P("ctx", None, None, "tp", None),
        P(),
        P(),
        P("ctx"),
        P("tp", "ctx"),
        P("tp", "ctx"),
        P(),
        P("tp", "ctx"),
        P("tp", "ctx"),
        P("tp"),
    )
    return jax.shard_map(
        per_device, mesh=mesh, in_specs=placed, out_specs=(P("ctx", "tp"), P("tp")), check_vma=False
    )
```

```python
import functools
import math

import jax
import jax.numpy as jnp
from jax import lax
from jax.experimental import pallas as pl
from jax.experimental.pallas import tpu as pltpu
from jax.sharding import PartitionSpec as P

lowest = -1e30
epsilon = 1e-06
LOG2E = 1.4426950408889634
NY, NZ, NC, NX = 4, 8, 2, 4
VMEM = pltpu.VMEM


def ctx_id(y, z, c):
    return (y % NY) * (NZ * NC) + (z % NZ) * NC + c % NC


def chips():
    return [(y, z, c) for y in range(NY) for z in range(NZ) for c in range(NC)]


core_swap = [(ctx_id(y, z, c), ctx_id(y, z, 1 - c)) for y, z, c in chips()]
z_groups = [[ctx_id(y, z, c) for z in range(NZ)] for y in range(NY) for c in range(NC)]


def y_shift(d):
    return [(ctx_id(y, z, c), ctx_id(y + d, z, c)) for y, z, c in chips()]


def x_shift(d):
    return [(t, (t + d) % NX) for t in range(NX)]


def turned(s):
    return [
        (ctx_id(y, z, c) * NX + t, ctx_id(t + s, z, c) * NX + y)
        for t in range(NX)
        for y, z, c in chips()
    ]


def split3(value):
    hi = value.astype(jnp.bfloat16).astype(jnp.float32)
    rest = value - hi
    mid = rest.astype(jnp.bfloat16).astype(jnp.float32)
    return hi, mid, rest - mid


def call(kernel, out_shape, args, flops, scratch=(), place=None, limit=24, far=()):
    size = sum(math.prod(a.shape) * a.dtype.itemsize for a in args)
    specs = [
        pl.BlockSpec(memory_space=pltpu.HBM if i in far else VMEM) for i in range(len(args))
    ]
    if place is not None:
        specs = [pl.BlockSpec(memory_space=pltpu.SMEM)] + specs
        args = (place,) + tuple(args)
    return pl.pallas_call(
        kernel,
        out_shape=out_shape,
        in_specs=specs,
        out_specs=jax.tree.map(lambda _: pl.BlockSpec(memory_space=VMEM), out_shape),
        scratch_shapes=list(scratch),
        compiler_params=pltpu.CompilerParams(vmem_limit_bytes=limit * 1024 * 1024),
        cost_estimate=pl.CostEstimate(flops=flops, bytes_accessed=size, transcendentals=0),
    )(*args)


def copies_kernel(q_ref, out_ref):
    for j in range(q_ref.shape[1]):
        part = q_ref[:, j, :]
        for i in range(out_ref.shape[0]):
            out_ref[i, :, j * 128 : (j + 1) * 128] = part


def attend_kernel(q_ref, own_ref, other_ref, reach_ref, out_ref, s_ref):
    rows = q_ref.shape[0]
    span = own_ref.shape[2]
    factor = LOG2E / math.sqrt(128)
    lane = lax.broadcasted_iota(jnp.int32, (rows, 128), 1)
    key = lax.broadcasted_iota(jnp.int32, (rows, span), 1)
    extra = jnp.zeros((rows, 128), jnp.float32)
    blocks = [(ref, p) for p in range(2) for ref in (own_ref, other_ref)]
    ones = jnp.ones((span, 128), jnp.bfloat16)
    for h in range(2):
        for half in range(2):
            heads = [h * 8 + half * 4 + g for g in range(4)]
            q = jnp.concatenate([q_ref[:, j * 128 : (j + 1) * 128] for j in heads], axis=0)
            high = jnp.full((4 * rows, 1), lowest, jnp.float32)
            for b, (ref, p) in enumerate(blocks):
                s = lax.dot_general(
                    q,
                    ref[p, 0, :, h * 128 : (h + 1) * 128],
                    (((1,), (1,)), ((), ())),
                    preferred_element_type=jnp.float32,
                )
                keep = key < reach_ref[:, b : b + 1]
                s = jnp.concatenate(
                    [jnp.where(keep, s[g * rows : (g + 1) * rows], lowest) for g in range(4)],
                    axis=0,
                )
                s_ref[:, b * span : (b + 1) * span] = s
                high = jnp.maximum(high, jnp.max(s, axis=1, keepdims=True))
            acc = jnp.zeros((4 * rows, 256), jnp.float32)
            for b, (ref, p) in enumerate(blocks):
                w = jnp.exp2((s_ref[:, b * span : (b + 1) * span] - high) * factor)
                v = jnp.concatenate([ref[p, 1, :, h * 128 : (h + 1) * 128], ones], axis=1)
                acc += jnp.dot(w.astype(jnp.bfloat16), v, preferred_element_type=jnp.float32)
            for g, j in enumerate(heads):
                part = slice(g * rows, (g + 1) * rows)
                total = acc[part, 128:]
                out_ref[:, j * 128 : (j + 1) * 128] = (acc[part, :128] / total).astype(jnp.bfloat16)
                level = high[part] * factor + jnp.log2(total)
                for i, piece in enumerate(split3(level)):
                    extra = jnp.where(lane == j + 16 * i, piece, extra)
    out_ref[:, 2048:] = extra.astype(jnp.bfloat16)


def level_of(extra):
    extra = extra.astype(jnp.float32)
    return extra + pltpu.roll(extra, 112, 1) + pltpu.roll(extra, 96, 1)


def join(parts, levels):
    high = levels[0]
    for level in levels[1:]:
        high = jnp.maximum(high, level)
    shares = [jnp.exp2(level - high) for level in levels]
    total = shares[0]
    for share in shares[1:]:
        total = total + share
    shares = [share / total for share in shares]
    heads = []
    for j in range(16):
        value = None
        for part, share in zip(parts, shares):
            term = part(j).astype(jnp.float32) * share[:, j : j + 1]
            value = term if value is None else value + term
        heads.append(value)
    return heads, high + jnp.log2(total)


def join4_kernel(a_ref, b_ref, c_ref, d_ref, out_ref):
    refs = (a_ref, b_ref, c_ref, d_ref)
    parts = [lambda j, r=r: r[:, j * 128 : (j + 1) * 128] for r in refs]
    heads, level = join(parts, [level_of(r[:, 2048:]) for r in refs])
    lane = lax.broadcasted_iota(jnp.int32, level.shape, 1)
    for j, value in enumerate(heads):
        out_ref[:, j * 128 : (j + 1) * 128] = value.astype(jnp.bfloat16)
    hi, mid, lo = split3(level)
    extra = jnp.where(
        lane < 16,
        hi,
        jnp.where(
            lane < 32,
            pltpu.roll(mid, 16, 1),
            jnp.where(lane < 48, pltpu.roll(lo, 32, 1), 0.0),
        ),
    )
    out_ref[:, 2048:] = extra.astype(jnp.bfloat16)


def join9_kernel(got_ref, tail_ref, tail_level_ref, out_ref, copies_ref):
    parts = [lambda j, i=i: got_ref[i, :, j * 128 : (j + 1) * 128] for i in range(NZ)]
    levels = [level_of(got_ref[i, :, 2048:]) for i in range(NZ)]
    parts.append(lambda j: tail_ref[:, j * 128 : (j + 1) * 128])
    levels.append(tail_level_ref[...])
    heads, _ = join(parts, levels)
    for j, value in enumerate(heads):
        value = value.astype(jnp.bfloat16)
        out_ref[:, j * 128 : (j + 1) * 128] = value
        for i in range(NZ):
            copies_ref[i, :, j * 128 : (j + 1) * 128] = value


def project_kernel(place_ref, own_ref, other_ref, w0_ref, w1_ref, w2_ref, w3_ref, out_ref, rows_ref):
    c, y = place_ref[0], place_ref[1]
    rows_ref[c] = own_ref[...]
    rows_ref[1 - c] = other_ref[...]
    rows = jnp.concatenate([rows_ref[0], rows_ref[1]], axis=0)
    for j, w_ref in enumerate((w0_ref, w1_ref, w2_ref, w3_ref)):
        part = lax.dot_general(
            w_ref[...], rows, (((1,), (1,)), ((), ())), preferred_element_type=jnp.float32
        )
        out_ref[lax.rem(y + j, NY)] = part.astype(jnp.bfloat16)


def stream_kernel(got_ref, residual_ref, gain_ref, out_ref):
    total = residual_ref[...].astype(jnp.float32)
    for t in range(NX):
        total = total + got_ref[t].astype(jnp.float32)
    stream = total.astype(jnp.bfloat16).astype(jnp.float32)
    second = jnp.sum(stream * stream, axis=0, keepdims=True)
    hi, mid, lo = split3(second)
    row = lax.broadcasted_iota(jnp.int32, (16, stream.shape[1]), 0)
    extra = jnp.where(row == 0, hi, jnp.where(row == 1, mid, jnp.where(row == 2, lo, 0.0)))
    scaled = (stream * gain_ref[...]).astype(jnp.bfloat16)
    extra = extra.astype(jnp.bfloat16)
    count = stream.shape[0]
    for i in range(NZ):
        out_ref[i, :count] = scaled
        out_ref[i, count:] = extra


def logits_kernel(place_ref, *refs):
    mine, theirs, w_hbm = refs[:4], refs[4:8], refs[8]
    own_ref, halves, a_ref, w_ref, sems = refs[9], refs[10:16], refs[16], refs[17], refs[18]
    blocks, _, span = w_ref.shape
    copies = [
        pltpu.make_async_copy(w_hbm.at[:, pl.ds(n * span, span)], w_ref.at[n], sems.at[n])
        for n in range(blocks)
    ]
    for copy in copies:
        copy.start()
    c, turn = place_ref[0], place_ref[2]
    for k in range(NY):
        a_ref[c, k] = mine[k][...]
        a_ref[1 - c, k] = theirs[k][...]
    chunk = mine[0].shape[0] // NZ
    count = chunk - 16

    def put(s, columns, value):
        if s == 0:
            own_ref[:, columns] = value
        else:
            halves[2 * s - 2][:, columns] = value[:64]
            halves[2 * s - 1][:, columns] = value[64:]

    lefts = []
    for s in range(NX):
        k = lax.rem(turn + NY - s, NY)
        left = jnp.concatenate(
            [
                a_ref[d, k, z * chunk : z * chunk + count]
                for z in range(NZ)
                for d in range(NC)
            ],
            axis=0,
        )
        extra = jnp.zeros((16, 128), jnp.float32)
        for z in range(NZ):
            for d in range(NC):
                extra += a_ref[d, k, z * chunk + count : (z + 1) * chunk].astype(jnp.float32)
        second = extra[0:1] + extra[1:2] + extra[2:3]
        hi, mid, lo = split3(second)
        row = lax.broadcasted_iota(jnp.int32, (128, 128), 0)
        table = jnp.where(row == 0, hi, jnp.where(row == 1, mid, jnp.where(row == 2, lo, 0.0)))
        put(s, slice(blocks * span, blocks * span + 128), jnp.transpose(table).astype(jnp.bfloat16))
        lefts.append(jnp.transpose(left))
    lefts = jnp.concatenate(lefts, axis=0)
    for n in range(blocks):
        copies[n].wait()
        part = jnp.dot(lefts, w_ref[n], preferred_element_type=jnp.float32).astype(jnp.bfloat16)
        for s in range(NX):
            put(s, slice(n * span, (n + 1) * span), part[s * 128 : (s + 1) * 128])


def add_kernel(a_ref, b_ref, c_ref, d_ref, ab_ref, cd_ref):
    for one, two, out_ref in ((a_ref, b_ref, ab_ref), (c_ref, d_ref, cd_ref)):
        width = one.shape[1] - 128
        value = one[:, :width].astype(jnp.float32) + two[:, :width].astype(jnp.float32)
        out_ref[:, :width] = value.astype(jnp.bfloat16)
        extra = one[:, width:].astype(jnp.float32) + two[:, width:].astype(jnp.float32)
        second = extra[:, 0:1] + extra[:, 1:2] + extra[:, 2:3]
        hi, mid, lo = split3(second)
        lane = lax.broadcasted_iota(jnp.int32, extra.shape, 1)
        extra = jnp.where(lane == 0, hi, jnp.where(lane == 1, mid, jnp.where(lane == 2, lo, 0.0)))
        out_ref[:, width:] = extra.astype(jnp.bfloat16)


def stats_kernel(own_ref, a_ref, b_ref, c_ref, d_ref, allowed_ref, column_ref, out_ref, l_ref):
    rows = own_ref.shape[0]
    width = allowed_ref.shape[1] * 128

    def summed(lo):
        part = [r[:, lo : lo + 128].astype(jnp.float32) for r in (a_ref, b_ref, c_ref, d_ref)]
        others = jnp.concatenate([part[0] + part[1], part[2] + part[3]], axis=0)
        return own_ref[:, lo : lo + 128].astype(jnp.float32) + others

    extra = summed(width)
    second = (extra[:, 0:1] + extra[:, 1:2] + extra[:, 2:3]) / 5120.0
    scale = lax.rsqrt(second + epsilon)
    lane = lax.broadcasted_iota(jnp.int32, (rows, 128), 1)
    column = column_ref[...]
    high = jnp.full((rows, 128), lowest, jnp.float32)
    pick = jnp.zeros((rows, 128), jnp.float32)
    for j in range(width // 128):
        logit = summed(j * 128) * scale
        pick += jnp.where(lane + j * 128 == column, logit, 0.0)
        logit = jnp.where(allowed_ref[:, j : j + 1] > 0, logit, lowest)
        l_ref[:, j * 128 : (j + 1) * 128] = logit
        high = jnp.maximum(high, logit)
    top = jnp.max(high, axis=1, keepdims=True)
    total = jnp.zeros((rows, 128), jnp.float32)
    for j in range(width // 128):
        logit = l_ref[:, j * 128 : (j + 1) * 128]
        total += jnp.where(allowed_ref[:, j : j + 1] > 0, jnp.exp(logit - top), 0.0)
    total = jnp.sum(total, axis=1, keepdims=True)
    pick = jnp.sum(pick, axis=1, keepdims=True)
    level = jnp.where(total > 0.0, top + jnp.log(jnp.where(total > 0.0, total, 1.0)), lowest)
    table = jnp.where(lane == 0, level, jnp.where(lane == 1, pick, 0.0))
    out_ref[...] = jnp.transpose(table)[:8]


def per_device(
    queries,
    prefix_kv,
    tail_kv,
    row_prompt,
    prefix_len,
    tail_len,
    out_weight,
    residual,
    norm_gain,
    vocab_weight,
    allowed,
    next_token,
):
    rows_dev, heads, head_dim = queries.shape
    kv_heads = tail_kv.shape[3]
    tail_width = tail_kv.shape[2]
    group = heads // kv_heads
    width = heads * head_dim
    owner = lax.axis_index("ctx")
    x = lax.axis_index("tp")
    y, z, c = owner // (NZ * NC), (owner // NC) % NZ, owner % NC
    inv_root = 1.0 / math.sqrt(head_dim)
    span = prefix_kv.shape[2]

    q_z = lax.all_to_all(
        call(
            copies_kernel,
            jax.ShapeDtypeStruct((NZ, rows_dev, width), jnp.bfloat16),
            (queries,),
            flops=1000,
        ),
        "ctx",
        split_axis=0,
        concat_axis=0,
        tiled=True,
        axis_index_groups=z_groups,
    ).reshape(NZ * rows_dev, width)
    kv_own = prefix_kv.reshape(2, 2, span, kv_heads * head_dim)
    kv_other = lax.ppermute(kv_own, "ctx", core_swap)

    local_rows = residual.shape[0]

    def core_major(array):
        rest = array.shape[1:]
        array = array.reshape((NZ, NC, rows_dev) + rest)
        return jnp.swapaxes(array, 0, 1).reshape((local_rows,) + rest)

    residual_t = lax.ppermute(core_major(residual).T, ("ctx", "tp"), turned(0))
    columns_dev = residual.shape[1]
    gain = lax.dynamic_slice_in_dim(
        norm_gain, (x * NZ * NC + z * NC + c) * columns_dev, columns_dev, 0
    ).astype(jnp.float32)
    gain = jnp.broadcast_to(gain[:, None], (columns_dev, local_rows))
    place = jnp.stack([c, y, (y + NY - x) % NY, x]).astype(jnp.int32)

    own_queries = queries.reshape(rows_dev, kv_heads, group, head_dim)
    tail_scores = (
        jnp.einsum(
            "rhgd,rkhd->rhgk", own_queries, tail_kv[:, 0], preferred_element_type=jnp.float32
        )
        * inv_root
    )
    base = jnp.stack([owner * span, (owner + 1 - 2 * c) * span])
    limit = jnp.clip(prefix_len[:, None] - base[None, :], 0, span)
    reach = jnp.where(
        row_prompt[:, None, None] == jnp.arange(2, dtype=jnp.int32)[None, :, None],
        limit[:, None, :],
        0,
    ).reshape(NY, NZ, NC, rows_dev, 4)
    reach = lax.dynamic_index_in_dim(reach, c, 2, keepdims=False).reshape(NY, NZ * rows_dev, 4)

    reaches = [
        lax.dynamic_index_in_dim(reach, (y + NY - k) % NY, 0, keepdims=False) for k in range(NY)
    ]
    q_z, kv_other, reaches, tail_scores = lax.optimization_barrier(
        (q_z, kv_other, reaches, tail_scores)
    )
    tail_keep = (jnp.arange(tail_width, dtype=jnp.int32)[None, :] < tail_len[:, None])[
        :, None, None, :
    ]
    tail_high = jnp.max(jnp.where(tail_keep, tail_scores, lowest), axis=-1)
    tail_weights = jnp.where(tail_keep, jnp.exp(tail_scores - tail_high[..., None]), 0.0).astype(
        jnp.bfloat16
    )
    tail_total = jnp.sum(tail_weights.astype(jnp.float32), axis=-1)
    tail_sum = jnp.einsum(
        "rhgk,rkhd->rhgd", tail_weights, tail_kv[:, 1], preferred_element_type=jnp.float32
    )
    tail_out = (tail_sum / tail_total[..., None]).reshape(rows_dev, width)
    tail_level = (tail_high * LOG2E + jnp.log2(tail_total)).reshape(rows_dev, heads)
    tail_level = jnp.pad(tail_level, ((0, 0), (0, 128 - heads)))

    group_rows = NZ * rows_dev

    def attend(q, k):
        return call(
            attend_kernel,
            jax.ShapeDtypeStruct((group_rows, width + 128), jnp.bfloat16),
            (q, kv_own, kv_other, reaches[k]),
            flops=2 * 2 * group_rows * 2048 * 2048,
            scratch=[VMEM((4 * group_rows, 4 * span), jnp.float32)],
        )

    visitors = {k: lax.ppermute(q_z, "ctx", y_shift(k)) for k in (2, 1, 3)}
    own_part = attend(q_z, 0)
    back = {}
    last = own_part
    for k in (2, 1, 3):
        visitor, last = lax.optimization_barrier((visitors[k], last))
        last = attend(visitor, k)
        back[k] = lax.ppermute(last, "ctx", y_shift(-k))
    joined = call(
        join4_kernel,
        jax.ShapeDtypeStruct((group_rows, width + 128), jnp.bfloat16),
        (own_part, back[2], back[1], back[3]),
        flops=1000000,
    )

    weight_own, joined = lax.optimization_barrier((out_weight.T, joined))
    weights = [weight_own] + [lax.ppermute(weight_own, "ctx", y_shift(-k)) for k in (2, 1, 3)]
    got = lax.all_to_all(
        joined.reshape(NZ, rows_dev, width + 128),
        "ctx",
        split_axis=0,
        concat_axis=0,
        tiled=True,
        axis_index_groups=z_groups,
    )
    attended, copies = call(
        join9_kernel,
        (
            jax.ShapeDtypeStruct((rows_dev, width), jnp.bfloat16),
            jax.ShapeDtypeStruct((NZ, rows_dev, width), jnp.bfloat16),
        ),
        (got, tail_out, tail_level),
        flops=1000000,
    )

    copies, weights = lax.optimization_barrier((copies, weights))
    rows_own = lax.all_to_all(
        copies, "ctx", split_axis=0, concat_axis=0, tiled=True, axis_index_groups=z_groups
    ).reshape(NZ * rows_dev, width)
    rows_other = lax.ppermute(rows_own, "ctx", core_swap)
    projected = call(
        project_kernel,
        jax.ShapeDtypeStruct((NY, columns_dev, local_rows), jnp.bfloat16),
        (rows_own, rows_other) + (weights[0], weights[2], weights[1], weights[3]),
        flops=2 * 128 * 320 * 2048,
        scratch=[VMEM((NC, NZ * rows_dev, width), jnp.bfloat16)],
        place=place,
    )
    pieces = lax.all_to_all(projected, "tp", split_axis=0, concat_axis=0, tiled=True)
    streams = call(
        stream_kernel,
        jax.ShapeDtypeStruct((NZ, columns_dev + 16, local_rows), jnp.bfloat16),
        (pieces, residual_t, gain),
        flops=1000000,
    )

    block = lax.all_to_all(
        streams, "ctx", split_axis=0, concat_axis=0, tiled=True, axis_index_groups=z_groups
    ).reshape(NZ * (columns_dev + 16), local_rows)
    mine = [block] + [lax.ppermute(block, "ctx", y_shift(k)) for k in (1, 2, 3)]
    theirs = [lax.ppermute(one, "ctx", core_swap) for one in mine]
    vocab_here = vocab_weight.shape[1]
    whole = jax.ShapeDtypeStruct((local_rows, vocab_here + 128), jnp.bfloat16)
    part = jax.ShapeDtypeStruct((local_rows // 2, vocab_here + 128), jnp.bfloat16)
    own, low1, high1, low2, high2, low3, high3 = call(
        logits_kernel,
        (whole,) + (part,) * 6,
        tuple(mine) + tuple(theirs) + (vocab_weight,),
        flops=2 * 512 * 1280 * 2048,
        scratch=[
            VMEM((NC, NY) + block.shape, jnp.bfloat16),
            VMEM((4, vocab_weight.shape[0], vocab_here // 4), jnp.bfloat16),
            pltpu.SemaphoreType.DMA((4,)),
        ],
        place=place,
        limit=50,
        far=(8,),
    )
    up, down = x_shift(1), x_shift(3)
    via_up = lax.ppermute(low2, "tp", up)
    via_down = lax.ppermute(high2, "tp", down)
    high_up = lax.ppermute(high1, "tp", up)
    low_down = lax.ppermute(low3, "tp", down)
    low_sum, high_sum = call(
        add_kernel, (part, part), (via_up, low1, via_down, high3), flops=1000000
    )
    low_up = lax.ppermute(low_sum, "tp", up)
    high_down = lax.ppermute(high_sum, "tp", down)
    sums = (own, low_up, low_down, high_up, high_down)
    stats = call(
        stats_kernel,
        jax.ShapeDtypeStruct((8, local_rows), jnp.float32),
        tuple(sums)
        + (core_major(allowed), core_major((next_token - owner * vocab_here)[:, None])),
        flops=1000000,
        scratch=[VMEM((local_rows, vocab_here), jnp.float32)],
    )[:2]
    every = lax.all_to_all(
        jnp.broadcast_to(stats[None], (NY * NZ * NC,) + stats.shape),
        "ctx",
        split_axis=0,
        concat_axis=0,
        tiled=True,
    )
    peak = jnp.max(every[:, 0], axis=0)
    total = jnp.sum(jnp.exp(every[:, 0] - peak[None]), axis=0)
    logprob = jnp.sum(every[:, 1], axis=0) - (peak + jnp.log(total))
    logprob = jnp.swapaxes(logprob.reshape(NC, NZ, rows_dev), 0, 1).reshape(local_rows)
    return (attended, logprob)


def solution(mesh):
    placed = (
        P("ctx", "tp", None),
        P(None, None, "ctx", "tp", None),
        P("ctx", None, None, "tp", None),
        P(),
        P(),
        P("ctx"),
        P("tp", "ctx"),
        P("tp", "ctx"),
        P(),
        P("tp", "ctx"),
        P("tp", "ctx"),
        P("tp"),
    )
    return jax.shard_map(
        per_device, mesh=mesh, in_specs=placed, out_specs=(P("ctx", "tp"), P("tp")), check_vma=False
    )
```

```python
import functools
import math

import jax
import jax.numpy as jnp
from jax import lax
from jax.experimental import pallas as pl
from jax.experimental.pallas import tpu as pltpu
from jax.sharding import PartitionSpec as P

lowest = -1e30
epsilon = 1e-06
LOG2E = 1.4426950408889634
NY, NZ, NC, NX = 4, 8, 2, 4
VMEM = pltpu.VMEM


def ctx_id(y, z, c):
    return (y % NY) * (NZ * NC) + (z % NZ) * NC + c % NC


def chips():
    return [(y, z, c) for y in range(NY) for z in range(NZ) for c in range(NC)]


core_swap = [(ctx_id(y, z, c), ctx_id(y, z, 1 - c)) for y, z, c in chips()]
z_groups = [[ctx_id(y, z, c) for z in range(NZ)] for y in range(NY) for c in range(NC)]


def y_shift(d):
    return [(ctx_id(y, z, c), ctx_id(y + d, z, c)) for y, z, c in chips()]


def x_shift(d):
    return [(t, (t + d) % NX) for t in range(NX)]


def turned(s):
    return [
        (ctx_id(y, z, c) * NX + t, ctx_id(t + s, z, c) * NX + y)
        for t in range(NX)
        for y, z, c in chips()
    ]


def split3(value):
    hi = value.astype(jnp.bfloat16).astype(jnp.float32)
    rest = value - hi
    mid = rest.astype(jnp.bfloat16).astype(jnp.float32)
    return hi, mid, rest - mid


def call(kernel, out_shape, args, flops, scratch=(), place=None, limit=24, far=()):
    size = sum(math.prod(a.shape) * a.dtype.itemsize for a in args)
    specs = [
        pl.BlockSpec(memory_space=pltpu.HBM if i in far else VMEM) for i in range(len(args))
    ]
    if place is not None:
        specs = [pl.BlockSpec(memory_space=pltpu.SMEM)] + specs
        args = (place,) + tuple(args)
    return pl.pallas_call(
        kernel,
        out_shape=out_shape,
        in_specs=specs,
        out_specs=jax.tree.map(lambda _: pl.BlockSpec(memory_space=VMEM), out_shape),
        scratch_shapes=list(scratch),
        compiler_params=pltpu.CompilerParams(vmem_limit_bytes=limit * 1024 * 1024),
        cost_estimate=pl.CostEstimate(flops=flops, bytes_accessed=size, transcendentals=0),
    )(*args)


def copies_kernel(q_ref, out_ref):
    for j in range(q_ref.shape[1]):
        part = q_ref[:, j, :]
        for i in range(out_ref.shape[0]):
            out_ref[i, :, j * 128 : (j + 1) * 128] = part


def attend_kernel(q_ref, own_ref, other_ref, reach_ref, out_ref, s_ref):
    rows = q_ref.shape[0]
    span = own_ref.shape[2]
    factor = LOG2E / math.sqrt(128)
    lane = lax.broadcasted_iota(jnp.int32, (rows, 128), 1)
    key = lax.broadcasted_iota(jnp.int32, (rows, span), 1)
    extra = jnp.zeros((rows, 128), jnp.float32)
    blocks = [(ref, p) for p in range(2) for ref in (own_ref, other_ref)]
    ones = jnp.ones((span, 128), jnp.bfloat16)
    for h in range(2):
        for half in range(2):
            heads = [h * 8 + half * 4 + g for g in range(4)]
            q = jnp.concatenate([q_ref[:, j * 128 : (j + 1) * 128] for j in heads], axis=0)
            high = jnp.full((4 * rows, 1), lowest, jnp.float32)
            for b, (ref, p) in enumerate(blocks):
                s = lax.dot_general(
                    q,
                    ref[p, 0, :, h * 128 : (h + 1) * 128],
                    (((1,), (1,)), ((), ())),
                    preferred_element_type=jnp.float32,
                )
                keep = key < reach_ref[:, b : b + 1]
                s = jnp.concatenate(
                    [jnp.where(keep, s[g * rows : (g + 1) * rows], lowest) for g in range(4)],
                    axis=0,
                )
                s_ref[:, b * span : (b + 1) * span] = s
                high = jnp.maximum(high, jnp.max(s, axis=1, keepdims=True))
            acc = jnp.zeros((4 * rows, 256), jnp.float32)
            for b, (ref, p) in enumerate(blocks):
                w = jnp.exp2((s_ref[:, b * span : (b + 1) * span] - high) * factor)
                v = jnp.concatenate([ref[p, 1, :, h * 128 : (h + 1) * 128], ones], axis=1)
                acc += jnp.dot(w.astype(jnp.bfloat16), v, preferred_element_type=jnp.float32)
            for g, j in enumerate(heads):
                part = slice(g * rows, (g + 1) * rows)
                total = acc[part, 128:]
                out_ref[:, j * 128 : (j + 1) * 128] = (acc[part, :128] / total).astype(jnp.bfloat16)
                level = high[part] * factor + jnp.log2(total)
                for i, piece in enumerate(split3(level)):
                    extra = jnp.where(lane == j + 16 * i, piece, extra)
    out_ref[:, 2048:] = extra.astype(jnp.bfloat16)


def level_of(extra):
    extra = extra.astype(jnp.float32)
    return extra + pltpu.roll(extra, 112, 1) + pltpu.roll(extra, 96, 1)


def join(parts, levels):
    high = levels[0]
    for level in levels[1:]:
        high = jnp.maximum(high, level)
    shares = [jnp.exp2(level - high) for level in levels]
    total = shares[0]
    for share in shares[1:]:
        total = total + share
    shares = [share / total for share in shares]
    heads = []
    for j in range(16):
        value = None
        for part, share in zip(parts, shares):
            term = part(j).astype(jnp.float32) * share[:, j : j + 1]
            value = term if value is None else value + term
        heads.append(value)
    return heads, high + jnp.log2(total)


def join4_kernel(a_ref, b_ref, c_ref, d_ref, out_ref):
    refs = (a_ref, b_ref, c_ref, d_ref)
    parts = [lambda j, r=r: r[:, j * 128 : (j + 1) * 128] for r in refs]
    heads, level = join(parts, [level_of(r[:, 2048:]) for r in refs])
    lane = lax.broadcasted_iota(jnp.int32, level.shape, 1)
    for j, value in enumerate(heads):
        out_ref[:, j * 128 : (j + 1) * 128] = value.astype(jnp.bfloat16)
    hi, mid, lo = split3(level)
    extra = jnp.where(
        lane < 16,
        hi,
        jnp.where(
            lane < 32,
            pltpu.roll(mid, 16, 1),
            jnp.where(lane < 48, pltpu.roll(lo, 32, 1), 0.0),
        ),
    )
    out_ref[:, 2048:] = extra.astype(jnp.bfloat16)


def join9_kernel(got_ref, tail_ref, tail_level_ref, out_ref, copies_ref):
    parts = [lambda j, i=i: got_ref[i, :, j * 128 : (j + 1) * 128] for i in range(NZ)]
    levels = [level_of(got_ref[i, :, 2048:]) for i in range(NZ)]
    parts.append(lambda j: tail_ref[:, j * 128 : (j + 1) * 128])
    levels.append(tail_level_ref[...])
    heads, _ = join(parts, levels)
    for j, value in enumerate(heads):
        value = value.astype(jnp.bfloat16)
        out_ref[:, j * 128 : (j + 1) * 128] = value
        for i in range(NZ):
            copies_ref[i, :, j * 128 : (j + 1) * 128] = value


def project_kernel(place_ref, own_ref, other_ref, w0_ref, w1_ref, w2_ref, w3_ref, out_ref, rows_ref):
    c, y = place_ref[0], place_ref[1]
    rows_ref[c] = own_ref[...]
    rows_ref[1 - c] = other_ref[...]
    rows = jnp.concatenate([rows_ref[0], rows_ref[1]], axis=0)
    for j, w_ref in enumerate((w0_ref, w1_ref, w2_ref, w3_ref)):
        part = lax.dot_general(
            w_ref[...], rows, (((1,), (1,)), ((), ())), preferred_element_type=jnp.float32
        )
        out_ref[lax.rem(y + j, NY)] = part.astype(jnp.bfloat16)


def stream_kernel(got_ref, residual_ref, gain_ref, out_ref):
    total = residual_ref[...].astype(jnp.float32)
    for t in range(NX):
        total = total + got_ref[t].astype(jnp.float32)
    stream = total.astype(jnp.bfloat16).astype(jnp.float32)
    second = jnp.sum(stream * stream, axis=0, keepdims=True)
    hi, mid, lo = split3(second)
    row = lax.broadcasted_iota(jnp.int32, (16, stream.shape[1]), 0)
    extra = jnp.where(row == 0, hi, jnp.where(row == 1, mid, jnp.where(row == 2, lo, 0.0)))
    scaled = (stream * gain_ref[...]).astype(jnp.bfloat16)
    extra = extra.astype(jnp.bfloat16)
    count = stream.shape[0]
    for i in range(NZ):
        out_ref[i, :count] = scaled
        out_ref[i, count:] = extra


def logits_kernel(slots, place_ref, *refs):
    mine, theirs, w_hbm = refs[:4], refs[4:8], refs[8]
    outs, (a_ref, w_ref, sems) = list(refs[9:-3]), refs[-3:]
    blocks, _, span = w_ref.shape
    copies = [
        pltpu.make_async_copy(w_hbm.at[:, pl.ds(n * span, span)], w_ref.at[n], sems.at[n])
        for n in range(blocks)
    ]
    ahead = 3
    for copy in copies[:ahead]:
        copy.start()
    c, turn = place_ref[0], place_ref[2]
    for k in range(NY):
        a_ref[c, k] = mine[k][...]
        a_ref[1 - c, k] = theirs[k][...]
    chunk = mine[0].shape[0] // NZ
    count = chunk - 16
    targets = []
    for s, whole in slots:
        targets.append(outs[:1] if whole else outs[:2])
        outs = outs[1:] if whole else outs[2:]

    def put(target, columns, value):
        rows = value.shape[0] // len(target)
        for i, ref in enumerate(target):
            ref[:, columns] = value[i * rows : (i + 1) * rows]

    lefts = []
    for (s, _), target in zip(slots, targets):
        k = lax.rem(turn + NY - s, NY)
        left = jnp.concatenate(
            [
                a_ref[d, k, z * chunk : z * chunk + count]
                for z in range(NZ)
                for d in range(NC)
            ],
            axis=0,
        )
        extra = jnp.zeros((16, 128), jnp.float32)
        for z in range(NZ):
            for d in range(NC):
                extra += a_ref[d, k, z * chunk + count : (z + 1) * chunk].astype(jnp.float32)
        second = extra[0:1] + extra[1:2] + extra[2:3]
        hi, mid, lo = split3(second)
        row = lax.broadcasted_iota(jnp.int32, (128, 128), 0)
        table = jnp.where(row == 0, hi, jnp.where(row == 1, mid, jnp.where(row == 2, lo, 0.0)))
        put(
            target,
            slice(blocks * span, blocks * span + 128),
            jnp.transpose(table).astype(jnp.bfloat16),
        )
        lefts.append(jnp.transpose(left))
    lefts = jnp.concatenate(lefts, axis=0)
    for n in range(blocks):
        copies[n].wait()
        if n + ahead < blocks:
            copies[n + ahead].start()
        part = jnp.dot(lefts, w_ref[n], preferred_element_type=jnp.float32).astype(jnp.bfloat16)
        for i, target in enumerate(targets):
            put(target, slice(n * span, (n + 1) * span), part[i * 128 : (i + 1) * 128])


def add_kernel(a_ref, b_ref, c_ref, d_ref, ab_ref, cd_ref):
    for one, two, out_ref in ((a_ref, b_ref, ab_ref), (c_ref, d_ref, cd_ref)):
        width = one.shape[1] - 128
        value = one[:, :width].astype(jnp.float32) + two[:, :width].astype(jnp.float32)
        out_ref[:, :width] = value.astype(jnp.bfloat16)
        extra = one[:, width:].astype(jnp.float32) + two[:, width:].astype(jnp.float32)
        second = extra[:, 0:1] + extra[:, 1:2] + extra[:, 2:3]
        hi, mid, lo = split3(second)
        lane = lax.broadcasted_iota(jnp.int32, extra.shape, 1)
        extra = jnp.where(lane == 0, hi, jnp.where(lane == 1, mid, jnp.where(lane == 2, lo, 0.0)))
        out_ref[:, width:] = extra.astype(jnp.bfloat16)


def stats_kernel(own_ref, a_ref, b_ref, c_ref, d_ref, allowed_ref, column_ref, out_ref, l_ref):
    rows = own_ref.shape[0]
    width = allowed_ref.shape[1] * 128

    def summed(lo):
        part = [r[:, lo : lo + 128].astype(jnp.float32) for r in (a_ref, b_ref, c_ref, d_ref)]
        others = jnp.concatenate([part[0] + part[1], part[2] + part[3]], axis=0)
        return own_ref[:, lo : lo + 128].astype(jnp.float32) + others

    extra = summed(width)
    second = (extra[:, 0:1] + extra[:, 1:2] + extra[:, 2:3]) / 5120.0
    scale = lax.rsqrt(second + epsilon)
    lane = lax.broadcasted_iota(jnp.int32, (rows, 128), 1)
    column = column_ref[...]
    high = jnp.full((rows, 128), lowest, jnp.float32)
    pick = jnp.zeros((rows, 128), jnp.float32)
    for j in range(width // 128):
        logit = summed(j * 128) * scale
        pick += jnp.where(lane + j * 128 == column, logit, 0.0)
        logit = jnp.where(allowed_ref[:, j : j + 1] > 0, logit, lowest)
        l_ref[:, j * 128 : (j + 1) * 128] = logit
        high = jnp.maximum(high, logit)
    top = jnp.max(high, axis=1, keepdims=True)
    total = jnp.zeros((rows, 128), jnp.float32)
    for j in range(width // 128):
        logit = l_ref[:, j * 128 : (j + 1) * 128]
        total += jnp.where(allowed_ref[:, j : j + 1] > 0, jnp.exp(logit - top), 0.0)
    total = jnp.sum(total, axis=1, keepdims=True)
    pick = jnp.sum(pick, axis=1, keepdims=True)
    level = jnp.where(total > 0.0, top + jnp.log(jnp.where(total > 0.0, total, 1.0)), lowest)
    table = jnp.where(lane == 0, level, jnp.where(lane == 1, pick, 0.0))
    out_ref[...] = jnp.transpose(table)[:8]


def per_device(
    queries,
    prefix_kv,
    tail_kv,
    row_prompt,
    prefix_len,
    tail_len,
    out_weight,
    residual,
    norm_gain,
    vocab_weight,
    allowed,
    next_token,
):
    rows_dev, heads, head_dim = queries.shape
    kv_heads = tail_kv.shape[3]
    tail_width = tail_kv.shape[2]
    group = heads // kv_heads
    width = heads * head_dim
    owner = lax.axis_index("ctx")
    x = lax.axis_index("tp")
    y, z, c = owner // (NZ * NC), (owner // NC) % NZ, owner % NC
    inv_root = 1.0 / math.sqrt(head_dim)
    span = prefix_kv.shape[2]

    q_copies = call(
        copies_kernel,
        jax.ShapeDtypeStruct((NZ, rows_dev, width), jnp.bfloat16),
        (queries,),
        flops=1000,
    )
    q_copies, prefix_kv = lax.optimization_barrier((q_copies, prefix_kv))
    q_z = lax.all_to_all(
        q_copies,
        "ctx",
        split_axis=0,
        concat_axis=0,
        tiled=True,
        axis_index_groups=z_groups,
    ).reshape(NZ * rows_dev, width)
    kv_own = prefix_kv.reshape(2, 2, span, kv_heads * head_dim)
    kv_other = lax.ppermute(kv_own, "ctx", core_swap)

    local_rows = residual.shape[0]

    def core_major(array):
        rest = array.shape[1:]
        array = array.reshape((NZ, NC, rows_dev) + rest)
        return jnp.swapaxes(array, 0, 1).reshape((local_rows,) + rest)

    residual_c = core_major(residual).T
    columns_dev = residual.shape[1]
    gain = lax.dynamic_slice_in_dim(
        norm_gain, (x * NZ * NC + z * NC + c) * columns_dev, columns_dev, 0
    ).astype(jnp.float32)
    gain = jnp.broadcast_to(gain[:, None], (columns_dev, local_rows))
    place = jnp.stack([c, y, (y + NY - x) % NY, x]).astype(jnp.int32)

    own_queries = queries.reshape(rows_dev, kv_heads, group, head_dim)
    tail_scores = (
        jnp.einsum(
            "rhgd,rkhd->rhgk", own_queries, tail_kv[:, 0], preferred_element_type=jnp.float32
        )
        * inv_root
    )
    base = jnp.stack([owner * span, (owner + 1 - 2 * c) * span])
    limit = jnp.clip(prefix_len[:, None] - base[None, :], 0, span)
    reach = jnp.where(
        row_prompt[:, None, None] == jnp.arange(2, dtype=jnp.int32)[None, :, None],
        limit[:, None, :],
        0,
    ).reshape(NY, NZ, NC, rows_dev, 4)
    reach = lax.dynamic_index_in_dim(reach, c, 2, keepdims=False).reshape(NY, NZ * rows_dev, 4)

    reaches = [
        lax.dynamic_index_in_dim(reach, (y + NY - k) % NY, 0, keepdims=False) for k in range(NY)
    ]
    q_z, kv_other, reaches, tail_scores, residual_c = lax.optimization_barrier(
        (q_z, kv_other, reaches, tail_scores, residual_c)
    )
    residual_t = lax.ppermute(residual_c, ("ctx", "tp"), turned(0))
    tail_keep = (jnp.arange(tail_width, dtype=jnp.int32)[None, :] < tail_len[:, None])[
        :, None, None, :
    ]
    tail_high = jnp.max(jnp.where(tail_keep, tail_scores, lowest), axis=-1)
    tail_weights = jnp.where(tail_keep, jnp.exp(tail_scores - tail_high[..., None]), 0.0).astype(
        jnp.bfloat16
    )
    tail_total = jnp.sum(tail_weights.astype(jnp.float32), axis=-1)
    tail_sum = jnp.einsum(
        "rhgk,rkhd->rhgd", tail_weights, tail_kv[:, 1], preferred_element_type=jnp.float32
    )
    tail_out = (tail_sum / tail_total[..., None]).reshape(rows_dev, width)
    tail_level = (tail_high * LOG2E + jnp.log2(tail_total)).reshape(rows_dev, heads)
    tail_level = jnp.pad(tail_level, ((0, 0), (0, 128 - heads)))

    group_rows = NZ * rows_dev

    def attend(q, k):
        return call(
            attend_kernel,
            jax.ShapeDtypeStruct((group_rows, width + 128), jnp.bfloat16),
            (q, kv_own, kv_other, reaches[k]),
            flops=2 * 2 * group_rows * 2048 * 2048,
            scratch=[VMEM((4 * group_rows, 4 * span), jnp.float32)],
        )

    visitors = {k: lax.ppermute(q_z, "ctx", y_shift(k)) for k in (2, 1, 3)}
    own_part = attend(q_z, 0)
    back = {}
    last = own_part
    for k in (2, 1, 3):
        visitor, last = lax.optimization_barrier((visitors[k], last))
        last = attend(visitor, k)
        back[k] = lax.ppermute(last, "ctx", y_shift(-k))
    residual_t, back[3] = lax.optimization_barrier((residual_t, back[3]))
    joined = call(
        join4_kernel,
        jax.ShapeDtypeStruct((group_rows, width + 128), jnp.bfloat16),
        (own_part, back[2], back[1], back[3]),
        flops=1000000,
    )

    weight_own, joined = lax.optimization_barrier((out_weight.T, joined))
    weights = [weight_own] + [lax.ppermute(weight_own, "ctx", y_shift(-k)) for k in (1, 2, 3)]
    got = lax.all_to_all(
        joined.reshape(NZ, rows_dev, width + 128),
        "ctx",
        split_axis=0,
        concat_axis=0,
        tiled=True,
        axis_index_groups=z_groups,
    )
    attended, copies = call(
        join9_kernel,
        (
            jax.ShapeDtypeStruct((rows_dev, width), jnp.bfloat16),
            jax.ShapeDtypeStruct((NZ, rows_dev, width), jnp.bfloat16),
        ),
        (got, tail_out, tail_level),
        flops=1000000,
    )

    copies, weights[1], weights[3] = lax.optimization_barrier((copies, weights[1], weights[3]))
    rows_own = lax.all_to_all(
        copies, "ctx", split_axis=0, concat_axis=0, tiled=True, axis_index_groups=z_groups
    ).reshape(NZ * rows_dev, width)
    rows_other = lax.ppermute(rows_own, "ctx", core_swap)
    projected = call(
        project_kernel,
        jax.ShapeDtypeStruct((NY, columns_dev, local_rows), jnp.bfloat16),
        (rows_own, rows_other) + tuple(weights),
        flops=2 * 128 * 320 * 2048,
        scratch=[VMEM((NC, NZ * rows_dev, width), jnp.bfloat16)],
        place=place,
    )
    pieces = lax.all_to_all(projected, "tp", split_axis=0, concat_axis=0, tiled=True)
    streams = call(
        stream_kernel,
        jax.ShapeDtypeStruct((NZ, columns_dev + 16, local_rows), jnp.bfloat16),
        (pieces, residual_t, gain),
        flops=1000000,
    )

    block = lax.all_to_all(
        streams, "ctx", split_axis=0, concat_axis=0, tiled=True, axis_index_groups=z_groups
    ).reshape(NZ * (columns_dev + 16), local_rows)
    mine = [block] + [lax.ppermute(block, "ctx", y_shift(k)) for k in (1, 2, 3)]
    theirs = [lax.ppermute(one, "ctx", core_swap) for one in mine]
    vocab_here = vocab_weight.shape[1]
    whole = jax.ShapeDtypeStruct((local_rows, vocab_here + 128), jnp.bfloat16)
    part = jax.ShapeDtypeStruct((local_rows // 2, vocab_here + 128), jnp.bfloat16)
    def logits_of(slots, shapes, mine):
        return call(
            functools.partial(logits_kernel, slots),
            shapes,
            tuple(mine) + tuple(theirs) + (vocab_weight,),
            flops=2 * 128 * len(slots) * 1280 * 2048,
            scratch=[
                VMEM((NC, NY) + block.shape, jnp.bfloat16),
                VMEM((8, vocab_weight.shape[0], vocab_here // 8), jnp.bfloat16),
                pltpu.SemaphoreType.DMA((8,)),
            ],
            place=place,
            limit=50,
            far=(8,),
        )

    low2, high2 = logits_of(((2, False),), (part,) * 2, mine)
    block, _, _ = lax.optimization_barrier((block, low2, high2))
    low1, high1, low3, high3, own = logits_of(
        ((1, False), (3, False), (0, True)), (part,) * 4 + (whole,), [block] + mine[1:]
    )
    up, down = x_shift(1), x_shift(3)
    via_up = lax.ppermute(low2, "tp", up)
    via_down = lax.ppermute(high2, "tp", down)
    high_up = lax.ppermute(high1, "tp", up)
    low_down = lax.ppermute(low3, "tp", down)
    low_sum, high_sum = call(
        add_kernel, (part, part), (via_up, low1, via_down, high3), flops=1000000
    )
    low_up = lax.ppermute(low_sum, "tp", up)
    high_down = lax.ppermute(high_sum, "tp", down)
    sums = (own, low_up, low_down, high_up, high_down)
    stats = call(
        stats_kernel,
        jax.ShapeDtypeStruct((8, local_rows), jnp.float32),
        tuple(sums)
        + (core_major(allowed), core_major((next_token - owner * vocab_here)[:, None])),
        flops=1000000,
        scratch=[VMEM((local_rows, vocab_here), jnp.float32)],
    )[:2]
    every = lax.all_to_all(
        jnp.broadcast_to(stats[None], (NY * NZ * NC,) + stats.shape),
        "ctx",
        split_axis=0,
        concat_axis=0,
        tiled=True,
    )
    peak = jnp.max(every[:, 0], axis=0)
    total = jnp.sum(jnp.exp(every[:, 0] - peak[None]), axis=0)
    logprob = jnp.sum(every[:, 1], axis=0) - (peak + jnp.log(total))
    logprob = jnp.swapaxes(logprob.reshape(NC, NZ, rows_dev), 0, 1).reshape(local_rows)
    return (attended, logprob)


def solution(mesh):
    placed = (
        P("ctx", "tp", None),
        P(None, None, "ctx", "tp", None),
        P("ctx", None, None, "tp", None),
        P(),
        P(),
        P("ctx"),
        P("tp", "ctx"),
        P("tp", "ctx"),
        P(),
        P("tp", "ctx"),
        P("tp", "ctx"),
        P("tp"),
    )
    return jax.shard_map(
        per_device, mesh=mesh, in_specs=placed, out_specs=(P("ctx", "tp"), P("tp")), check_vma=False
    )
```

```python
import functools
import math

import jax
import jax.numpy as jnp
from jax import lax
from jax.experimental import pallas as pl
from jax.experimental.pallas import tpu as pltpu
from jax.sharding import PartitionSpec as P

lowest = -1e30
epsilon = 1e-06
LOG2E = 1.4426950408889634
NY, NZ, NC, NX = 4, 8, 2, 4
VMEM = pltpu.VMEM


def ctx_id(y, z, c):
    return (y % NY) * (NZ * NC) + (z % NZ) * NC + c % NC


def chips():
    return [(y, z, c) for y in range(NY) for z in range(NZ) for c in range(NC)]


core_swap = [(ctx_id(y, z, c), ctx_id(y, z, 1 - c)) for y, z, c in chips()]
z_groups = [[ctx_id(y, z, c) for z in range(NZ)] for y in range(NY) for c in range(NC)]


def y_shift(d):
    return [(ctx_id(y, z, c), ctx_id(y + d, z, c)) for y, z, c in chips()]


def x_shift(d):
    return [(t, (t + d) % NX) for t in range(NX)]


def turned(s):
    return [
        (ctx_id(y, z, c) * NX + t, ctx_id(t + s, z, c) * NX + y)
        for t in range(NX)
        for y, z, c in chips()
    ]


def split3(value):
    hi = value.astype(jnp.bfloat16).astype(jnp.float32)
    rest = value - hi
    mid = rest.astype(jnp.bfloat16).astype(jnp.float32)
    return hi, mid, rest - mid


def call(kernel, out_shape, args, flops, scratch=(), place=None, limit=24, far=()):
    size = sum(math.prod(a.shape) * a.dtype.itemsize for a in args)
    specs = [
        pl.BlockSpec(memory_space=pltpu.HBM if i in far else VMEM) for i in range(len(args))
    ]
    if place is not None:
        specs = [pl.BlockSpec(memory_space=pltpu.SMEM)] + specs
        args = (place,) + tuple(args)
    return pl.pallas_call(
        kernel,
        out_shape=out_shape,
        in_specs=specs,
        out_specs=jax.tree.map(lambda _: pl.BlockSpec(memory_space=VMEM), out_shape),
        scratch_shapes=list(scratch),
        compiler_params=pltpu.CompilerParams(vmem_limit_bytes=limit * 1024 * 1024),
        cost_estimate=pl.CostEstimate(flops=flops, bytes_accessed=size, transcendentals=0),
    )(*args)


def copies_kernel(q_ref, out_ref):
    for j in range(q_ref.shape[1]):
        part = q_ref[:, j, :]
        for i in range(out_ref.shape[0]):
            out_ref[i, :, j * 128 : (j + 1) * 128] = part


def attend_kernel(q_ref, own_ref, other_ref, reach_ref, out_ref, s_ref):
    rows = q_ref.shape[0]
    span = own_ref.shape[2]
    factor = LOG2E / math.sqrt(128)
    lane = lax.broadcasted_iota(jnp.int32, (rows, 128), 1)
    key = lax.broadcasted_iota(jnp.int32, (rows, span), 1)
    extra = jnp.zeros((rows, 128), jnp.float32)
    blocks = [(ref, p) for p in range(2) for ref in (own_ref, other_ref)]
    ones = jnp.ones((span, 128), jnp.bfloat16)
    for h in range(2):
        for half in range(2):
            heads = [h * 8 + half * 4 + g for g in range(4)]
            q = jnp.concatenate([q_ref[:, j * 128 : (j + 1) * 128] for j in heads], axis=0)
            high = jnp.full((4 * rows, 1), lowest, jnp.float32)
            for b, (ref, p) in enumerate(blocks):
                s = lax.dot_general(
                    q,
                    ref[p, 0, :, h * 128 : (h + 1) * 128],
                    (((1,), (1,)), ((), ())),
                    preferred_element_type=jnp.float32,
                )
                keep = key < reach_ref[:, b : b + 1]
                s = jnp.concatenate(
                    [jnp.where(keep, s[g * rows : (g + 1) * rows], lowest) for g in range(4)],
                    axis=0,
                )
                s_ref[:, b * span : (b + 1) * span] = s
                high = jnp.maximum(high, jnp.max(s, axis=1, keepdims=True))
            acc = jnp.zeros((4 * rows, 256), jnp.float32)
            for b, (ref, p) in enumerate(blocks):
                w = jnp.exp2((s_ref[:, b * span : (b + 1) * span] - high) * factor)
                v = jnp.concatenate([ref[p, 1, :, h * 128 : (h + 1) * 128], ones], axis=1)
                acc += jnp.dot(w.astype(jnp.bfloat16), v, preferred_element_type=jnp.float32)
            for g, j in enumerate(heads):
                part = slice(g * rows, (g + 1) * rows)
                total = acc[part, 128:]
                out_ref[:, j * 128 : (j + 1) * 128] = (acc[part, :128] / total).astype(jnp.bfloat16)
                level = high[part] * factor + jnp.log2(total)
                for i, piece in enumerate(split3(level)):
                    extra = jnp.where(lane == j + 16 * i, piece, extra)
    out_ref[:, 2048:] = extra.astype(jnp.bfloat16)


def level_of(extra):
    extra = extra.astype(jnp.float32)
    return extra + pltpu.roll(extra, 112, 1) + pltpu.roll(extra, 96, 1)


def join(parts, levels):
    high = levels[0]
    for level in levels[1:]:
        high = jnp.maximum(high, level)
    shares = [jnp.exp2(level - high) for level in levels]
    total = shares[0]
    for share in shares[1:]:
        total = total + share
    shares = [share / total for share in shares]
    heads = []
    for j in range(16):
        value = None
        for part, share in zip(parts, shares):
            term = part(j).astype(jnp.float32) * share[:, j : j + 1]
            value = term if value is None else value + term
        heads.append(value)
    return heads, high + jnp.log2(total)


def join4_kernel(a_ref, b_ref, c_ref, d_ref, out_ref):
    refs = (a_ref, b_ref, c_ref, d_ref)
    parts = [lambda j, r=r: r[:, j * 128 : (j + 1) * 128] for r in refs]
    heads, level = join(parts, [level_of(r[:, 2048:]) for r in refs])
    lane = lax.broadcasted_iota(jnp.int32, level.shape, 1)
    for j, value in enumerate(heads):
        out_ref[:, j * 128 : (j + 1) * 128] = value.astype(jnp.bfloat16)
    hi, mid, lo = split3(level)
    extra = jnp.where(
        lane < 16,
        hi,
        jnp.where(
            lane < 32,
            pltpu.roll(mid, 16, 1),
            jnp.where(lane < 48, pltpu.roll(lo, 32, 1), 0.0),
        ),
    )
    out_ref[:, 2048:] = extra.astype(jnp.bfloat16)


def join9_kernel(got_ref, tail_ref, tail_level_ref, out_ref, copies_ref):
    parts = [lambda j, i=i: got_ref[i, :, j * 128 : (j + 1) * 128] for i in range(NZ)]
    levels = [level_of(got_ref[i, :, 2048:]) for i in range(NZ)]
    parts.append(lambda j: tail_ref[:, j * 128 : (j + 1) * 128])
    levels.append(tail_level_ref[...])
    heads, _ = join(parts, levels)
    for j, value in enumerate(heads):
        value = value.astype(jnp.bfloat16)
        out_ref[:, j * 128 : (j + 1) * 128] = value
        for i in range(NZ):
            copies_ref[i, :, j * 128 : (j + 1) * 128] = value


def project_kernel(place_ref, own_ref, other_ref, w0_ref, w1_ref, w2_ref, w3_ref, out_ref, rows_ref):
    c, y = place_ref[0], place_ref[1]
    rows_ref[c] = own_ref[...]
    rows_ref[1 - c] = other_ref[...]
    rows = jnp.concatenate([rows_ref[0], rows_ref[1]], axis=0)
    for j, w_ref in enumerate((w0_ref, w1_ref, w2_ref, w3_ref)):
        part = lax.dot_general(
            w_ref[...], rows, (((1,), (1,)), ((), ())), preferred_element_type=jnp.float32
        )
        out_ref[lax.rem(y + j, NY)] = part.astype(jnp.bfloat16)


def stream_kernel(got_ref, residual_ref, gain_ref, out_ref):
    total = residual_ref[...].astype(jnp.float32)
    for t in range(NX):
        total = total + got_ref[t].astype(jnp.float32)
    stream = total.astype(jnp.bfloat16).astype(jnp.float32)
    second = jnp.sum(stream * stream, axis=0, keepdims=True)
    hi, mid, lo = split3(second)
    row = lax.broadcasted_iota(jnp.int32, (16, stream.shape[1]), 0)
    extra = jnp.where(row == 0, hi, jnp.where(row == 1, mid, jnp.where(row == 2, lo, 0.0)))
    scaled = (stream * gain_ref[...]).astype(jnp.bfloat16)
    extra = extra.astype(jnp.bfloat16)
    count = stream.shape[0]
    for i in range(NZ):
        out_ref[i, :count] = scaled
        out_ref[i, count:] = extra


def fetch_kernel(w_hbm, out_ref, sem):
    copy = pltpu.make_async_copy(w_hbm, out_ref, sem)
    copy.start()
    copy.wait()


def logits_kernel(place_ref, *refs):
    mine, theirs, w_ref = refs[:4], refs[4:8], refs[8]
    own_ref, halves, a_ref = refs[9], refs[10:16], refs[16]
    span = 512
    blocks = w_ref.shape[1] // span
    c, turn = place_ref[0], place_ref[2]
    for k in range(NY):
        a_ref[c, k] = mine[k][...]
        a_ref[1 - c, k] = theirs[k][...]
    chunk = mine[0].shape[0] // NZ
    count = chunk - 16

    def put(s, columns, value):
        if s == 0:
            own_ref[:, columns] = value
        else:
            halves[2 * s - 2][:, columns] = value[:64]
            halves[2 * s - 1][:, columns] = value[64:]

    lefts = []
    for s in range(NX):
        k = lax.rem(turn + NY - s, NY)
        left = jnp.concatenate(
            [
                a_ref[d, k, z * chunk : z * chunk + count]
                for z in range(NZ)
                for d in range(NC)
            ],
            axis=0,
        )
        extra = jnp.zeros((16, 128), jnp.float32)
        for z in range(NZ):
            for d in range(NC):
                extra += a_ref[d, k, z * chunk + count : (z + 1) * chunk].astype(jnp.float32)
        second = extra[0:1] + extra[1:2] + extra[2:3]
        hi, mid, lo = split3(second)
        row = lax.broadcasted_iota(jnp.int32, (128, 128), 0)
        table = jnp.where(row == 0, hi, jnp.where(row == 1, mid, jnp.where(row == 2, lo, 0.0)))
        put(s, slice(blocks * span, blocks * span + 128), jnp.transpose(table).astype(jnp.bfloat16))
        lefts.append(jnp.transpose(left))
    lefts = jnp.concatenate(lefts, axis=0)
    for n in range(blocks):
        part = jnp.dot(
            lefts, w_ref[:, n * span : (n + 1) * span], preferred_element_type=jnp.float32
        ).astype(jnp.bfloat16)
        for s in range(NX):
            put(s, slice(n * span, (n + 1) * span), part[s * 128 : (s + 1) * 128])


def add_kernel(a_ref, b_ref, c_ref, d_ref, ab_ref, cd_ref):
    for one, two, out_ref in ((a_ref, b_ref, ab_ref), (c_ref, d_ref, cd_ref)):
        width = one.shape[1] - 128
        value = one[:, :width].astype(jnp.float32) + two[:, :width].astype(jnp.float32)
        out_ref[:, :width] = value.astype(jnp.bfloat16)
        extra = one[:, width:].astype(jnp.float32) + two[:, width:].astype(jnp.float32)
        second = extra[:, 0:1] + extra[:, 1:2] + extra[:, 2:3]
        hi, mid, lo = split3(second)
        lane = lax.broadcasted_iota(jnp.int32, extra.shape, 1)
        extra = jnp.where(lane == 0, hi, jnp.where(lane == 1, mid, jnp.where(lane == 2, lo, 0.0)))
        out_ref[:, width:] = extra.astype(jnp.bfloat16)


def stats_kernel(own_ref, a_ref, b_ref, c_ref, d_ref, allowed_ref, column_ref, out_ref, l_ref):
    rows = own_ref.shape[0]
    width = allowed_ref.shape[1] * 128

    def summed(lo):
        part = [r[:, lo : lo + 128].astype(jnp.float32) for r in (a_ref, b_ref, c_ref, d_ref)]
        others = jnp.concatenate([part[0] + part[1], part[2] + part[3]], axis=0)
        return own_ref[:, lo : lo + 128].astype(jnp.float32) + others

    extra = summed(width)
    second = (extra[:, 0:1] + extra[:, 1:2] + extra[:, 2:3]) / 5120.0
    scale = lax.rsqrt(second + epsilon)
    lane = lax.broadcasted_iota(jnp.int32, (rows, 128), 1)
    column = column_ref[...]
    high = jnp.full((rows, 128), lowest, jnp.float32)
    pick = jnp.zeros((rows, 128), jnp.float32)
    for j in range(width // 128):
        logit = summed(j * 128) * scale
        pick += jnp.where(lane + j * 128 == column, logit, 0.0)
        logit = jnp.where(allowed_ref[:, j : j + 1] > 0, logit, lowest)
        l_ref[:, j * 128 : (j + 1) * 128] = logit
        high = jnp.maximum(high, logit)
    top = jnp.max(high, axis=1, keepdims=True)
    total = jnp.zeros((rows, 128), jnp.float32)
    for j in range(width // 128):
        logit = l_ref[:, j * 128 : (j + 1) * 128]
        total += jnp.where(allowed_ref[:, j : j + 1] > 0, jnp.exp(logit - top), 0.0)
    total = jnp.sum(total, axis=1, keepdims=True)
    pick = jnp.sum(pick, axis=1, keepdims=True)
    level = jnp.where(total > 0.0, top + jnp.log(jnp.where(total > 0.0, total, 1.0)), lowest)
    table = jnp.where(lane == 0, level, jnp.where(lane == 1, pick, 0.0))
    out_ref[...] = jnp.transpose(table)[:8]


def per_device(
    queries,
    prefix_kv,
    tail_kv,
    row_prompt,
    prefix_len,
    tail_len,
    out_weight,
    residual,
    norm_gain,
    vocab_weight,
    allowed,
    next_token,
):
    rows_dev, heads, head_dim = queries.shape
    kv_heads = tail_kv.shape[3]
    tail_width = tail_kv.shape[2]
    group = heads // kv_heads
    width = heads * head_dim
    owner = lax.axis_index("ctx")
    x = lax.axis_index("tp")
    y, z, c = owner // (NZ * NC), (owner // NC) % NZ, owner % NC
    inv_root = 1.0 / math.sqrt(head_dim)
    span = prefix_kv.shape[2]

    q_copies = call(
        copies_kernel,
        jax.ShapeDtypeStruct((NZ, rows_dev, width), jnp.bfloat16),
        (queries,),
        flops=1000,
    )
    q_copies, prefix_kv = lax.optimization_barrier((q_copies, prefix_kv))
    q_z = lax.all_to_all(
        q_copies,
        "ctx",
        split_axis=0,
        concat_axis=0,
        tiled=True,
        axis_index_groups=z_groups,
    ).reshape(NZ * rows_dev, width)
    kv_own = prefix_kv.reshape(2, 2, span, kv_heads * head_dim)
    kv_other = lax.ppermute(kv_own, "ctx", core_swap)

    local_rows = residual.shape[0]

    def core_major(array):
        rest = array.shape[1:]
        array = array.reshape((NZ, NC, rows_dev) + rest)
        return jnp.swapaxes(array, 0, 1).reshape((local_rows,) + rest)

    residual_c = core_major(residual).T
    columns_dev = residual.shape[1]
    gain = lax.dynamic_slice_in_dim(
        norm_gain, (x * NZ * NC + z * NC + c) * columns_dev, columns_dev, 0
    ).astype(jnp.float32)
    gain = jnp.broadcast_to(gain[:, None], (columns_dev, local_rows))
    place = jnp.stack([c, y, (y + NY - x) % NY, x]).astype(jnp.int32)

    own_queries = queries.reshape(rows_dev, kv_heads, group, head_dim)
    tail_scores = (
        jnp.einsum(
            "rhgd,rkhd->rhgk", own_queries, tail_kv[:, 0], preferred_element_type=jnp.float32
        )
        * inv_root
    )
    base = jnp.stack([owner * span, (owner + 1 - 2 * c) * span])
    limit = jnp.clip(prefix_len[:, None] - base[None, :], 0, span)
    reach = jnp.where(
        row_prompt[:, None, None] == jnp.arange(2, dtype=jnp.int32)[None, :, None],
        limit[:, None, :],
        0,
    ).reshape(NY, NZ, NC, rows_dev, 4)
    reach = lax.dynamic_index_in_dim(reach, c, 2, keepdims=False).reshape(NY, NZ * rows_dev, 4)

    reaches = [
        lax.dynamic_index_in_dim(reach, (y + NY - k) % NY, 0, keepdims=False) for k in range(NY)
    ]
    q_z, kv_other, reaches, tail_scores = lax.optimization_barrier(
        (q_z, kv_other, reaches, tail_scores)
    )
    tail_keep = (jnp.arange(tail_width, dtype=jnp.int32)[None, :] < tail_len[:, None])[
        :, None, None, :
    ]
    tail_high = jnp.max(jnp.where(tail_keep, tail_scores, lowest), axis=-1)
    tail_weights = jnp.where(tail_keep, jnp.exp(tail_scores - tail_high[..., None]), 0.0).astype(
        jnp.bfloat16
    )
    tail_total = jnp.sum(tail_weights.astype(jnp.float32), axis=-1)
    tail_sum = jnp.einsum(
        "rhgk,rkhd->rhgd", tail_weights, tail_kv[:, 1], preferred_element_type=jnp.float32
    )
    tail_out = (tail_sum / tail_total[..., None]).reshape(rows_dev, width)
    tail_level = (tail_high * LOG2E + jnp.log2(tail_total)).reshape(rows_dev, heads)
    tail_level = jnp.pad(tail_level, ((0, 0), (0, 128 - heads)))

    group_rows = NZ * rows_dev

    def attend(q, k):
        return call(
            attend_kernel,
            jax.ShapeDtypeStruct((group_rows, width + 128), jnp.bfloat16),
            (q, kv_own, kv_other, reaches[k]),
            flops=2 * 2 * group_rows * 2048 * 2048,
            scratch=[VMEM((4 * group_rows, 4 * span), jnp.float32)],
        )

    visitors = {k: lax.ppermute(q_z, "ctx", y_shift(k)) for k in (1, 3)}
    own_part = attend(q_z, 0)
    q_later, last = lax.optimization_barrier((q_z, own_part))
    visitors[2] = lax.ppermute(q_later, "ctx", y_shift(2))
    back = {}
    for k in (1, 3, 2):
        visitor, last = lax.optimization_barrier((visitors[k], last))
        last = attend(visitor, k)
        back[k] = lax.ppermute(last, "ctx", y_shift(-k))
    joined = call(
        join4_kernel,
        jax.ShapeDtypeStruct((group_rows, width + 128), jnp.bfloat16),
        (own_part, back[2], back[1], back[3]),
        flops=1000000,
    )

    weight_own, joined = lax.optimization_barrier((out_weight.T, joined))
    weights = [weight_own] + [lax.ppermute(weight_own, "ctx", y_shift(-k)) for k in (1, 2, 3)]
    got = lax.all_to_all(
        joined.reshape(NZ, rows_dev, width + 128),
        "ctx",
        split_axis=0,
        concat_axis=0,
        tiled=True,
        axis_index_groups=z_groups,
    )
    attended, copies = call(
        join9_kernel,
        (
            jax.ShapeDtypeStruct((rows_dev, width), jnp.bfloat16),
            jax.ShapeDtypeStruct((NZ, rows_dev, width), jnp.bfloat16),
        ),
        (got, tail_out, tail_level),
        flops=1000000,
    )

    copies, weights[1], weights[3], residual_c = lax.optimization_barrier(
        (copies, weights[1], weights[3], residual_c)
    )
    residual_t = lax.ppermute(residual_c, ("ctx", "tp"), turned(0))
    rows_own = lax.all_to_all(
        copies, "ctx", split_axis=0, concat_axis=0, tiled=True, axis_index_groups=z_groups
    ).reshape(NZ * rows_dev, width)
    rows_own, residual_t = lax.optimization_barrier((rows_own, residual_t))
    rows_other = lax.ppermute(rows_own, "ctx", core_swap)
    projected = call(
        project_kernel,
        jax.ShapeDtypeStruct((NY, columns_dev, local_rows), jnp.bfloat16),
        (rows_own, rows_other) + tuple(weights),
        flops=2 * 128 * 320 * 2048,
        scratch=[VMEM((NC, NZ * rows_dev, width), jnp.bfloat16)],
        place=place,
    )
    pieces = lax.all_to_all(projected, "tp", split_axis=0, concat_axis=0, tiled=True)
    streams = call(
        stream_kernel,
        jax.ShapeDtypeStruct((NZ, columns_dev + 16, local_rows), jnp.bfloat16),
        (pieces, residual_t, gain),
        flops=1000000,
    )

    block = lax.all_to_all(
        streams, "ctx", split_axis=0, concat_axis=0, tiled=True, axis_index_groups=z_groups
    ).reshape(NZ * (columns_dev + 16), local_rows)
    mine = [block] + [lax.ppermute(block, "ctx", y_shift(k)) for k in (1, 2, 3)]
    _, vocab_later = lax.optimization_barrier((block, vocab_weight))
    vocab_local = call(
        fetch_kernel,
        jax.ShapeDtypeStruct(vocab_weight.shape, jnp.bfloat16),
        (vocab_later,),
        flops=1000,
        scratch=[pltpu.SemaphoreType.DMA],
        far=(0,),
    )
    mine[2], vocab_local = lax.optimization_barrier((mine[2], vocab_local))
    theirs = [lax.ppermute(one, "ctx", core_swap) for one in mine]
    vocab_here = vocab_weight.shape[1]
    whole = jax.ShapeDtypeStruct((local_rows, vocab_here + 128), jnp.bfloat16)
    part = jax.ShapeDtypeStruct((local_rows // 2, vocab_here + 128), jnp.bfloat16)
    own, low1, high1, low2, high2, low3, high3 = call(
        logits_kernel,
        (whole,) + (part,) * 6,
        tuple(mine) + tuple(theirs) + (vocab_local,),
        flops=2 * 512 * 1280 * 2048,
        scratch=[VMEM((NC, NY) + block.shape, jnp.bfloat16)],
        place=place,
        limit=24,
    )
    up, down = x_shift(1), x_shift(3)
    via_up = lax.ppermute(low2, "tp", up)
    via_down = lax.ppermute(high2, "tp", down)
    high_up = lax.ppermute(high1, "tp", up)
    low_down = lax.ppermute(low3, "tp", down)
    low_sum, high_sum = call(
        add_kernel, (part, part), (via_up, low1, via_down, high3), flops=1000000
    )
    low_up = lax.ppermute(low_sum, "tp", up)
    high_down = lax.ppermute(high_sum, "tp", down)
    sums = (own, low_up, low_down, high_up, high_down)
    stats = call(
        stats_kernel,
        jax.ShapeDtypeStruct((8, local_rows), jnp.float32),
        tuple(sums)
        + (core_major(allowed), core_major((next_token - owner * vocab_here)[:, None])),
        flops=1000000,
        scratch=[VMEM((local_rows, vocab_here), jnp.float32)],
    )[:2]
    every = lax.all_to_all(
        jnp.broadcast_to(stats[None], (NY * NZ * NC,) + stats.shape),
        "ctx",
        split_axis=0,
        concat_axis=0,
        tiled=True,
    )
    peak = jnp.max(every[:, 0], axis=0)
    total = jnp.sum(jnp.exp(every[:, 0] - peak[None]), axis=0)
    logprob = jnp.sum(every[:, 1], axis=0) - (peak + jnp.log(total))
    logprob = jnp.swapaxes(logprob.reshape(NC, NZ, rows_dev), 0, 1).reshape(local_rows)
    return (attended, logprob)


def solution(mesh):
    placed = (
        P("ctx", "tp", None),
        P(None, None, "ctx", "tp", None),
        P("ctx", None, None, "tp", None),
        P(),
        P(),
        P("ctx"),
        P("tp", "ctx"),
        P("tp", "ctx"),
        P(),
        P("tp", "ctx"),
        P("tp", "ctx"),
        P("tp"),
    )
    return jax.shard_map(
        per_device, mesh=mesh, in_specs=placed, out_specs=(P("ctx", "tp"), P("tp")), check_vma=False
    )
```

```python
import functools
import math

import jax
import jax.numpy as jnp
from jax import lax
from jax.experimental import pallas as pl
from jax.experimental.pallas import tpu as pltpu
from jax.sharding import PartitionSpec as P

lowest = -1e30
epsilon = 1e-06
LOG2E = 1.4426950408889634
NY, NZ, NC, NX = 4, 8, 2, 4
VMEM = pltpu.VMEM


def ctx_id(y, z, c):
    return (y % NY) * (NZ * NC) + (z % NZ) * NC + c % NC


def chips():
    return [(y, z, c) for y in range(NY) for z in range(NZ) for c in range(NC)]


core_swap = [(ctx_id(y, z, c), ctx_id(y, z, 1 - c)) for y, z, c in chips()]
z_groups = [[ctx_id(y, z, c) for z in range(NZ)] for y in range(NY) for c in range(NC)]


def y_shift(d):
    return [(ctx_id(y, z, c), ctx_id(y + d, z, c)) for y, z, c in chips()]


def x_shift(d):
    return [(t, (t + d) % NX) for t in range(NX)]


def turned(s):
    return [
        (ctx_id(y, z, c) * NX + t, ctx_id(t + s, z, c) * NX + y)
        for t in range(NX)
        for y, z, c in chips()
    ]


def split3(value):
    hi = value.astype(jnp.bfloat16).astype(jnp.float32)
    rest = value - hi
    mid = rest.astype(jnp.bfloat16).astype(jnp.float32)
    return hi, mid, rest - mid


def call(kernel, out_shape, args, flops, scratch=(), place=None, limit=24, far=()):
    size = sum(math.prod(a.shape) * a.dtype.itemsize for a in args)
    specs = [
        pl.BlockSpec(memory_space=pltpu.HBM if i in far else VMEM) for i in range(len(args))
    ]
    if place is not None:
        specs = [pl.BlockSpec(memory_space=pltpu.SMEM)] + specs
        args = (place,) + tuple(args)
    return pl.pallas_call(
        kernel,
        out_shape=out_shape,
        in_specs=specs,
        out_specs=jax.tree.map(lambda _: pl.BlockSpec(memory_space=VMEM), out_shape),
        scratch_shapes=list(scratch),
        compiler_params=pltpu.CompilerParams(vmem_limit_bytes=limit * 1024 * 1024),
        cost_estimate=pl.CostEstimate(flops=flops, bytes_accessed=size, transcendentals=0),
    )(*args)


def copies_kernel(q_ref, out_ref):
    for j in range(q_ref.shape[1]):
        part = q_ref[:, j, :]
        for i in range(out_ref.shape[0]):
            out_ref[i, :, j * 128 : (j + 1) * 128] = part


def attend_kernel(first, rows, q_ref, own_ref, other_ref, reach_ref, out_ref, s_ref):
    here = slice(first, first + rows)
    each = 256 // rows
    span = own_ref.shape[2]
    factor = LOG2E / math.sqrt(128)
    lane = lax.broadcasted_iota(jnp.int32, (rows, 128), 1)
    key = lax.broadcasted_iota(jnp.int32, (rows, span), 1)
    extra = jnp.zeros((rows, 128), jnp.float32)
    blocks = [(ref, p) for p in range(2) for ref in (own_ref, other_ref)]
    ones = jnp.ones((span, 128), jnp.bfloat16)
    for step in range(16 // each):
        h = step * each // 8
        heads = [step * each + g for g in range(each)]
        q = jnp.concatenate([q_ref[here, j * 128 : (j + 1) * 128] for j in heads], axis=0)
        high = jnp.full((each * rows, 1), lowest, jnp.float32)
        for b, (ref, p) in enumerate(blocks):
            s = lax.dot_general(
                q,
                ref[p, 0, :, h * 128 : (h + 1) * 128],
                (((1,), (1,)), ((), ())),
                preferred_element_type=jnp.float32,
            )
            keep = key < reach_ref[here, b : b + 1]
            s = jnp.concatenate(
                [jnp.where(keep, s[g * rows : (g + 1) * rows], lowest) for g in range(each)],
                axis=0,
            )
            s_ref[:, b * span : (b + 1) * span] = s
            high = jnp.maximum(high, jnp.max(s, axis=1, keepdims=True))
        acc = jnp.zeros((each * rows, 256), jnp.float32)
        for b, (ref, p) in enumerate(blocks):
            w = jnp.exp2((s_ref[:, b * span : (b + 1) * span] - high) * factor)
            v = jnp.concatenate([ref[p, 1, :, h * 128 : (h + 1) * 128], ones], axis=1)
            acc += jnp.dot(w.astype(jnp.bfloat16), v, preferred_element_type=jnp.float32)
        for g, j in enumerate(heads):
            part = slice(g * rows, (g + 1) * rows)
            total = acc[part, 128:]
            out_ref[:, j * 128 : (j + 1) * 128] = (acc[part, :128] / total).astype(jnp.bfloat16)
            level = high[part] * factor + jnp.log2(total)
            for i, piece in enumerate(split3(level)):
                extra = jnp.where(lane == j + 16 * i, piece, extra)
    out_ref[:, 2048:] = extra.astype(jnp.bfloat16)


def level_of(extra):
    extra = extra.astype(jnp.float32)
    return extra + pltpu.roll(extra, 112, 1) + pltpu.roll(extra, 96, 1)


def join(parts, levels):
    high = levels[0]
    for level in levels[1:]:
        high = jnp.maximum(high, level)
    shares = [jnp.exp2(level - high) for level in levels]
    total = shares[0]
    for share in shares[1:]:
        total = total + share
    shares = [share / total for share in shares]
    heads = []
    for j in range(16):
        value = None
        for part, share in zip(parts, shares):
            term = part(j).astype(jnp.float32) * share[:, j : j + 1]
            value = term if value is None else value + term
        heads.append(value)
    return heads, high + jnp.log2(total)


def join4_kernel(a_ref, b_ref, c_ref, low_ref, high_ref, out_ref):
    refs = (a_ref, b_ref, c_ref)

    def halves(columns):
        return jnp.concatenate([low_ref[:, columns], high_ref[:, columns]], axis=0)

    parts = [lambda j, r=r: r[:, j * 128 : (j + 1) * 128] for r in refs]
    parts.append(lambda j: halves(slice(j * 128, (j + 1) * 128)))
    levels = [level_of(r[:, 2048:]) for r in refs] + [level_of(halves(slice(2048, 2176)))]
    heads, level = join(parts, levels)
    lane = lax.broadcasted_iota(jnp.int32, level.shape, 1)
    for j, value in enumerate(heads):
        out_ref[:, j * 128 : (j + 1) * 128] = value.astype(jnp.bfloat16)
    hi, mid, lo = split3(level)
    extra = jnp.where(
        lane < 16,
        hi,
        jnp.where(
            lane < 32,
            pltpu.roll(mid, 16, 1),
            jnp.where(lane < 48, pltpu.roll(lo, 32, 1), 0.0),
        ),
    )
    out_ref[:, 2048:] = extra.astype(jnp.bfloat16)


def join9_kernel(got_ref, tail_ref, tail_level_ref, out_ref, copies_ref):
    parts = [lambda j, i=i: got_ref[i, :, j * 128 : (j + 1) * 128] for i in range(NZ)]
    levels = [level_of(got_ref[i, :, 2048:]) for i in range(NZ)]
    parts.append(lambda j: tail_ref[:, j * 128 : (j + 1) * 128])
    levels.append(tail_level_ref[...])
    heads, _ = join(parts, levels)
    for j, value in enumerate(heads):
        value = value.astype(jnp.bfloat16)
        out_ref[:, j * 128 : (j + 1) * 128] = value
        for i in range(NZ):
            copies_ref[i, :, j * 128 : (j + 1) * 128] = value


def project_kernel(place_ref, own_ref, other_ref, w0_ref, w1_ref, w2_ref, w3_ref, out_ref, rows_ref):
    c, y = place_ref[0], place_ref[1]
    rows_ref[c] = own_ref[...]
    rows_ref[1 - c] = other_ref[...]
    rows = jnp.concatenate([rows_ref[0], rows_ref[1]], axis=0)
    for j, w_ref in enumerate((w0_ref, w1_ref, w2_ref, w3_ref)):
        part = lax.dot_general(
            w_ref[...], rows, (((1,), (1,)), ((), ())), preferred_element_type=jnp.float32
        )
        out_ref[lax.rem(y + j, NY)] = part.astype(jnp.bfloat16)


def stream_kernel(got_ref, residual_ref, gain_ref, out_ref):
    total = residual_ref[...].astype(jnp.float32)
    for t in range(NX):
        total = total + got_ref[t].astype(jnp.float32)
    stream = total.astype(jnp.bfloat16).astype(jnp.float32)
    second = jnp.sum(stream * stream, axis=0, keepdims=True)
    hi, mid, lo = split3(second)
    row = lax.broadcasted_iota(jnp.int32, (16, stream.shape[1]), 0)
    extra = jnp.where(row == 0, hi, jnp.where(row == 1, mid, jnp.where(row == 2, lo, 0.0)))
    scaled = (stream * gain_ref[...]).astype(jnp.bfloat16)
    extra = extra.astype(jnp.bfloat16)
    count = stream.shape[0]
    for i in range(NZ):
        out_ref[i, :count] = scaled
        out_ref[i, count:] = extra


def fetch_kernel(w_hbm, out_ref, sem):
    copy = pltpu.make_async_copy(w_hbm, out_ref, sem)
    copy.start()
    copy.wait()


def logits_kernel(slots, place_ref, *refs):
    mine, theirs, w_ref = refs[:4], refs[4:8], refs[8]
    outs, a_ref = list(refs[9:-1]), refs[-1]
    span = 512
    width = w_ref.shape[1]
    c, turn = place_ref[0], place_ref[2]
    for k in range(NY):
        a_ref[c, k] = mine[k][...]
        a_ref[1 - c, k] = theirs[k][...]
    chunk = mine[0].shape[0] // NZ
    count = chunk - 16
    targets = []
    for s, whole in slots:
        targets.append(outs[:1] if whole else outs[:2])
        outs = outs[1:] if whole else outs[2:]

    def put(target, columns, value):
        rows = value.shape[0] // len(target)
        for i, ref in enumerate(target):
            ref[:, columns] = value[i * rows : (i + 1) * rows]

    lefts = []
    for (s, _), target in zip(slots, targets):
        k = lax.rem(turn + NY - s, NY)
        left = jnp.concatenate(
            [
                a_ref[d, k, z * chunk : z * chunk + count]
                for z in range(NZ)
                for d in range(NC)
            ],
            axis=0,
        )
        extra = jnp.zeros((16, 128), jnp.float32)
        for z in range(NZ):
            for d in range(NC):
                extra += a_ref[d, k, z * chunk + count : (z + 1) * chunk].astype(jnp.float32)
        second = extra[0:1] + extra[1:2] + extra[2:3]
        hi, mid, lo = split3(second)
        row = lax.broadcasted_iota(jnp.int32, (128, 128), 0)
        table = jnp.where(row == 0, hi, jnp.where(row == 1, mid, jnp.where(row == 2, lo, 0.0)))
        put(target, slice(width, width + 128), jnp.transpose(table).astype(jnp.bfloat16))
        lefts.append(jnp.transpose(left))
    lefts = jnp.concatenate(lefts, axis=0)
    for n in range(width // span):
        columns = slice(n * span, (n + 1) * span)
        part = jnp.dot(lefts, w_ref[:, columns], preferred_element_type=jnp.float32)
        part = part.astype(jnp.bfloat16)
        for i, target in enumerate(targets):
            put(target, columns, part[i * 128 : (i + 1) * 128])


def add_kernel(a_ref, b_ref, c_ref, d_ref, ab_ref, cd_ref):
    for one, two, out_ref in ((a_ref, b_ref, ab_ref), (c_ref, d_ref, cd_ref)):
        width = one.shape[1] - 128
        value = one[:, :width].astype(jnp.float32) + two[:, :width].astype(jnp.float32)
        out_ref[:, :width] = value.astype(jnp.bfloat16)
        extra = one[:, width:].astype(jnp.float32) + two[:, width:].astype(jnp.float32)
        second = extra[:, 0:1] + extra[:, 1:2] + extra[:, 2:3]
        hi, mid, lo = split3(second)
        lane = lax.broadcasted_iota(jnp.int32, extra.shape, 1)
        extra = jnp.where(lane == 0, hi, jnp.where(lane == 1, mid, jnp.where(lane == 2, lo, 0.0)))
        out_ref[:, width:] = extra.astype(jnp.bfloat16)


def stats_kernel(own_ref, a_ref, b_ref, c_ref, d_ref, allowed_ref, column_ref, out_ref, l_ref):
    rows = own_ref.shape[0]
    width = allowed_ref.shape[1] * 128

    def summed(lo):
        part = [r[:, lo : lo + 128].astype(jnp.float32) for r in (a_ref, b_ref, c_ref, d_ref)]
        others = jnp.concatenate([part[0] + part[1], part[2] + part[3]], axis=0)
        return own_ref[:, lo : lo + 128].astype(jnp.float32) + others

    extra = summed(width)
    second = (extra[:, 0:1] + extra[:, 1:2] + extra[:, 2:3]) / 5120.0
    scale = lax.rsqrt(second + epsilon)
    lane = lax.broadcasted_iota(jnp.int32, (rows, 128), 1)
    column = column_ref[...]
    high = jnp.full((rows, 128), lowest, jnp.float32)
    pick = jnp.zeros((rows, 128), jnp.float32)
    for j in range(width // 128):
        logit = summed(j * 128) * scale
        pick += jnp.where(lane + j * 128 == column, logit, 0.0)
        logit = jnp.where(allowed_ref[:, j : j + 1] > 0, logit, lowest)
        l_ref[:, j * 128 : (j + 1) * 128] = logit
        high = jnp.maximum(high, logit)
    top = jnp.max(high, axis=1, keepdims=True)
    total = jnp.zeros((rows, 128), jnp.float32)
    for j in range(width // 128):
        logit = l_ref[:, j * 128 : (j + 1) * 128]
        total += jnp.where(allowed_ref[:, j : j + 1] > 0, jnp.exp(logit - top), 0.0)
    total = jnp.sum(total, axis=1, keepdims=True)
    pick = jnp.sum(pick, axis=1, keepdims=True)
    level = jnp.where(total > 0.0, top + jnp.log(jnp.where(total > 0.0, total, 1.0)), lowest)
    table = jnp.where(lane == 0, level, jnp.where(lane == 1, pick, 0.0))
    out_ref[...] = jnp.transpose(table)[:8]


def per_device(
    queries,
    prefix_kv,
    tail_kv,
    row_prompt,
    prefix_len,
    tail_len,
    out_weight,
    residual,
    norm_gain,
    vocab_weight,
    allowed,
    next_token,
):
    rows_dev, heads, head_dim = queries.shape
    kv_heads = tail_kv.shape[3]
    tail_width = tail_kv.shape[2]
    group = heads // kv_heads
    width = heads * head_dim
    owner = lax.axis_index("ctx")
    x = lax.axis_index("tp")
    y, z, c = owner // (NZ * NC), (owner // NC) % NZ, owner % NC
    inv_root = 1.0 / math.sqrt(head_dim)
    span = prefix_kv.shape[2]

    q_copies = call(
        copies_kernel,
        jax.ShapeDtypeStruct((NZ, rows_dev, width), jnp.bfloat16),
        (queries,),
        flops=1000,
    )
    q_copies, prefix_kv = lax.optimization_barrier((q_copies, prefix_kv))
    q_z = lax.all_to_all(
        q_copies,
        "ctx",
        split_axis=0,
        concat_axis=0,
        tiled=True,
        axis_index_groups=z_groups,
    ).reshape(NZ * rows_dev, width)
    kv_own = prefix_kv.reshape(2, 2, span, kv_heads * head_dim)
    kv_other = lax.ppermute(kv_own, "ctx", core_swap)

    local_rows = residual.shape[0]

    def core_major(array):
        rest = array.shape[1:]
        array = array.reshape((NZ, NC, rows_dev) + rest)
        return jnp.swapaxes(array, 0, 1).reshape((local_rows,) + rest)

    residual_c = core_major(residual).T
    columns_dev = residual.shape[1]
    gain = lax.dynamic_slice_in_dim(
        norm_gain, (x * NZ * NC + z * NC + c) * columns_dev, columns_dev, 0
    ).astype(jnp.float32)
    gain = jnp.broadcast_to(gain[:, None], (columns_dev, local_rows))
    place = jnp.stack([c, y, (y + NY - x) % NY, x]).astype(jnp.int32)

    base = jnp.stack([owner * span, (owner + 1 - 2 * c) * span])
    limit = jnp.clip(prefix_len[:, None] - base[None, :], 0, span)
    reach = jnp.where(
        row_prompt[:, None, None] == jnp.arange(2, dtype=jnp.int32)[None, :, None],
        limit[:, None, :],
        0,
    ).reshape(NY, NZ, NC, rows_dev, 4)
    reach = lax.dynamic_index_in_dim(reach, c, 2, keepdims=False).reshape(NY, NZ * rows_dev, 4)

    reaches = [
        lax.dynamic_index_in_dim(reach, (y + NY - k) % NY, 0, keepdims=False) for k in range(NY)
    ]
    q_z, kv_other, reaches = lax.optimization_barrier((q_z, kv_other, reaches))
    group_rows = NZ * rows_dev

    def attend(q, k, first=0, rows=group_rows):
        return call(
            functools.partial(attend_kernel, first, rows),
            jax.ShapeDtypeStruct((rows, width + 128), jnp.bfloat16),
            (q, kv_own, kv_other, reaches[k]),
            flops=2 * 2 * rows * 2048 * 2048,
            scratch=[VMEM((256, 4 * span), jnp.float32)],
        )

    visitors = {k: lax.ppermute(q_z, "ctx", y_shift(k)) for k in (1, 3)}
    own_part = attend(q_z, 0)
    q_later, last = lax.optimization_barrier((q_z, own_part))
    visitors[2] = lax.ppermute(q_later, "ctx", y_shift(2))
    back = []
    half = group_rows // 2
    for k, first, rows in (
        (1, 0, group_rows),
        (3, 0, group_rows),
        (2, 0, half),
        (2, half, half),
    ):
        visitor, last = lax.optimization_barrier((visitors[k], last))
        last = attend(visitor, k, first, rows)
        back.append(lax.ppermute(last, "ctx", y_shift(-k)))

    own_queries, tail_kv, _ = lax.optimization_barrier((queries, tail_kv, last))
    own_queries = own_queries.reshape(rows_dev, kv_heads, group, head_dim)
    tail_scores = (
        jnp.einsum(
            "rhgd,rkhd->rhgk", own_queries, tail_kv[:, 0], preferred_element_type=jnp.float32
        )
        * inv_root
    )
    tail_scores, back[3] = lax.optimization_barrier((tail_scores, back[3]))
    tail_keep = (jnp.arange(tail_width, dtype=jnp.int32)[None, :] < tail_len[:, None])[
        :, None, None, :
    ]
    tail_high = jnp.max(jnp.where(tail_keep, tail_scores, lowest), axis=-1)
    tail_weights = jnp.where(tail_keep, jnp.exp(tail_scores - tail_high[..., None]), 0.0).astype(
        jnp.bfloat16
    )
    tail_total = jnp.sum(tail_weights.astype(jnp.float32), axis=-1)
    tail_sum = jnp.einsum(
        "rhgk,rkhd->rhgd", tail_weights, tail_kv[:, 1], preferred_element_type=jnp.float32
    )
    tail_out = (tail_sum / tail_total[..., None]).reshape(rows_dev, width)
    tail_level = (tail_high * LOG2E + jnp.log2(tail_total)).reshape(rows_dev, heads)
    tail_level = jnp.pad(tail_level, ((0, 0), (0, 128 - heads)))

    joined = call(
        join4_kernel,
        jax.ShapeDtypeStruct((group_rows, width + 128), jnp.bfloat16),
        (own_part,) + tuple(back),
        flops=1000000,
    )

    weight_own, joined = lax.optimization_barrier((out_weight.T, joined))
    weights = [weight_own] + [lax.ppermute(weight_own, "ctx", y_shift(-k)) for k in (1, 2, 3)]
    got = lax.all_to_all(
        joined.reshape(NZ, rows_dev, width + 128),
        "ctx",
        split_axis=0,
        concat_axis=0,
        tiled=True,
        axis_index_groups=z_groups,
    )
    attended, copies = call(
        join9_kernel,
        (
            jax.ShapeDtypeStruct((rows_dev, width), jnp.bfloat16),
            jax.ShapeDtypeStruct((NZ, rows_dev, width), jnp.bfloat16),
        ),
        (got, tail_out, tail_level),
        flops=1000000,
    )

    copies, weights[1], weights[3] = lax.optimization_barrier((copies, weights[1], weights[3]))
    rows_own = lax.all_to_all(
        copies, "ctx", split_axis=0, concat_axis=0, tiled=True, axis_index_groups=z_groups
    ).reshape(NZ * rows_dev, width)
    rows_other = lax.ppermute(rows_own, "ctx", core_swap)
    projected = call(
        project_kernel,
        jax.ShapeDtypeStruct((NY, columns_dev, local_rows), jnp.bfloat16),
        (rows_own, rows_other) + tuple(weights),
        flops=2 * 128 * 320 * 2048,
        scratch=[VMEM((NC, NZ * rows_dev, width), jnp.bfloat16)],
        place=place,
    )
    residual_c, projected = lax.optimization_barrier((residual_c, projected))
    residual_t = lax.ppermute(residual_c, ("ctx", "tp"), turned(0))
    pieces = lax.all_to_all(projected, "tp", split_axis=0, concat_axis=0, tiled=True)
    streams = call(
        stream_kernel,
        jax.ShapeDtypeStruct((NZ, columns_dev + 16, local_rows), jnp.bfloat16),
        (pieces, residual_t, gain),
        flops=1000000,
    )

    block = lax.all_to_all(
        streams, "ctx", split_axis=0, concat_axis=0, tiled=True, axis_index_groups=z_groups
    ).reshape(NZ * (columns_dev + 16), local_rows)
    mine = [block] + [lax.ppermute(block, "ctx", y_shift(k)) for k in (1, 2, 3)]
    _, vocab_later = lax.optimization_barrier((block, vocab_weight))
    vocab_local = call(
        fetch_kernel,
        jax.ShapeDtypeStruct(vocab_weight.shape, jnp.bfloat16),
        (vocab_later,),
        flops=1000,
        scratch=[pltpu.SemaphoreType.DMA],
        far=(0,),
    )
    mine[2], vocab_local = lax.optimization_barrier((mine[2], vocab_local))
    theirs = [lax.ppermute(one, "ctx", core_swap) for one in mine]
    vocab_here = vocab_weight.shape[1]
    whole = jax.ShapeDtypeStruct((local_rows, vocab_here + 128), jnp.bfloat16)
    part = jax.ShapeDtypeStruct((local_rows // 2, vocab_here + 128), jnp.bfloat16)
    def logits_of(slots, shapes, mine):
        return call(
            functools.partial(logits_kernel, slots),
            shapes,
            tuple(mine) + tuple(theirs) + (vocab_local,),
            flops=2 * 128 * len(slots) * 1280 * 2048,
            scratch=[VMEM((NC, NY) + block.shape, jnp.bfloat16)],
            place=place,
            limit=24,
        )

    low2, high2 = logits_of(((2, False),), (part,) * 2, mine)
    block, _, _ = lax.optimization_barrier((block, low2, high2))
    low1, high1, low3, high3, own = logits_of(
        ((1, False), (3, False), (0, True)), (part,) * 4 + (whole,), [block] + mine[1:]
    )
    up, down = x_shift(1), x_shift(3)
    via_up = lax.ppermute(low2, "tp", up)
    via_down = lax.ppermute(high2, "tp", down)
    high_up = lax.ppermute(high1, "tp", up)
    low_down = lax.ppermute(low3, "tp", down)
    low_sum, high_sum = call(
        add_kernel, (part, part), (via_up, low1, via_down, high3), flops=1000000
    )
    low_up = lax.ppermute(low_sum, "tp", up)
    high_down = lax.ppermute(high_sum, "tp", down)
    sums = (own, low_up, low_down, high_up, high_down)
    stats = call(
        stats_kernel,
        jax.ShapeDtypeStruct((8, local_rows), jnp.float32),
        tuple(sums)
        + (core_major(allowed), core_major((next_token - owner * vocab_here)[:, None])),
        flops=1000000,
        scratch=[VMEM((local_rows, vocab_here), jnp.float32)],
    )[:2]
    every = lax.all_to_all(
        jnp.broadcast_to(stats[None], (NY * NZ * NC,) + stats.shape),
        "ctx",
        split_axis=0,
        concat_axis=0,
        tiled=True,
    )
    peak = jnp.max(every[:, 0], axis=0)
    total = jnp.sum(jnp.exp(every[:, 0] - peak[None]), axis=0)
    logprob = jnp.sum(every[:, 1], axis=0) - (peak + jnp.log(total))
    logprob = jnp.swapaxes(logprob.reshape(NC, NZ, rows_dev), 0, 1).reshape(local_rows)
    return (attended, logprob)


def solution(mesh):
    placed = (
        P("ctx", "tp", None),
        P(None, None, "ctx", "tp", None),
        P("ctx", None, None, "tp", None),
        P(),
        P(),
        P("ctx"),
        P("tp", "ctx"),
        P("tp", "ctx"),
        P(),
        P("tp", "ctx"),
        P("tp", "ctx"),
        P("tp"),
    )
    return jax.shard_map(
        per_device, mesh=mesh, in_specs=placed, out_specs=(P("ctx", "tp"), P("tp")), check_vma=False
    )
```

```python
import functools
import math

import jax
import jax.numpy as jnp
from jax import lax
from jax.experimental import pallas as pl
from jax.experimental.pallas import tpu as pltpu
from jax.sharding import PartitionSpec as P

lowest = -1e30
epsilon = 1e-06
LOG2E = 1.4426950408889634
NY, NZ, NC, NX = 4, 8, 2, 4
VMEM = pltpu.VMEM


def ctx_id(y, z, c):
    return (y % NY) * (NZ * NC) + (z % NZ) * NC + c % NC


def chips():
    return [(y, z, c) for y in range(NY) for z in range(NZ) for c in range(NC)]


core_swap = [(ctx_id(y, z, c), ctx_id(y, z, 1 - c)) for y, z, c in chips()]
z_groups = [[ctx_id(y, z, c) for z in range(NZ)] for y in range(NY) for c in range(NC)]


def y_shift(d):
    return [(ctx_id(y, z, c), ctx_id(y + d, z, c)) for y, z, c in chips()]


def x_shift(d):
    return [(t, (t + d) % NX) for t in range(NX)]


def turned(s):
    return [
        (ctx_id(y, z, c) * NX + t, ctx_id(t + s, z, c) * NX + y)
        for t in range(NX)
        for y, z, c in chips()
    ]


def split3(value):
    hi = value.astype(jnp.bfloat16).astype(jnp.float32)
    rest = value - hi
    mid = rest.astype(jnp.bfloat16).astype(jnp.float32)
    return hi, mid, rest - mid


def call(kernel, out_shape, args, flops, scratch=(), place=None, limit=24, far=()):
    size = sum(math.prod(a.shape) * a.dtype.itemsize for a in args)
    specs = [
        pl.BlockSpec(memory_space=pltpu.HBM if i in far else VMEM) for i in range(len(args))
    ]
    if place is not None:
        specs = [pl.BlockSpec(memory_space=pltpu.SMEM)] + specs
        args = (place,) + tuple(args)
    return pl.pallas_call(
        kernel,
        out_shape=out_shape,
        in_specs=specs,
        out_specs=jax.tree.map(lambda _: pl.BlockSpec(memory_space=VMEM), out_shape),
        scratch_shapes=list(scratch),
        compiler_params=pltpu.CompilerParams(vmem_limit_bytes=limit * 1024 * 1024),
        cost_estimate=pl.CostEstimate(flops=flops, bytes_accessed=size, transcendentals=0),
    )(*args)


def copies_kernel(q_ref, out_ref):
    for j in range(q_ref.shape[1]):
        part = q_ref[:, j, :]
        for i in range(out_ref.shape[0]):
            out_ref[i, :, j * 128 : (j + 1) * 128] = part


def attend_kernel(first, rows, q_ref, own_ref, other_ref, reach_ref, out_ref, s_ref):
    here = slice(first, first + rows)
    each = 256 // rows
    span = own_ref.shape[2]
    factor = LOG2E / math.sqrt(128)
    lane = lax.broadcasted_iota(jnp.int32, (rows, 128), 1)
    key = lax.broadcasted_iota(jnp.int32, (rows, span), 1)
    extra = jnp.zeros((rows, 128), jnp.float32)
    blocks = (own_ref, other_ref)
    prompt = jnp.broadcast_to(reach_ref[here, 2:3], (rows, 128))
    is_one = prompt.astype(jnp.float32).astype(jnp.bfloat16)
    is_zero = (1.0 - prompt.astype(jnp.float32)).astype(jnp.bfloat16)
    for step in range(16 // each):
        h = step * each // 8
        columns = slice(h * 128, (h + 1) * 128)
        heads = [step * each + g for g in range(each)]
        q = [q_ref[here, j * 128 : (j + 1) * 128] for j in heads]
        q = jnp.concatenate(
            [
                jnp.concatenate([part * is_zero for part in q], axis=0),
                jnp.concatenate([part * is_one for part in q], axis=0),
            ],
            axis=1,
        )
        high = jnp.full((each * rows, 1), lowest, jnp.float32)
        for b, ref in enumerate(blocks):
            s = lax.dot_general(
                q,
                jnp.concatenate([ref[0, 0, :, columns], ref[1, 0, :, columns]], axis=1),
                (((1,), (1,)), ((), ())),
                preferred_element_type=jnp.float32,
            )
            keep = key < reach_ref[here, b : b + 1]
            s = jnp.concatenate(
                [jnp.where(keep, s[g * rows : (g + 1) * rows], lowest) for g in range(each)],
                axis=0,
            )
            s_ref[:, b * span : (b + 1) * span] = s
            high = jnp.maximum(high, jnp.max(s, axis=1, keepdims=True))
        acc = jnp.zeros((each * rows, 256), jnp.float32)
        total = jnp.zeros((each * rows, 128), jnp.float32)
        for b, ref in enumerate(blocks):
            w = jnp.exp2((s_ref[:, b * span : (b + 1) * span] - high) * factor)
            w = w.astype(jnp.bfloat16)
            v = jnp.concatenate([ref[0, 1, :, columns], ref[1, 1, :, columns]], axis=1)
            acc += jnp.dot(w, v, preferred_element_type=jnp.float32)
            wide = w.astype(jnp.float32)
            for i in range(span // 128):
                total += wide[:, i * 128 : (i + 1) * 128]
        total = jnp.sum(total, axis=1, keepdims=True)
        for g, j in enumerate(heads):
            part = slice(g * rows, (g + 1) * rows)
            value = jnp.where(prompt == 0, acc[part, :128], acc[part, 128:]) / total[part]
            out_ref[:, j * 128 : (j + 1) * 128] = value.astype(jnp.bfloat16)
            level = high[part] * factor + jnp.log2(total[part])
            for i, piece in enumerate(split3(level)):
                extra = jnp.where(lane == j + 16 * i, piece, extra)
    out_ref[:, 2048:] = extra.astype(jnp.bfloat16)


def level_of(extra):
    extra = extra.astype(jnp.float32)
    return extra + pltpu.roll(extra, 112, 1) + pltpu.roll(extra, 96, 1)


def join(parts, levels):
    high = levels[0]
    for level in levels[1:]:
        high = jnp.maximum(high, level)
    shares = [jnp.exp2(level - high) for level in levels]
    total = shares[0]
    for share in shares[1:]:
        total = total + share
    shares = [share / total for share in shares]
    heads = []
    for j in range(16):
        value = None
        for part, share in zip(parts, shares):
            term = part(j).astype(jnp.float32) * share[:, j : j + 1]
            value = term if value is None else value + term
        heads.append(value)
    return heads, high + jnp.log2(total)


def join4_kernel(a_ref, b_ref, c_ref, low_ref, high_ref, out_ref):
    refs = (a_ref, b_ref, c_ref)

    def halves(columns):
        return jnp.concatenate([low_ref[:, columns], high_ref[:, columns]], axis=0)

    parts = [lambda j, r=r: r[:, j * 128 : (j + 1) * 128] for r in refs]
    parts.append(lambda j: halves(slice(j * 128, (j + 1) * 128)))
    levels = [level_of(r[:, 2048:]) for r in refs] + [level_of(halves(slice(2048, 2176)))]
    heads, level = join(parts, levels)
    lane = lax.broadcasted_iota(jnp.int32, level.shape, 1)
    for j, value in enumerate(heads):
        out_ref[:, j * 128 : (j + 1) * 128] = value.astype(jnp.bfloat16)
    hi, mid, lo = split3(level)
    extra = jnp.where(
        lane < 16,
        hi,
        jnp.where(
            lane < 32,
            pltpu.roll(mid, 16, 1),
            jnp.where(lane < 48, pltpu.roll(lo, 32, 1), 0.0),
        ),
    )
    out_ref[:, 2048:] = extra.astype(jnp.bfloat16)


def join9_kernel(got_ref, tail_ref, tail_level_ref, out_ref, copies_ref):
    parts = [lambda j, i=i: got_ref[i, :, j * 128 : (j + 1) * 128] for i in range(NZ)]
    levels = [level_of(got_ref[i, :, 2048:]) for i in range(NZ)]
    parts.append(lambda j: tail_ref[:, j * 128 : (j + 1) * 128])
    levels.append(tail_level_ref[...])
    heads, _ = join(parts, levels)
    for j, value in enumerate(heads):
        value = value.astype(jnp.bfloat16)
        out_ref[:, j * 128 : (j + 1) * 128] = value
        for i in range(NZ):
            copies_ref[i, :, j * 128 : (j + 1) * 128] = value


def project_kernel(place_ref, own_ref, other_ref, w0_ref, w1_ref, w2_ref, w3_ref, out_ref, rows_ref):
    c, y = place_ref[0], place_ref[1]
    rows_ref[c] = own_ref[...]
    rows_ref[1 - c] = other_ref[...]
    rows = jnp.concatenate([rows_ref[0], rows_ref[1]], axis=0)
    for j, w_ref in enumerate((w0_ref, w1_ref, w2_ref, w3_ref)):
        part = lax.dot_general(
            w_ref[...], rows, (((1,), (1,)), ((), ())), preferred_element_type=jnp.float32
        )
        out_ref[lax.rem(y + j, NY)] = part.astype(jnp.bfloat16)


def stream_kernel(got_ref, residual_ref, gain_ref, out_ref):
    total = residual_ref[...].astype(jnp.float32)
    for t in range(NX):
        total = total + got_ref[t].astype(jnp.float32)
    stream = total.astype(jnp.bfloat16).astype(jnp.float32)
    second = jnp.sum(stream * stream, axis=0, keepdims=True)
    hi, mid, lo = split3(second)
    row = lax.broadcasted_iota(jnp.int32, (16, stream.shape[1]), 0)
    extra = jnp.where(row == 0, hi, jnp.where(row == 1, mid, jnp.where(row == 2, lo, 0.0)))
    scaled = (stream * gain_ref[...]).astype(jnp.bfloat16)
    extra = extra.astype(jnp.bfloat16)
    count = stream.shape[0]
    for i in range(NZ):
        out_ref[i, :count] = scaled
        out_ref[i, count:] = extra


def fetch_kernel(w_hbm, out_ref, sem):
    copy = pltpu.make_async_copy(w_hbm, out_ref, sem)
    copy.start()
    copy.wait()


def logits_kernel(slots, place_ref, *refs):
    mine, theirs, w_ref = refs[:4], refs[4:8], refs[8]
    outs, a_ref = list(refs[9:-1]), refs[-1]
    span = 512
    width = w_ref.shape[1]
    c, turn = place_ref[0], place_ref[2]
    for k in range(NY):
        a_ref[c, k] = mine[k][...]
        a_ref[1 - c, k] = theirs[k][...]
    chunk = mine[0].shape[0] // NZ
    count = chunk - 16
    targets = []
    for s, whole in slots:
        targets.append(outs[:1] if whole else outs[:2])
        outs = outs[1:] if whole else outs[2:]

    def put(target, columns, value):
        rows = value.shape[0] // len(target)
        for i, ref in enumerate(target):
            ref[:, columns] = value[i * rows : (i + 1) * rows]

    lefts = []
    for (s, _), target in zip(slots, targets):
        k = lax.rem(turn + NY - s, NY)
        left = jnp.concatenate(
            [
                a_ref[d, k, z * chunk : z * chunk + count]
                for z in range(NZ)
                for d in range(NC)
            ],
            axis=0,
        )
        extra = jnp.zeros((16, 128), jnp.float32)
        for z in range(NZ):
            for d in range(NC):
                extra += a_ref[d, k, z * chunk + count : (z + 1) * chunk].astype(jnp.float32)
        second = extra[0:1] + extra[1:2] + extra[2:3]
        hi, mid, lo = split3(second)
        row = lax.broadcasted_iota(jnp.int32, (128, 128), 0)
        table = jnp.where(row == 0, hi, jnp.where(row == 1, mid, jnp.where(row == 2, lo, 0.0)))
        put(target, slice(width, width + 128), jnp.transpose(table).astype(jnp.bfloat16))
        lefts.append(jnp.transpose(left))
    lefts = jnp.concatenate(lefts, axis=0)
    for n in range(width // span):
        columns = slice(n * span, (n + 1) * span)
        part = jnp.dot(lefts, w_ref[:, columns], preferred_element_type=jnp.float32)
        part = part.astype(jnp.bfloat16)
        for i, target in enumerate(targets):
            put(target, columns, part[i * 128 : (i + 1) * 128])


def add_kernel(a_ref, b_ref, c_ref, d_ref, ab_ref, cd_ref):
    for one, two, out_ref in ((a_ref, b_ref, ab_ref), (c_ref, d_ref, cd_ref)):
        width = one.shape[1] - 128
        value = one[:, :width].astype(jnp.float32) + two[:, :width].astype(jnp.float32)
        out_ref[:, :width] = value.astype(jnp.bfloat16)
        extra = one[:, width:].astype(jnp.float32) + two[:, width:].astype(jnp.float32)
        second = extra[:, 0:1] + extra[:, 1:2] + extra[:, 2:3]
        hi, mid, lo = split3(second)
        lane = lax.broadcasted_iota(jnp.int32, extra.shape, 1)
        extra = jnp.where(lane == 0, hi, jnp.where(lane == 1, mid, jnp.where(lane == 2, lo, 0.0)))
        out_ref[:, width:] = extra.astype(jnp.bfloat16)


def stats_kernel(own_ref, a_ref, b_ref, c_ref, d_ref, allowed_ref, column_ref, out_ref, l_ref):
    rows = own_ref.shape[0]
    width = allowed_ref.shape[1] * 128

    def summed(lo):
        part = [r[:, lo : lo + 128].astype(jnp.float32) for r in (a_ref, b_ref, c_ref, d_ref)]
        others = jnp.concatenate([part[0] + part[1], part[2] + part[3]], axis=0)
        return own_ref[:, lo : lo + 128].astype(jnp.float32) + others

    extra = summed(width)
    second = (extra[:, 0:1] + extra[:, 1:2] + extra[:, 2:3]) / 5120.0
    scale = lax.rsqrt(second + epsilon)
    lane = lax.broadcasted_iota(jnp.int32, (rows, 128), 1)
    column = column_ref[...]
    high = jnp.full((rows, 128), lowest, jnp.float32)
    pick = jnp.zeros((rows, 128), jnp.float32)
    for j in range(width // 128):
        logit = summed(j * 128) * scale
        pick += jnp.where(lane + j * 128 == column, logit, 0.0)
        logit = jnp.where(allowed_ref[:, j : j + 1] > 0, logit, lowest)
        l_ref[:, j * 128 : (j + 1) * 128] = logit
        high = jnp.maximum(high, logit)
    top = jnp.max(high, axis=1, keepdims=True)
    total = jnp.zeros((rows, 128), jnp.float32)
    for j in range(width // 128):
        logit = l_ref[:, j * 128 : (j + 1) * 128]
        total += jnp.where(allowed_ref[:, j : j + 1] > 0, jnp.exp(logit - top), 0.0)
    total = jnp.sum(total, axis=1, keepdims=True)
    pick = jnp.sum(pick, axis=1, keepdims=True)
    level = jnp.where(total > 0.0, top + jnp.log(jnp.where(total > 0.0, total, 1.0)), lowest)
    table = jnp.where(lane == 0, level, jnp.where(lane == 1, pick, 0.0))
    out_ref[...] = jnp.transpose(table)[:8]


def per_device(
    queries,
    prefix_kv,
    tail_kv,
    row_prompt,
    prefix_len,
    tail_len,
    out_weight,
    residual,
    norm_gain,
    vocab_weight,
    allowed,
    next_token,
):
    rows_dev, heads, head_dim = queries.shape
    kv_heads = tail_kv.shape[3]
    tail_width = tail_kv.shape[2]
    group = heads // kv_heads
    width = heads * head_dim
    owner = lax.axis_index("ctx")
    x = lax.axis_index("tp")
    y, z, c = owner // (NZ * NC), (owner // NC) % NZ, owner % NC
    inv_root = 1.0 / math.sqrt(head_dim)
    span = prefix_kv.shape[2]

    q_copies = call(
        copies_kernel,
        jax.ShapeDtypeStruct((NZ, rows_dev, width), jnp.bfloat16),
        (queries,),
        flops=1000,
    )
    q_copies, prefix_kv = lax.optimization_barrier((q_copies, prefix_kv))
    q_z = lax.all_to_all(
        q_copies,
        "ctx",
        split_axis=0,
        concat_axis=0,
        tiled=True,
        axis_index_groups=z_groups,
    ).reshape(NZ * rows_dev, width)
    kv_own = prefix_kv.reshape(2, 2, span, kv_heads * head_dim)
    kv_other = lax.ppermute(kv_own, "ctx", core_swap)

    local_rows = residual.shape[0]

    def core_major(array):
        rest = array.shape[1:]
        array = array.reshape((NZ, NC, rows_dev) + rest)
        return jnp.swapaxes(array, 0, 1).reshape((local_rows,) + rest)

    residual_c = core_major(residual).T
    columns_dev = residual.shape[1]
    gain = lax.dynamic_slice_in_dim(
        norm_gain, (x * NZ * NC + z * NC + c) * columns_dev, columns_dev, 0
    ).astype(jnp.float32)
    gain = jnp.broadcast_to(gain[:, None], (columns_dev, local_rows))
    place = jnp.stack([c, y, (y + NY - x) % NY, x]).astype(jnp.int32)

    base = jnp.stack([owner * span, (owner + 1 - 2 * c) * span])
    limit = jnp.clip(prefix_len[:, None] - base[None, :], 0, span)
    reach = jnp.concatenate([limit, row_prompt[:, None], row_prompt[:, None]], axis=1).reshape(
        NY, NZ, NC, rows_dev, 4
    )
    reach = lax.dynamic_index_in_dim(reach, c, 2, keepdims=False).reshape(NY, NZ * rows_dev, 4)

    reaches = [
        lax.dynamic_index_in_dim(reach, (y + NY - k) % NY, 0, keepdims=False) for k in range(NY)
    ]
    kv_other, residual_c = lax.optimization_barrier((kv_other, residual_c))
    residual_t = lax.ppermute(residual_c, ("ctx", "tp"), turned(0))
    q_z, kv_other, reaches, residual_t = lax.optimization_barrier(
        (q_z, kv_other, reaches, residual_t)
    )
    group_rows = NZ * rows_dev

    def attend(q, k, first=0, rows=group_rows):
        return call(
            functools.partial(attend_kernel, first, rows),
            jax.ShapeDtypeStruct((rows, width + 128), jnp.bfloat16),
            (q, kv_own, kv_other, reaches[k]),
            flops=2 * 2 * rows * 2048 * 2048,
            scratch=[VMEM((256, 2 * span), jnp.float32)],
        )

    visitors = {k: lax.ppermute(q_z, "ctx", y_shift(k)) for k in (1, 3)}
    own_part = attend(q_z, 0)
    q_later, last = lax.optimization_barrier((q_z, own_part))
    visitors[2] = lax.ppermute(q_later, "ctx", y_shift(2))
    back = []
    half = group_rows // 2
    for k, first, rows in (
        (1, 0, group_rows),
        (3, 0, group_rows),
        (2, 0, half),
        (2, half, half),
    ):
        visitor, last = lax.optimization_barrier((visitors[k], last))
        last = attend(visitor, k, first, rows)
        back.append(lax.ppermute(last, "ctx", y_shift(-k)))

    own_queries, tail_kv, _ = lax.optimization_barrier((queries, tail_kv, last))
    own_queries = own_queries.reshape(rows_dev, kv_heads, group, head_dim)
    tail_scores = (
        jnp.einsum(
            "rhgd,rkhd->rhgk", own_queries, tail_kv[:, 0], preferred_element_type=jnp.float32
        )
        * inv_root
    )
    tail_scores, back[3] = lax.optimization_barrier((tail_scores, back[3]))
    tail_keep = (jnp.arange(tail_width, dtype=jnp.int32)[None, :] < tail_len[:, None])[
        :, None, None, :
    ]
    tail_high = jnp.max(jnp.where(tail_keep, tail_scores, lowest), axis=-1)
    tail_weights = jnp.where(tail_keep, jnp.exp(tail_scores - tail_high[..., None]), 0.0).astype(
        jnp.bfloat16
    )
    tail_total = jnp.sum(tail_weights.astype(jnp.float32), axis=-1)
    tail_sum = jnp.einsum(
        "rhgk,rkhd->rhgd", tail_weights, tail_kv[:, 1], preferred_element_type=jnp.float32
    )
    tail_out = (tail_sum / tail_total[..., None]).reshape(rows_dev, width)
    tail_level = (tail_high * LOG2E + jnp.log2(tail_total)).reshape(rows_dev, heads)
    tail_level = jnp.pad(tail_level, ((0, 0), (0, 128 - heads)))

    joined = call(
        join4_kernel,
        jax.ShapeDtypeStruct((group_rows, width + 128), jnp.bfloat16),
        (own_part,) + tuple(back),
        flops=1000000,
    )

    weight_own, joined = lax.optimization_barrier((out_weight.T, joined))
    weights = [weight_own] + [lax.ppermute(weight_own, "ctx", y_shift(-k)) for k in (1, 2, 3)]
    got = lax.all_to_all(
        joined.reshape(NZ, rows_dev, width + 128),
        "ctx",
        split_axis=0,
        concat_axis=0,
        tiled=True,
        axis_index_groups=z_groups,
    )
    attended, copies = call(
        join9_kernel,
        (
            jax.ShapeDtypeStruct((rows_dev, width), jnp.bfloat16),
            jax.ShapeDtypeStruct((NZ, rows_dev, width), jnp.bfloat16),
        ),
        (got, tail_out, tail_level),
        flops=1000000,
    )

    copies, weights[1], weights[3] = lax.optimization_barrier((copies, weights[1], weights[3]))
    rows_own = lax.all_to_all(
        copies, "ctx", split_axis=0, concat_axis=0, tiled=True, axis_index_groups=z_groups
    ).reshape(NZ * rows_dev, width)
    rows_other = lax.ppermute(rows_own, "ctx", core_swap)
    projected = call(
        project_kernel,
        jax.ShapeDtypeStruct((NY, columns_dev, local_rows), jnp.bfloat16),
        (rows_own, rows_other) + tuple(weights),
        flops=2 * 128 * 320 * 2048,
        scratch=[VMEM((NC, NZ * rows_dev, width), jnp.bfloat16)],
        place=place,
    )
    pieces = lax.all_to_all(projected, "tp", split_axis=0, concat_axis=0, tiled=True)
    streams = call(
        stream_kernel,
        jax.ShapeDtypeStruct((NZ, columns_dev + 16, local_rows), jnp.bfloat16),
        (pieces, residual_t, gain),
        flops=1000000,
    )

    block = lax.all_to_all(
        streams, "ctx", split_axis=0, concat_axis=0, tiled=True, axis_index_groups=z_groups
    ).reshape(NZ * (columns_dev + 16), local_rows)
    mine = [block] + [lax.ppermute(block, "ctx", y_shift(k)) for k in (1, 2, 3)]
    _, vocab_later = lax.optimization_barrier((block, vocab_weight))
    vocab_local = call(
        fetch_kernel,
        jax.ShapeDtypeStruct(vocab_weight.shape, jnp.bfloat16),
        (vocab_later,),
        flops=1000,
        scratch=[pltpu.SemaphoreType.DMA],
        far=(0,),
    )
    mine[2], vocab_local = lax.optimization_barrier((mine[2], vocab_local))
    theirs = [lax.ppermute(one, "ctx", core_swap) for one in mine]
    vocab_here = vocab_weight.shape[1]
    whole = jax.ShapeDtypeStruct((local_rows, vocab_here + 128), jnp.bfloat16)
    part = jax.ShapeDtypeStruct((local_rows // 2, vocab_here + 128), jnp.bfloat16)
    def logits_of(slots, shapes, mine):
        return call(
            functools.partial(logits_kernel, slots),
            shapes,
            tuple(mine) + tuple(theirs) + (vocab_local,),
            flops=2 * 128 * len(slots) * 1280 * 2048,
            scratch=[VMEM((NC, NY) + block.shape, jnp.bfloat16)],
            place=place,
            limit=24,
        )

    low2, high2 = logits_of(((2, False),), (part,) * 2, mine)
    block, _, _ = lax.optimization_barrier((block, low2, high2))
    low1, high1, low3, high3, own = logits_of(
        ((1, False), (3, False), (0, True)), (part,) * 4 + (whole,), [block] + mine[1:]
    )
    up, down = x_shift(1), x_shift(3)
    via_up = lax.ppermute(low2, "tp", up)
    via_down = lax.ppermute(high2, "tp", down)
    high_up = lax.ppermute(high1, "tp", up)
    low_down = lax.ppermute(low3, "tp", down)
    low_sum, high_sum = call(
        add_kernel, (part, part), (via_up, low1, via_down, high3), flops=1000000
    )
    low_up = lax.ppermute(low_sum, "tp", up)
    high_down = lax.ppermute(high_sum, "tp", down)
    sums = (own, low_up, low_down, high_up, high_down)
    stats = call(
        stats_kernel,
        jax.ShapeDtypeStruct((8, local_rows), jnp.float32),
        tuple(sums)
        + (core_major(allowed), core_major((next_token - owner * vocab_here)[:, None])),
        flops=1000000,
        scratch=[VMEM((local_rows, vocab_here), jnp.float32)],
    )[:2]
    every = lax.all_to_all(
        jnp.broadcast_to(stats[None], (NY * NZ * NC,) + stats.shape),
        "ctx",
        split_axis=0,
        concat_axis=0,
        tiled=True,
    )
    peak = jnp.max(every[:, 0], axis=0)
    total = jnp.sum(jnp.exp(every[:, 0] - peak[None]), axis=0)
    logprob = jnp.sum(every[:, 1], axis=0) - (peak + jnp.log(total))
    logprob = jnp.swapaxes(logprob.reshape(NC, NZ, rows_dev), 0, 1).reshape(local_rows)
    return (attended, logprob)


def solution(mesh):
    placed = (
        P("ctx", "tp", None),
        P(None, None, "ctx", "tp", None),
        P("ctx", None, None, "tp", None),
        P(),
        P(),
        P("ctx"),
        P("tp", "ctx"),
        P("tp", "ctx"),
        P(),
        P("tp", "ctx"),
        P("tp", "ctx"),
        P("tp"),
    )
    return jax.shard_map(
        per_device, mesh=mesh, in_specs=placed, out_specs=(P("ctx", "tp"), P("tp")), check_vma=False
    )
```

```python
import functools
import math

import jax
import jax.numpy as jnp
from jax import lax
from jax.experimental import pallas as pl
from jax.experimental.pallas import tpu as pltpu
from jax.sharding import PartitionSpec as P

lowest = -1e30
epsilon = 1e-06
LOG2E = 1.4426950408889634
NY, NZ, NC, NX = 4, 8, 2, 4
VMEM = pltpu.VMEM


def ctx_id(y, z, c):
    return (y % NY) * (NZ * NC) + (z % NZ) * NC + c % NC


def chips():
    return [(y, z, c) for y in range(NY) for z in range(NZ) for c in range(NC)]


core_swap = [(ctx_id(y, z, c), ctx_id(y, z, 1 - c)) for y, z, c in chips()]
z_groups = [[ctx_id(y, z, c) for z in range(NZ)] for y in range(NY) for c in range(NC)]


def y_shift(d):
    return [(ctx_id(y, z, c), ctx_id(y + d, z, c)) for y, z, c in chips()]


def x_shift(d):
    return [(t, (t + d) % NX) for t in range(NX)]


def turned(s):
    return [
        (ctx_id(y, z, c) * NX + t, ctx_id(t + s, z, c) * NX + y)
        for t in range(NX)
        for y, z, c in chips()
    ]


def split3(value):
    hi = value.astype(jnp.bfloat16).astype(jnp.float32)
    rest = value - hi
    mid = rest.astype(jnp.bfloat16).astype(jnp.float32)
    return hi, mid, rest - mid


def call(kernel, out_shape, args, flops, scratch=(), place=None, limit=24, far=()):
    size = sum(math.prod(a.shape) * a.dtype.itemsize for a in args)
    specs = [
        pl.BlockSpec(memory_space=pltpu.HBM if i in far else VMEM) for i in range(len(args))
    ]
    if place is not None:
        specs = [pl.BlockSpec(memory_space=pltpu.SMEM)] + specs
        args = (place,) + tuple(args)
    return pl.pallas_call(
        kernel,
        out_shape=out_shape,
        in_specs=specs,
        out_specs=jax.tree.map(lambda _: pl.BlockSpec(memory_space=VMEM), out_shape),
        scratch_shapes=list(scratch),
        compiler_params=pltpu.CompilerParams(vmem_limit_bytes=limit * 1024 * 1024),
        cost_estimate=pl.CostEstimate(flops=flops, bytes_accessed=size, transcendentals=0),
    )(*args)


def copies_kernel(q_ref, out_ref):
    for j in range(q_ref.shape[1]):
        part = q_ref[:, j, :]
        for i in range(out_ref.shape[0]):
            out_ref[i, :, j * 128 : (j + 1) * 128] = part


def attend_kernel(first, rows, q_ref, own_ref, other_ref, reach_ref, out_ref, s_ref):
    here = slice(first, first + rows)
    each = 256 // rows
    span = own_ref.shape[2]
    factor = LOG2E / math.sqrt(128)
    lane = lax.broadcasted_iota(jnp.int32, (rows, 128), 1)
    key = lax.broadcasted_iota(jnp.int32, (rows, span), 1)
    extra = jnp.zeros((rows, 128), jnp.float32)
    blocks = (own_ref, other_ref)
    prompt = jnp.broadcast_to(reach_ref[here, 2:3], (rows, 128))
    is_one = prompt.astype(jnp.float32).astype(jnp.bfloat16)
    is_zero = (1.0 - prompt.astype(jnp.float32)).astype(jnp.bfloat16)
    for step in range(16 // each):
        h = step * each // 8
        columns = slice(h * 128, (h + 1) * 128)
        heads = [step * each + g for g in range(each)]
        q = [q_ref[here, j * 128 : (j + 1) * 128] for j in heads]
        q = jnp.concatenate(
            [
                jnp.concatenate([part * is_zero for part in q], axis=0),
                jnp.concatenate([part * is_one for part in q], axis=0),
            ],
            axis=1,
        )
        high = jnp.full((each * rows, 1), lowest, jnp.float32)
        for b, ref in enumerate(blocks):
            s = lax.dot_general(
                q,
                jnp.concatenate([ref[0, 0, :, columns], ref[1, 0, :, columns]], axis=1),
                (((1,), (1,)), ((), ())),
                preferred_element_type=jnp.float32,
            )
            keep = key < reach_ref[here, b : b + 1]
            s = jnp.concatenate(
                [jnp.where(keep, s[g * rows : (g + 1) * rows], lowest) for g in range(each)],
                axis=0,
            )
            s_ref[:, b * span : (b + 1) * span] = s
            high = jnp.maximum(high, jnp.max(s, axis=1, keepdims=True))
        acc = jnp.zeros((each * rows, 256), jnp.float32)
        total = jnp.zeros((each * rows, 128), jnp.float32)
        for b, ref in enumerate(blocks):
            w = jnp.exp2((s_ref[:, b * span : (b + 1) * span] - high) * factor)
            w = w.astype(jnp.bfloat16)
            v = jnp.concatenate([ref[0, 1, :, columns], ref[1, 1, :, columns]], axis=1)
            acc += jnp.dot(w, v, preferred_element_type=jnp.float32)
            wide = w.astype(jnp.float32)
            for i in range(span // 128):
                total += wide[:, i * 128 : (i + 1) * 128]
        total = jnp.sum(total, axis=1, keepdims=True)
        for g, j in enumerate(heads):
            part = slice(g * rows, (g + 1) * rows)
            value = jnp.where(prompt == 0, acc[part, :128], acc[part, 128:]) / total[part]
            out_ref[:, j * 128 : (j + 1) * 128] = value.astype(jnp.bfloat16)
            level = high[part] * factor + jnp.log2(total[part])
            for i, piece in enumerate(split3(level)):
                extra = jnp.where(lane == j + 16 * i, piece, extra)
    out_ref[:, 2048:] = extra.astype(jnp.bfloat16)


def level_of(extra):
    extra = extra.astype(jnp.float32)
    return extra + pltpu.roll(extra, 112, 1) + pltpu.roll(extra, 96, 1)


def join(parts, levels):
    high = levels[0]
    for level in levels[1:]:
        high = jnp.maximum(high, level)
    shares = [jnp.exp2(level - high) for level in levels]
    total = shares[0]
    for share in shares[1:]:
        total = total + share
    shares = [share / total for share in shares]
    heads = []
    for j in range(16):
        value = None
        for part, share in zip(parts, shares):
            term = part(j).astype(jnp.float32) * share[:, j : j + 1]
            value = term if value is None else value + term
        heads.append(value)
    return heads, high + jnp.log2(total)


def join4_kernel(a_ref, b_ref, c_ref, low_ref, high_ref, out_ref):
    refs = (a_ref, b_ref, c_ref)

    def halves(columns):
        return jnp.concatenate([low_ref[:, columns], high_ref[:, columns]], axis=0)

    parts = [lambda j, r=r: r[:, j * 128 : (j + 1) * 128] for r in refs]
    parts.append(lambda j: halves(slice(j * 128, (j + 1) * 128)))
    levels = [level_of(r[:, 2048:]) for r in refs] + [level_of(halves(slice(2048, 2176)))]
    heads, level = join(parts, levels)
    lane = lax.broadcasted_iota(jnp.int32, level.shape, 1)
    for j, value in enumerate(heads):
        out_ref[:, j * 128 : (j + 1) * 128] = value.astype(jnp.bfloat16)
    hi, mid, lo = split3(level)
    extra = jnp.where(
        lane < 16,
        hi,
        jnp.where(
            lane < 32,
            pltpu.roll(mid, 16, 1),
            jnp.where(lane < 48, pltpu.roll(lo, 32, 1), 0.0),
        ),
    )
    out_ref[:, 2048:] = extra.astype(jnp.bfloat16)


def join9_kernel(got_ref, tail_ref, tail_level_ref, out_ref, copies_ref):
    parts = [lambda j, i=i: got_ref[i, :, j * 128 : (j + 1) * 128] for i in range(NZ)]
    levels = [level_of(got_ref[i, :, 2048:]) for i in range(NZ)]
    parts.append(lambda j: tail_ref[:, j * 128 : (j + 1) * 128])
    levels.append(tail_level_ref[...])
    heads, _ = join(parts, levels)
    for j, value in enumerate(heads):
        value = value.astype(jnp.bfloat16)
        out_ref[:, j * 128 : (j + 1) * 128] = value
        for i in range(NZ):
            copies_ref[i, :, j * 128 : (j + 1) * 128] = value


def project_kernel(place_ref, own_ref, other_ref, w0_ref, w1_ref, w2_ref, w3_ref, out_ref, rows_ref):
    c, y = place_ref[0], place_ref[1]
    rows_ref[c] = own_ref[...]
    rows_ref[1 - c] = other_ref[...]
    rows = jnp.concatenate([rows_ref[0], rows_ref[1]], axis=0)
    for j, w_ref in enumerate((w0_ref, w1_ref, w2_ref, w3_ref)):
        part = lax.dot_general(
            w_ref[...], rows, (((1,), (1,)), ((), ())), preferred_element_type=jnp.float32
        )
        out_ref[lax.rem(y + j, NY)] = part.astype(jnp.bfloat16)


def stream_kernel(got_ref, residual_ref, gain_ref, out_ref):
    total = residual_ref[...].astype(jnp.float32)
    for t in range(NX):
        total = total + got_ref[t].astype(jnp.float32)
    stream = total.astype(jnp.bfloat16).astype(jnp.float32)
    second = jnp.sum(stream * stream, axis=0, keepdims=True)
    hi, mid, lo = split3(second)
    row = lax.broadcasted_iota(jnp.int32, (16, stream.shape[1]), 0)
    extra = jnp.where(row == 0, hi, jnp.where(row == 1, mid, jnp.where(row == 2, lo, 0.0)))
    scaled = (stream * gain_ref[...]).astype(jnp.bfloat16)
    extra = extra.astype(jnp.bfloat16)
    count = stream.shape[0]
    for i in range(NZ):
        out_ref[i, :count] = scaled
        out_ref[i, count:] = extra


def fetch_kernel(w_hbm, out_ref, sem):
    copy = pltpu.make_async_copy(w_hbm, out_ref, sem)
    copy.start()
    copy.wait()


def logits_kernel(slots, place_ref, *refs):
    mine, theirs, w_ref = refs[:4], refs[4:8], refs[8]
    outs, a_ref = list(refs[9:-1]), refs[-1]
    span = 512
    width = w_ref.shape[1]
    c, turn = place_ref[0], place_ref[2]
    for k in range(NY):
        a_ref[c, k] = mine[k][...]
        a_ref[1 - c, k] = theirs[k][...]
    chunk = mine[0].shape[0] // NZ
    count = chunk - 16
    targets = []
    for s, whole in slots:
        targets.append(outs[:1] if whole else outs[:2])
        outs = outs[1:] if whole else outs[2:]

    def put(target, columns, value):
        rows = value.shape[0] // len(target)
        for i, ref in enumerate(target):
            ref[:, columns] = value[i * rows : (i + 1) * rows]

    lefts = []
    for (s, _), target in zip(slots, targets):
        k = lax.rem(turn + NY - s, NY)
        left = jnp.concatenate(
            [
                a_ref[d, k, z * chunk : z * chunk + count]
                for z in range(NZ)
                for d in range(NC)
            ],
            axis=0,
        )
        extra = jnp.zeros((16, 128), jnp.float32)
        for z in range(NZ):
            for d in range(NC):
                extra += a_ref[d, k, z * chunk + count : (z + 1) * chunk].astype(jnp.float32)
        second = extra[0:1] + extra[1:2] + extra[2:3]
        hi, mid, lo = split3(second)
        row = lax.broadcasted_iota(jnp.int32, (128, 128), 0)
        table = jnp.where(row == 0, hi, jnp.where(row == 1, mid, jnp.where(row == 2, lo, 0.0)))
        put(target, slice(width, width + 128), jnp.transpose(table).astype(jnp.bfloat16))
        lefts.append(jnp.transpose(left))
    lefts = jnp.concatenate(lefts, axis=0)
    for n in range(width // span):
        columns = slice(n * span, (n + 1) * span)
        part = jnp.dot(lefts, w_ref[:, columns], preferred_element_type=jnp.float32)
        part = part.astype(jnp.bfloat16)
        for i, target in enumerate(targets):
            put(target, columns, part[i * 128 : (i + 1) * 128])


def add_kernel(a_ref, b_ref, c_ref, d_ref, ab_ref, cd_ref):
    for one, two, out_ref in ((a_ref, b_ref, ab_ref), (c_ref, d_ref, cd_ref)):
        width = one.shape[1] - 128
        value = one[:, :width].astype(jnp.float32) + two[:, :width].astype(jnp.float32)
        out_ref[:, :width] = value.astype(jnp.bfloat16)
        extra = one[:, width:].astype(jnp.float32) + two[:, width:].astype(jnp.float32)
        second = extra[:, 0:1] + extra[:, 1:2] + extra[:, 2:3]
        hi, mid, lo = split3(second)
        lane = lax.broadcasted_iota(jnp.int32, extra.shape, 1)
        extra = jnp.where(lane == 0, hi, jnp.where(lane == 1, mid, jnp.where(lane == 2, lo, 0.0)))
        out_ref[:, width:] = extra.astype(jnp.bfloat16)


def stats_kernel(own_ref, a_ref, b_ref, c_ref, d_ref, allowed_ref, column_ref, out_ref, l_ref):
    rows = own_ref.shape[0]
    width = allowed_ref.shape[1] * 128

    def summed(lo):
        part = [r[:, lo : lo + 128].astype(jnp.float32) for r in (a_ref, b_ref, c_ref, d_ref)]
        others = jnp.concatenate([part[0] + part[1], part[2] + part[3]], axis=0)
        return own_ref[:, lo : lo + 128].astype(jnp.float32) + others

    extra = summed(width)
    second = (extra[:, 0:1] + extra[:, 1:2] + extra[:, 2:3]) / 5120.0
    scale = lax.rsqrt(second + epsilon)
    lane = lax.broadcasted_iota(jnp.int32, (rows, 128), 1)
    column = column_ref[...]
    high = jnp.full((rows, 128), lowest, jnp.float32)
    pick = jnp.zeros((rows, 128), jnp.float32)
    for j in range(width // 128):
        logit = summed(j * 128) * scale
        pick += jnp.where(lane + j * 128 == column, logit, 0.0)
        logit = jnp.where(allowed_ref[:, j : j + 1] > 0, logit, lowest)
        l_ref[:, j * 128 : (j + 1) * 128] = logit
        high = jnp.maximum(high, logit)
    top = jnp.max(high, axis=1, keepdims=True)
    total = jnp.zeros((rows, 128), jnp.float32)
    for j in range(width // 128):
        logit = l_ref[:, j * 128 : (j + 1) * 128]
        total += jnp.where(allowed_ref[:, j : j + 1] > 0, jnp.exp(logit - top), 0.0)
    total = jnp.sum(total, axis=1, keepdims=True)
    pick = jnp.sum(pick, axis=1, keepdims=True)
    level = jnp.where(total > 0.0, top + jnp.log(jnp.where(total > 0.0, total, 1.0)), lowest)
    table = jnp.where(lane == 0, level, jnp.where(lane == 1, pick, 0.0))
    out_ref[...] = jnp.transpose(table)[:8]


def per_device(
    queries,
    prefix_kv,
    tail_kv,
    row_prompt,
    prefix_len,
    tail_len,
    out_weight,
    residual,
    norm_gain,
    vocab_weight,
    allowed,
    next_token,
):
    rows_dev, heads, head_dim = queries.shape
    kv_heads = tail_kv.shape[3]
    tail_width = tail_kv.shape[2]
    group = heads // kv_heads
    width = heads * head_dim
    owner = lax.axis_index("ctx")
    x = lax.axis_index("tp")
    y, z, c = owner // (NZ * NC), (owner // NC) % NZ, owner % NC
    inv_root = 1.0 / math.sqrt(head_dim)
    span = prefix_kv.shape[2]

    q_copies = call(
        copies_kernel,
        jax.ShapeDtypeStruct((NZ, rows_dev, width), jnp.bfloat16),
        (queries,),
        flops=1000,
    )
    q_copies, prefix_kv = lax.optimization_barrier((q_copies, prefix_kv))
    q_z = lax.all_to_all(
        q_copies,
        "ctx",
        split_axis=0,
        concat_axis=0,
        tiled=True,
        axis_index_groups=z_groups,
    ).reshape(NZ * rows_dev, width)
    swapped = lax.ppermute(prefix_kv, "ctx", core_swap)

    local_rows = residual.shape[0]

    def core_major(array):
        rest = array.shape[1:]
        array = array.reshape((NZ, NC, rows_dev) + rest)
        return jnp.swapaxes(array, 0, 1).reshape((local_rows,) + rest)

    residual_c = core_major(residual).T
    columns_dev = residual.shape[1]
    gain = lax.dynamic_slice_in_dim(
        norm_gain, (x * NZ * NC + z * NC + c) * columns_dev, columns_dev, 0
    ).astype(jnp.float32)
    gain = jnp.broadcast_to(gain[:, None], (columns_dev, local_rows))
    place = jnp.stack([c, y, (y + NY - x) % NY, x]).astype(jnp.int32)

    base = jnp.stack([owner * span, (owner + 1 - 2 * c) * span])
    limit = jnp.clip(prefix_len[:, None] - base[None, :], 0, span)
    reach = jnp.concatenate([limit, row_prompt[:, None], row_prompt[:, None]], axis=1).reshape(
        NY, NZ, NC, rows_dev, 4
    )
    reach = lax.dynamic_index_in_dim(reach, c, 2, keepdims=False).reshape(NY, NZ * rows_dev, 4)

    reaches = [
        lax.dynamic_index_in_dim(reach, (y + NY - k) % NY, 0, keepdims=False) for k in range(NY)
    ]
    swapped, residual_c = lax.optimization_barrier((swapped, residual_c))
    residual_t = lax.ppermute(residual_c, ("ctx", "tp"), turned(0))
    flat_kv = (2, 2, span, kv_heads * head_dim)
    kv_own, kv_other = prefix_kv.reshape(flat_kv), swapped.reshape(flat_kv)
    q_z, kv_own, kv_other, reaches, residual_t = lax.optimization_barrier(
        (q_z, kv_own, kv_other, reaches, residual_t)
    )
    group_rows = NZ * rows_dev

    def attend(q, k, first=0, rows=group_rows):
        return call(
            functools.partial(attend_kernel, first, rows),
            jax.ShapeDtypeStruct((rows, width + 128), jnp.bfloat16),
            (q, kv_own, kv_other, reaches[k]),
            flops=2 * 2 * rows * 2048 * 2048,
            scratch=[VMEM((256, 2 * span), jnp.float32)],
        )

    visitors = {k: lax.ppermute(q_z, "ctx", y_shift(k)) for k in (1, 3)}
    own_part = attend(q_z, 0)
    q_later, last = lax.optimization_barrier((q_z, own_part))
    visitors[2] = lax.ppermute(q_later, "ctx", y_shift(2))
    back = []
    half = group_rows // 2
    for k, first, rows in (
        (1, 0, group_rows),
        (3, 0, group_rows),
        (2, 0, half),
        (2, half, half),
    ):
        visitor, last = lax.optimization_barrier((visitors[k], last))
        last = attend(visitor, k, first, rows)
        back.append(lax.ppermute(last, "ctx", y_shift(-k)))

    own_queries, tail_kv, _ = lax.optimization_barrier((queries, tail_kv, last))
    own_queries = own_queries.reshape(rows_dev, kv_heads, group, head_dim)
    tail_scores = (
        jnp.einsum(
            "rhgd,rkhd->rhgk", own_queries, tail_kv[:, 0], preferred_element_type=jnp.float32
        )
        * inv_root
    )
    tail_scores, back[3] = lax.optimization_barrier((tail_scores, back[3]))
    tail_keep = (jnp.arange(tail_width, dtype=jnp.int32)[None, :] < tail_len[:, None])[
        :, None, None, :
    ]
    tail_high = jnp.max(jnp.where(tail_keep, tail_scores, lowest), axis=-1)
    tail_weights = jnp.where(tail_keep, jnp.exp(tail_scores - tail_high[..., None]), 0.0).astype(
        jnp.bfloat16
    )
    tail_total = jnp.sum(tail_weights.astype(jnp.float32), axis=-1)
    tail_sum = jnp.einsum(
        "rhgk,rkhd->rhgd", tail_weights, tail_kv[:, 1], preferred_element_type=jnp.float32
    )
    tail_out = (tail_sum / tail_total[..., None]).reshape(rows_dev, width)
    tail_level = (tail_high * LOG2E + jnp.log2(tail_total)).reshape(rows_dev, heads)
    tail_level = jnp.pad(tail_level, ((0, 0), (0, 128 - heads)))

    joined = call(
        join4_kernel,
        jax.ShapeDtypeStruct((group_rows, width + 128), jnp.bfloat16),
        (own_part,) + tuple(back),
        flops=1000000,
    )

    weight_own, joined = lax.optimization_barrier((out_weight.T, joined))
    weights = [weight_own] + [lax.ppermute(weight_own, "ctx", y_shift(-k)) for k in (1, 2, 3)]
    got = lax.all_to_all(
        joined.reshape(NZ, rows_dev, width + 128),
        "ctx",
        split_axis=0,
        concat_axis=0,
        tiled=True,
        axis_index_groups=z_groups,
    )
    attended, copies = call(
        join9_kernel,
        (
            jax.ShapeDtypeStruct((rows_dev, width), jnp.bfloat16),
            jax.ShapeDtypeStruct((NZ, rows_dev, width), jnp.bfloat16),
        ),
        (got, tail_out, tail_level),
        flops=1000000,
    )

    copies, weights[1], weights[3] = lax.optimization_barrier((copies, weights[1], weights[3]))
    rows_own = lax.all_to_all(
        copies, "ctx", split_axis=0, concat_axis=0, tiled=True, axis_index_groups=z_groups
    ).reshape(NZ * rows_dev, width)
    rows_other = lax.ppermute(rows_own, "ctx", core_swap)
    projected = call(
        project_kernel,
        jax.ShapeDtypeStruct((NY, columns_dev, local_rows), jnp.bfloat16),
        (rows_own, rows_other) + tuple(weights),
        flops=2 * 128 * 320 * 2048,
        scratch=[VMEM((NC, NZ * rows_dev, width), jnp.bfloat16)],
        place=place,
    )
    pieces = lax.all_to_all(projected, "tp", split_axis=0, concat_axis=0, tiled=True)
    streams = call(
        stream_kernel,
        jax.ShapeDtypeStruct((NZ, columns_dev + 16, local_rows), jnp.bfloat16),
        (pieces, residual_t, gain),
        flops=1000000,
    )

    block = lax.all_to_all(
        streams, "ctx", split_axis=0, concat_axis=0, tiled=True, axis_index_groups=z_groups
    ).reshape(NZ * (columns_dev + 16), local_rows)
    mine = [block] + [lax.ppermute(block, "ctx", y_shift(k)) for k in (1, 2, 3)]
    _, vocab_later = lax.optimization_barrier((block, vocab_weight))
    vocab_local = call(
        fetch_kernel,
        jax.ShapeDtypeStruct(vocab_weight.shape, jnp.bfloat16),
        (vocab_later,),
        flops=1000,
        scratch=[pltpu.SemaphoreType.DMA],
        far=(0,),
    )
    mine[2], vocab_local = lax.optimization_barrier((mine[2], vocab_local))
    theirs = [lax.ppermute(one, "ctx", core_swap) for one in mine]
    vocab_here = vocab_weight.shape[1]
    whole = jax.ShapeDtypeStruct((local_rows, vocab_here + 128), jnp.bfloat16)
    part = jax.ShapeDtypeStruct((local_rows // 2, vocab_here + 128), jnp.bfloat16)
    def logits_of(slots, shapes, mine):
        return call(
            functools.partial(logits_kernel, slots),
            shapes,
            tuple(mine) + tuple(theirs) + (vocab_local,),
            flops=2 * 128 * len(slots) * 1280 * 2048,
            scratch=[VMEM((NC, NY) + block.shape, jnp.bfloat16)],
            place=place,
            limit=24,
        )

    low2, high2 = logits_of(((2, False),), (part,) * 2, mine)
    block, _, _ = lax.optimization_barrier((block, low2, high2))
    low1, high1, low3, high3, own = logits_of(
        ((1, False), (3, False), (0, True)), (part,) * 4 + (whole,), [block] + mine[1:]
    )
    up, down = x_shift(1), x_shift(3)
    via_up = lax.ppermute(low2, "tp", up)
    via_down = lax.ppermute(high2, "tp", down)
    high_up = lax.ppermute(high1, "tp", up)
    low_down = lax.ppermute(low3, "tp", down)
    low_sum, high_sum = call(
        add_kernel, (part, part), (via_up, low1, via_down, high3), flops=1000000
    )
    low_up = lax.ppermute(low_sum, "tp", up)
    high_down = lax.ppermute(high_sum, "tp", down)
    sums = (own, low_up, low_down, high_up, high_down)
    stats = call(
        stats_kernel,
        jax.ShapeDtypeStruct((8, local_rows), jnp.float32),
        tuple(sums)
        + (core_major(allowed), core_major((next_token - owner * vocab_here)[:, None])),
        flops=1000000,
        scratch=[VMEM((local_rows, vocab_here), jnp.float32)],
    )[:2]
    every = lax.all_to_all(
        jnp.broadcast_to(stats[None], (NY * NZ * NC,) + stats.shape),
        "ctx",
        split_axis=0,
        concat_axis=0,
        tiled=True,
    )
    peak = jnp.max(every[:, 0], axis=0)
    total = jnp.sum(jnp.exp(every[:, 0] - peak[None]), axis=0)
    logprob = jnp.sum(every[:, 1], axis=0) - (peak + jnp.log(total))
    logprob = jnp.swapaxes(logprob.reshape(NC, NZ, rows_dev), 0, 1).reshape(local_rows)
    return (attended, logprob)


def solution(mesh):
    placed = (
        P("ctx", "tp", None),
        P(None, None, "ctx", "tp", None),
        P("ctx", None, None, "tp", None),
        P(),
        P(),
        P("ctx"),
        P("tp", "ctx"),
        P("tp", "ctx"),
        P(),
        P("tp", "ctx"),
        P("tp", "ctx"),
        P("tp"),
    )
    return jax.shard_map(
        per_device, mesh=mesh, in_specs=placed, out_specs=(P("ctx", "tp"), P("tp")), check_vma=False
    )
```

```python
import functools
import math

import jax
import jax.numpy as jnp
from jax import lax
from jax.experimental import pallas as pl
from jax.experimental.pallas import tpu as pltpu
from jax.sharding import PartitionSpec as P

lowest = -1e30
epsilon = 1e-06
LOG2E = 1.4426950408889634
NY, NZ, NC, NX = 4, 8, 2, 4
VMEM = pltpu.VMEM


def ctx_id(y, z, c):
    return (y % NY) * (NZ * NC) + (z % NZ) * NC + c % NC


def chips():
    return [(y, z, c) for y in range(NY) for z in range(NZ) for c in range(NC)]


core_swap = [(ctx_id(y, z, c), ctx_id(y, z, 1 - c)) for y, z, c in chips()]
z_groups = [[ctx_id(y, z, c) for z in range(NZ)] for y in range(NY) for c in range(NC)]


def y_shift(d):
    return [(ctx_id(y, z, c), ctx_id(y + d, z, c)) for y, z, c in chips()]


def x_shift(d):
    return [(t, (t + d) % NX) for t in range(NX)]


def turned(s):
    return [
        (ctx_id(y, z, c) * NX + t, ctx_id(t + s, z, c) * NX + y)
        for t in range(NX)
        for y, z, c in chips()
    ]


def split3(value):
    hi = value.astype(jnp.bfloat16).astype(jnp.float32)
    rest = value - hi
    mid = rest.astype(jnp.bfloat16).astype(jnp.float32)
    return hi, mid, rest - mid


def call(kernel, out_shape, args, flops, scratch=(), place=None, limit=24, far=()):
    size = sum(math.prod(a.shape) * a.dtype.itemsize for a in args)
    specs = [
        pl.BlockSpec(memory_space=pltpu.HBM if i in far else VMEM) for i in range(len(args))
    ]
    if place is not None:
        specs = [pl.BlockSpec(memory_space=pltpu.SMEM)] + specs
        args = (place,) + tuple(args)
    return pl.pallas_call(
        kernel,
        out_shape=out_shape,
        in_specs=specs,
        out_specs=jax.tree.map(lambda _: pl.BlockSpec(memory_space=VMEM), out_shape),
        scratch_shapes=list(scratch),
        compiler_params=pltpu.CompilerParams(vmem_limit_bytes=limit * 1024 * 1024),
        cost_estimate=pl.CostEstimate(flops=flops, bytes_accessed=size, transcendentals=0),
    )(*args)


def copies_kernel(q_ref, out_ref):
    for j in range(q_ref.shape[1]):
        part = q_ref[:, j, :]
        for i in range(out_ref.shape[0]):
            out_ref[i, :, j * 128 : (j + 1) * 128] = part


def attend_kernel(first, rows, q_ref, own_ref, other_ref, reach_ref, out_ref, s_ref):
    here = slice(first, first + rows)
    each = 256 // rows
    span = own_ref.shape[2]
    factor = LOG2E / math.sqrt(128)
    lane = lax.broadcasted_iota(jnp.int32, (rows, 128), 1)
    key = lax.broadcasted_iota(jnp.int32, (rows, span), 1)
    extra = jnp.zeros((rows, 128), jnp.float32)
    blocks = (own_ref, other_ref)
    prompt = jnp.broadcast_to(reach_ref[here, 2:3], (rows, 128))
    is_one = prompt.astype(jnp.float32).astype(jnp.bfloat16)
    is_zero = (1.0 - prompt.astype(jnp.float32)).astype(jnp.bfloat16)
    for step in range(16 // each):
        h = step * each // 8
        columns = slice(h * 128, (h + 1) * 128)
        heads = [step * each + g for g in range(each)]
        q = [q_ref[here, j * 128 : (j + 1) * 128] for j in heads]
        q = jnp.concatenate(
            [
                jnp.concatenate([part * is_zero for part in q], axis=0),
                jnp.concatenate([part * is_one for part in q], axis=0),
            ],
            axis=1,
        )
        high = jnp.full((each * rows, 1), lowest, jnp.float32)
        for b, ref in enumerate(blocks):
            s = lax.dot_general(
                q,
                jnp.concatenate([ref[0, 0, :, columns], ref[1, 0, :, columns]], axis=1),
                (((1,), (1,)), ((), ())),
                preferred_element_type=jnp.float32,
            )
            keep = key < reach_ref[here, b : b + 1]
            s = jnp.concatenate(
                [jnp.where(keep, s[g * rows : (g + 1) * rows], lowest) for g in range(each)],
                axis=0,
            )
            s_ref[:, b * span : (b + 1) * span] = s
            high = jnp.maximum(high, jnp.max(s, axis=1, keepdims=True))
        acc = jnp.zeros((each * rows, 256), jnp.float32)
        total = jnp.zeros((each * rows, 128), jnp.float32)
        for b, ref in enumerate(blocks):
            w = jnp.exp2((s_ref[:, b * span : (b + 1) * span] - high) * factor)
            w = w.astype(jnp.bfloat16)
            v = jnp.concatenate([ref[0, 1, :, columns], ref[1, 1, :, columns]], axis=1)
            acc += jnp.dot(w, v, preferred_element_type=jnp.float32)
            wide = w.astype(jnp.float32)
            for i in range(span // 128):
                total += wide[:, i * 128 : (i + 1) * 128]
        total = jnp.sum(total, axis=1, keepdims=True)
        for g, j in enumerate(heads):
            part = slice(g * rows, (g + 1) * rows)
            value = jnp.where(prompt == 0, acc[part, :128], acc[part, 128:]) / total[part]
            out_ref[:, j * 128 : (j + 1) * 128] = value.astype(jnp.bfloat16)
            level = high[part] * factor + jnp.log2(total[part])
            for i, piece in enumerate(split3(level)):
                extra = jnp.where(lane == j + 16 * i, piece, extra)
    out_ref[:, 2048:] = extra.astype(jnp.bfloat16)


def level_of(extra):
    extra = extra.astype(jnp.float32)
    return extra + pltpu.roll(extra, 112, 1) + pltpu.roll(extra, 96, 1)


def join(parts, levels):
    high = levels[0]
    for level in levels[1:]:
        high = jnp.maximum(high, level)
    shares = [jnp.exp2(level - high) for level in levels]
    total = shares[0]
    for share in shares[1:]:
        total = total + share
    shares = [share / total for share in shares]
    heads = []
    for j in range(16):
        value = None
        for part, share in zip(parts, shares):
            term = part(j).astype(jnp.float32) * share[:, j : j + 1]
            value = term if value is None else value + term
        heads.append(value)
    return heads, high + jnp.log2(total)


def join4_kernel(a_ref, b_ref, c_ref, low_ref, high_ref, out_ref):
    refs = (a_ref, b_ref, c_ref)

    def halves(columns):
        return jnp.concatenate([low_ref[:, columns], high_ref[:, columns]], axis=0)

    parts = [lambda j, r=r: r[:, j * 128 : (j + 1) * 128] for r in refs]
    parts.append(lambda j: halves(slice(j * 128, (j + 1) * 128)))
    levels = [level_of(r[:, 2048:]) for r in refs] + [level_of(halves(slice(2048, 2176)))]
    heads, level = join(parts, levels)
    lane = lax.broadcasted_iota(jnp.int32, level.shape, 1)
    for j, value in enumerate(heads):
        out_ref[:, j * 128 : (j + 1) * 128] = value.astype(jnp.bfloat16)
    hi, mid, lo = split3(level)
    extra = jnp.where(
        lane < 16,
        hi,
        jnp.where(
            lane < 32,
            pltpu.roll(mid, 16, 1),
            jnp.where(lane < 48, pltpu.roll(lo, 32, 1), 0.0),
        ),
    )
    out_ref[:, 2048:] = extra.astype(jnp.bfloat16)


def join9_kernel(got_ref, tail_ref, tail_level_ref, out_ref, copies_ref):
    parts = [lambda j, i=i: got_ref[i, :, j * 128 : (j + 1) * 128] for i in range(NZ)]
    levels = [level_of(got_ref[i, :, 2048:]) for i in range(NZ)]
    parts.append(lambda j: tail_ref[:, j * 128 : (j + 1) * 128])
    levels.append(tail_level_ref[...])
    heads, _ = join(parts, levels)
    for j, value in enumerate(heads):
        value = value.astype(jnp.bfloat16)
        out_ref[:, j * 128 : (j + 1) * 128] = value
        for i in range(NZ):
            copies_ref[i, :, j * 128 : (j + 1) * 128] = value


def project_kernel(place_ref, own_ref, other_ref, w0_ref, w1_ref, w2_ref, w3_ref, out_ref, rows_ref):
    c, y = place_ref[0], place_ref[1]
    rows_ref[c] = own_ref[...]
    rows_ref[1 - c] = other_ref[...]
    rows = jnp.concatenate([rows_ref[0], rows_ref[1]], axis=0)
    weights = jnp.concatenate([r[...] for r in (w0_ref, w1_ref, w2_ref, w3_ref)], axis=0)
    part = lax.dot_general(
        weights, rows, (((1,), (1,)), ((), ())), preferred_element_type=jnp.float32
    ).astype(jnp.bfloat16)
    count = w0_ref.shape[0]
    for j in range(NY):
        out_ref[lax.rem(y + j, NY)] = part[j * count : (j + 1) * count]


def stream_kernel(got_ref, residual_ref, gain_ref, out_ref):
    total = residual_ref[...].astype(jnp.float32)
    for t in range(NX):
        total = total + got_ref[t].astype(jnp.float32)
    stream = total.astype(jnp.bfloat16).astype(jnp.float32)
    second = jnp.sum(stream * stream, axis=0, keepdims=True)
    hi, mid, lo = split3(second)
    row = lax.broadcasted_iota(jnp.int32, (16, stream.shape[1]), 0)
    extra = jnp.where(row == 0, hi, jnp.where(row == 1, mid, jnp.where(row == 2, lo, 0.0)))
    scaled = (stream * gain_ref[...]).astype(jnp.bfloat16)
    extra = extra.astype(jnp.bfloat16)
    count = stream.shape[0]
    for i in range(NZ):
        out_ref[i, :count] = scaled
        out_ref[i, count:] = extra


def fetch_kernel(w_hbm, out_ref, sem):
    copy = pltpu.make_async_copy(w_hbm, out_ref, sem)
    copy.start()
    copy.wait()


def logits_kernel(slots, place_ref, *refs):
    mine, theirs, w_ref = refs[:4], refs[4:8], refs[8]
    outs, a_ref = list(refs[9:-1]), refs[-1]
    span = 512
    width = w_ref.shape[1]
    c, turn = place_ref[0], place_ref[2]
    for k in range(NY):
        a_ref[c, k] = mine[k][...]
        a_ref[1 - c, k] = theirs[k][...]
    chunk = mine[0].shape[0] // NZ
    count = chunk - 16
    targets = []
    for s, whole in slots:
        targets.append(outs[:1] if whole else outs[:2])
        outs = outs[1:] if whole else outs[2:]

    def put(target, columns, value):
        rows = value.shape[0] // len(target)
        for i, ref in enumerate(target):
            ref[:, columns] = value[i * rows : (i + 1) * rows]

    lefts = []
    for (s, _), target in zip(slots, targets):
        k = lax.rem(turn + NY - s, NY)
        left = jnp.concatenate(
            [
                a_ref[d, k, z * chunk : z * chunk + count]
                for z in range(NZ)
                for d in range(NC)
            ],
            axis=0,
        )
        extra = jnp.zeros((16, 128), jnp.float32)
        for z in range(NZ):
            for d in range(NC):
                extra += a_ref[d, k, z * chunk + count : (z + 1) * chunk].astype(jnp.float32)
        second = extra[0:1] + extra[1:2] + extra[2:3]
        hi, mid, lo = split3(second)
        row = lax.broadcasted_iota(jnp.int32, (128, 128), 0)
        table = jnp.where(row == 0, hi, jnp.where(row == 1, mid, jnp.where(row == 2, lo, 0.0)))
        put(target, slice(width, width + 128), jnp.transpose(table).astype(jnp.bfloat16))
        lefts.append(jnp.transpose(left))
    lefts = jnp.concatenate(lefts, axis=0)
    for n in range(width // span):
        columns = slice(n * span, (n + 1) * span)
        part = jnp.dot(lefts, w_ref[:, columns], preferred_element_type=jnp.float32)
        part = part.astype(jnp.bfloat16)
        for i, target in enumerate(targets):
            put(target, columns, part[i * 128 : (i + 1) * 128])


def add_kernel(a_ref, b_ref, c_ref, d_ref, ab_ref, cd_ref):
    for one, two, out_ref in ((a_ref, b_ref, ab_ref), (c_ref, d_ref, cd_ref)):
        width = one.shape[1] - 128
        value = one[:, :width].astype(jnp.float32) + two[:, :width].astype(jnp.float32)
        out_ref[:, :width] = value.astype(jnp.bfloat16)
        extra = one[:, width:].astype(jnp.float32) + two[:, width:].astype(jnp.float32)
        second = extra[:, 0:1] + extra[:, 1:2] + extra[:, 2:3]
        hi, mid, lo = split3(second)
        lane = lax.broadcasted_iota(jnp.int32, extra.shape, 1)
        extra = jnp.where(lane == 0, hi, jnp.where(lane == 1, mid, jnp.where(lane == 2, lo, 0.0)))
        out_ref[:, width:] = extra.astype(jnp.bfloat16)


def stats_kernel(own_ref, a_ref, b_ref, c_ref, d_ref, allowed_ref, column_ref, out_ref, l_ref):
    rows = own_ref.shape[0]
    width = allowed_ref.shape[1] * 128

    def summed(lo):
        part = [r[:, lo : lo + 128].astype(jnp.float32) for r in (a_ref, b_ref, c_ref, d_ref)]
        others = jnp.concatenate([part[0] + part[1], part[2] + part[3]], axis=0)
        return own_ref[:, lo : lo + 128].astype(jnp.float32) + others

    extra = summed(width)
    second = (extra[:, 0:1] + extra[:, 1:2] + extra[:, 2:3]) / 5120.0
    scale = lax.rsqrt(second + epsilon)
    lane = lax.broadcasted_iota(jnp.int32, (rows, 128), 1)
    column = column_ref[...]
    high = jnp.full((rows, 128), lowest, jnp.float32)
    pick = jnp.zeros((rows, 128), jnp.float32)
    for j in range(width // 128):
        logit = summed(j * 128) * scale
        pick += jnp.where(lane + j * 128 == column, logit, 0.0)
        logit = jnp.where(allowed_ref[:, j : j + 1] > 0, logit, lowest)
        l_ref[:, j * 128 : (j + 1) * 128] = logit
        high = jnp.maximum(high, logit)
    top = jnp.max(high, axis=1, keepdims=True)
    total = jnp.zeros((rows, 128), jnp.float32)
    for j in range(width // 128):
        logit = l_ref[:, j * 128 : (j + 1) * 128]
        total += jnp.where(allowed_ref[:, j : j + 1] > 0, jnp.exp(logit - top), 0.0)
    total = jnp.sum(total, axis=1, keepdims=True)
    pick = jnp.sum(pick, axis=1, keepdims=True)
    level = jnp.where(total > 0.0, top + jnp.log(jnp.where(total > 0.0, total, 1.0)), lowest)
    table = jnp.where(lane == 0, level, jnp.where(lane == 1, pick, 0.0))
    out_ref[...] = jnp.transpose(table)[:8]


def per_device(
    queries,
    prefix_kv,
    tail_kv,
    row_prompt,
    prefix_len,
    tail_len,
    out_weight,
    residual,
    norm_gain,
    vocab_weight,
    allowed,
    next_token,
):
    rows_dev, heads, head_dim = queries.shape
    kv_heads = tail_kv.shape[3]
    tail_width = tail_kv.shape[2]
    group = heads // kv_heads
    width = heads * head_dim
    owner = lax.axis_index("ctx")
    x = lax.axis_index("tp")
    y, z, c = owner // (NZ * NC), (owner // NC) % NZ, owner % NC
    inv_root = 1.0 / math.sqrt(head_dim)
    span = prefix_kv.shape[2]

    q_copies = call(
        copies_kernel,
        jax.ShapeDtypeStruct((NZ, rows_dev, width), jnp.bfloat16),
        (queries,),
        flops=1000,
    )
    q_copies, prefix_kv = lax.optimization_barrier((q_copies, prefix_kv))
    q_z = lax.all_to_all(
        q_copies,
        "ctx",
        split_axis=0,
        concat_axis=0,
        tiled=True,
        axis_index_groups=z_groups,
    ).reshape(NZ * rows_dev, width)
    kv_own = prefix_kv.reshape(2, 2, span, kv_heads * head_dim)
    kv_other = lax.ppermute(kv_own, "ctx", core_swap)

    local_rows = residual.shape[0]

    def core_major(array):
        rest = array.shape[1:]
        array = array.reshape((NZ, NC, rows_dev) + rest)
        return jnp.swapaxes(array, 0, 1).reshape((local_rows,) + rest)

    residual_c = core_major(residual).T
    columns_dev = residual.shape[1]
    gain = lax.dynamic_slice_in_dim(
        norm_gain, (x * NZ * NC + z * NC + c) * columns_dev, columns_dev, 0
    ).astype(jnp.float32)
    gain = jnp.broadcast_to(gain[:, None], (columns_dev, local_rows))
    place = jnp.stack([c, y, (y + NY - x) % NY, x]).astype(jnp.int32)

    base = jnp.stack([owner * span, (owner + 1 - 2 * c) * span])
    limit = jnp.clip(prefix_len[:, None] - base[None, :], 0, span)
    reach = jnp.concatenate([limit, row_prompt[:, None], row_prompt[:, None]], axis=1).reshape(
        NY, NZ, NC, rows_dev, 4
    )
    reach = lax.dynamic_index_in_dim(reach, c, 2, keepdims=False).reshape(NY, NZ * rows_dev, 4)

    reaches = [
        lax.dynamic_index_in_dim(reach, (y + NY - k) % NY, 0, keepdims=False) for k in range(NY)
    ]
    kv_other, residual_c = lax.optimization_barrier((kv_other, residual_c))
    residual_t = lax.ppermute(residual_c, ("ctx", "tp"), turned(0))
    q_z, kv_other, reaches, residual_t = lax.optimization_barrier(
        (q_z, kv_other, reaches, residual_t)
    )
    group_rows = NZ * rows_dev

    def attend(q, k, first=0, rows=group_rows):
        return call(
            functools.partial(attend_kernel, first, rows),
            jax.ShapeDtypeStruct((rows, width + 128), jnp.bfloat16),
            (q, kv_own, kv_other, reaches[k]),
            flops=2 * 2 * rows * 2048 * 2048,
            scratch=[VMEM((256, 2 * span), jnp.float32)],
        )

    visitors = {k: lax.ppermute(q_z, "ctx", y_shift(k)) for k in (1, 3)}
    own_part = attend(q_z, 0)
    q_later, last = lax.optimization_barrier((q_z, own_part))
    visitors[2] = lax.ppermute(q_later, "ctx", y_shift(2))
    back = []
    half = group_rows // 2
    for k, first, rows in (
        (1, 0, group_rows),
        (3, 0, group_rows),
        (2, 0, half),
        (2, half, half),
    ):
        visitor, last = lax.optimization_barrier((visitors[k], last))
        last = attend(visitor, k, first, rows)
        back.append(lax.ppermute(last, "ctx", y_shift(-k)))

    own_queries, tail_kv, _ = lax.optimization_barrier((queries, tail_kv, last))
    own_queries = own_queries.reshape(rows_dev, kv_heads, group, head_dim)
    tail_scores = (
        jnp.einsum(
            "rhgd,rkhd->rhgk", own_queries, tail_kv[:, 0], preferred_element_type=jnp.float32
        )
        * inv_root
    )
    tail_scores, back[3] = lax.optimization_barrier((tail_scores, back[3]))
    tail_keep = (jnp.arange(tail_width, dtype=jnp.int32)[None, :] < tail_len[:, None])[
        :, None, None, :
    ]
    tail_high = jnp.max(jnp.where(tail_keep, tail_scores, lowest), axis=-1)
    tail_weights = jnp.where(tail_keep, jnp.exp(tail_scores - tail_high[..., None]), 0.0).astype(
        jnp.bfloat16
    )
    tail_total = jnp.sum(tail_weights.astype(jnp.float32), axis=-1)
    tail_sum = jnp.einsum(
        "rhgk,rkhd->rhgd", tail_weights, tail_kv[:, 1], preferred_element_type=jnp.float32
    )
    tail_out = (tail_sum / tail_total[..., None]).reshape(rows_dev, width)
    tail_level = (tail_high * LOG2E + jnp.log2(tail_total)).reshape(rows_dev, heads)
    tail_level = jnp.pad(tail_level, ((0, 0), (0, 128 - heads)))

    joined = call(
        join4_kernel,
        jax.ShapeDtypeStruct((group_rows, width + 128), jnp.bfloat16),
        (own_part,) + tuple(back),
        flops=1000000,
    )

    weight_own, joined = lax.optimization_barrier((out_weight.T, joined))
    weights = [weight_own] + [lax.ppermute(weight_own, "ctx", y_shift(-k)) for k in (1, 2, 3)]
    got = lax.all_to_all(
        joined.reshape(NZ, rows_dev, width + 128),
        "ctx",
        split_axis=0,
        concat_axis=0,
        tiled=True,
        axis_index_groups=z_groups,
    )
    attended, copies = call(
        join9_kernel,
        (
            jax.ShapeDtypeStruct((rows_dev, width), jnp.bfloat16),
            jax.ShapeDtypeStruct((NZ, rows_dev, width), jnp.bfloat16),
        ),
        (got, tail_out, tail_level),
        flops=1000000,
    )

    copies, weights[1], weights[3] = lax.optimization_barrier((copies, weights[1], weights[3]))
    rows_own = lax.all_to_all(
        copies, "ctx", split_axis=0, concat_axis=0, tiled=True, axis_index_groups=z_groups
    ).reshape(NZ * rows_dev, width)
    rows_other = lax.ppermute(rows_own, "ctx", core_swap)
    projected = call(
        project_kernel,
        jax.ShapeDtypeStruct((NY, columns_dev, local_rows), jnp.bfloat16),
        (rows_own, rows_other) + tuple(weights),
        flops=2 * 128 * 320 * 2048,
        scratch=[VMEM((NC, NZ * rows_dev, width), jnp.bfloat16)],
        place=place,
    )
    pieces = lax.all_to_all(projected, "tp", split_axis=0, concat_axis=0, tiled=True)
    streams = call(
        stream_kernel,
        jax.ShapeDtypeStruct((NZ, columns_dev + 16, local_rows), jnp.bfloat16),
        (pieces, residual_t, gain),
        flops=1000000,
    )

    block = lax.all_to_all(
        streams, "ctx", split_axis=0, concat_axis=0, tiled=True, axis_index_groups=z_groups
    ).reshape(NZ * (columns_dev + 16), local_rows)
    mine = [block] + [lax.ppermute(block, "ctx", y_shift(k)) for k in (1, 2, 3)]
    _, vocab_later = lax.optimization_barrier((block, vocab_weight))
    vocab_local = call(
        fetch_kernel,
        jax.ShapeDtypeStruct(vocab_weight.shape, jnp.bfloat16),
        (vocab_later,),
        flops=1000,
        scratch=[pltpu.SemaphoreType.DMA],
        far=(0,),
    )
    mine[2], vocab_local = lax.optimization_barrier((mine[2], vocab_local))
    theirs = [lax.ppermute(one, "ctx", core_swap) for one in mine]
    vocab_here = vocab_weight.shape[1]
    whole = jax.ShapeDtypeStruct((local_rows, vocab_here + 128), jnp.bfloat16)
    part = jax.ShapeDtypeStruct((local_rows // 2, vocab_here + 128), jnp.bfloat16)
    def logits_of(slots, shapes, mine):
        return call(
            functools.partial(logits_kernel, slots),
            shapes,
            tuple(mine) + tuple(theirs) + (vocab_local,),
            flops=2 * 128 * len(slots) * 1280 * 2048,
            scratch=[VMEM((NC, NY) + block.shape, jnp.bfloat16)],
            place=place,
            limit=24,
        )

    low2, high2 = logits_of(((2, False),), (part,) * 2, mine)
    block, _, _ = lax.optimization_barrier((block, low2, high2))
    low1, high1, low3, high3, own = logits_of(
        ((1, False), (3, False), (0, True)), (part,) * 4 + (whole,), [block] + mine[1:]
    )
    up, down = x_shift(1), x_shift(3)
    via_up = lax.ppermute(low2, "tp", up)
    via_down = lax.ppermute(high2, "tp", down)
    high_up = lax.ppermute(high1, "tp", up)
    low_down = lax.ppermute(low3, "tp", down)
    low_sum, high_sum = call(
        add_kernel, (part, part), (via_up, low1, via_down, high3), flops=1000000
    )
    low_up = lax.ppermute(low_sum, "tp", up)
    high_down = lax.ppermute(high_sum, "tp", down)
    sums = (own, low_up, low_down, high_up, high_down)
    stats = call(
        stats_kernel,
        jax.ShapeDtypeStruct((8, local_rows), jnp.float32),
        tuple(sums)
        + (core_major(allowed), core_major((next_token - owner * vocab_here)[:, None])),
        flops=1000000,
        scratch=[VMEM((local_rows, vocab_here), jnp.float32)],
    )[:2]
    every = lax.all_to_all(
        jnp.broadcast_to(stats[None], (NY * NZ * NC,) + stats.shape),
        "ctx",
        split_axis=0,
        concat_axis=0,
        tiled=True,
    )
    peak = jnp.max(every[:, 0], axis=0)
    total = jnp.sum(jnp.exp(every[:, 0] - peak[None]), axis=0)
    logprob = jnp.sum(every[:, 1], axis=0) - (peak + jnp.log(total))
    logprob = jnp.swapaxes(logprob.reshape(NC, NZ, rows_dev), 0, 1).reshape(local_rows)
    return (attended, logprob)


def solution(mesh):
    placed = (
        P("ctx", "tp", None),
        P(None, None, "ctx", "tp", None),
        P("ctx", None, None, "tp", None),
        P(),
        P(),
        P("ctx"),
        P("tp", "ctx"),
        P("tp", "ctx"),
        P(),
        P("tp", "ctx"),
        P("tp", "ctx"),
        P("tp"),
    )
    return jax.shard_map(
        per_device, mesh=mesh, in_specs=placed, out_specs=(P("ctx", "tp"), P("tp")), check_vma=False
    )
```
